32 devices in a mesh: enc: 8 (over z, core), seq: 4 (over y, x).
Axes of the slice: x: 2, y: 2, z: 4, core: 2. Of those that a mesh axis runs over, the one named last changes fastest.
Arguments:
- queries: bfloat16 [8, 512, 8192], P('enc', 'seq'), may hold values from -160 to 160
- kv_pool: bfloat16 [32, 2, 128, 8192], P('enc', None, None, 'seq'), may hold values from -16 to 16
- send_lists: int32 [8, 8, 1], P('enc'), may hold values from 0 to 3, as said below
- block_slots: int32 [8, 8, 2], P('enc'), may hold values from 0 to 7, as said below
- grad_context: bfloat16 [8, 512, 8192], P('enc', 'seq'), may hold values from -24 to 24
Outputs:
- context: bfloat16 [8, 512, 8192], P('enc', 'seq')
- grad_queries: bfloat16 [8, 512, 8192], P('enc', 'seq')
- grad_pool: bfloat16 [32, 2, 128, 8192], P('enc', None, None, 'seq')
The draws below stay inside these ranges and needn't reach their ends.
Inputs may be any that keep to these rules, and one draw needn't show every extreme that they name: send_lists[o, e] names 1 different local entries; each of a shard's 4 entries is named for at least one sequence. `block_slots`: the two slots of a block differ; every slot of a sequence is named by at least one of its blocks.
All inputs are finite; a program needn't handle non-finite values.
Results may differ from the reference program's by a relative error of at most 0.0065.
Values may be sent and summed in bfloat16 or wider, within the bound.
No kernel may reach another device: no remote copies, remote signals or barrier semaphores. Data moves between devices by JAX's collectives and lax.ppermute only.
A program may use at most 128 MiB of HBM per device.

```python
import math
import jax
import jax.numpy as jnp
from jax import lax

HEADS = 64
DH = 128
BLOCK = 64
CAP = 1
NBLEN = 128
SEQS = 8
SEQLEN = 512
BLOCKS = 8
SLOTS = 8
POOL = 4
POOLS = 32


def draw_queries(key, part):
    first_key, scale_key = jax.random.split(key, 2)
    shape = (SEQS, SEQLEN, HEADS, DH)
    values = jnp.clip(jax.random.normal(first_key, shape, jnp.float32), -6.0, 6.0)
    row_scale = jnp.exp(jax.random.uniform(scale_key, (SEQS, SEQLEN, HEADS, 1), jnp.float32, math.log(0.4), math.log(2.5)))
    values = values * row_scale
    return values.reshape(SEQS, SEQLEN, HEADS * DH).astype(jnp.bfloat16)


def draw_kv_pool(key, part):
    first_key, scale_key = jax.random.split(key, 2)
    shape = (POOLS, 2, NBLEN, HEADS, DH)
    values = jnp.clip(jax.random.normal(first_key, shape, jnp.float32), -6.0, 6.0)
    row_scale = jnp.exp(jax.random.uniform(scale_key, (POOLS, 2, NBLEN, HEADS, 1), jnp.float32, math.log(0.4), math.log(2.5)))
    values = values * row_scale
    return values.reshape(POOLS, 2, NBLEN, HEADS * DH).astype(jnp.bfloat16)


def draw_send_lists(key, part):
    owner_keys = jax.random.split(jax.random.fold_in(key, 7), SEQS)

    def one_owner(owner_key):
        first_key, order_key = jax.random.split(owner_key)
        first_entry = jax.random.permutation(first_key, SEQS) % POOL
        orders = jax.vmap(lambda sub_key: jax.random.permutation(sub_key, POOL))(jax.random.split(order_key, SEQS))
        where_first = jnp.argmax(orders == first_entry[:, None], axis=1)
        picked = (where_first[:, None] + jnp.arange(CAP)[None, :]) % POOL
        return jnp.take_along_axis(orders, picked, axis=1)
    return jax.vmap(one_owner)(owner_keys).astype(jnp.int32)


def draw_block_slots(key, part):
    sequence_keys = jax.random.split(jax.random.fold_in(key, 9), SEQS)

    def one_sequence(sequence_key):
        first_key, step_key = jax.random.split(sequence_key)
        first_slot = jax.random.permutation(first_key, BLOCKS) % SLOTS
        step_size = jax.random.randint(step_key, (BLOCKS,), 1, SLOTS)
        return jnp.stack([first_slot, (first_slot + step_size) % SLOTS], axis=1)
    return jax.vmap(one_sequence)(sequence_keys).astype(jnp.int32)


def block_scale(rng, extent, cuts, least, largest):
    factor_of = 1.0
    for position, parts in cuts:
        steps = jax.random.uniform(jax.random.fold_in(jax.random.fold_in(rng, 6), position), (parts,), jnp.float32, least / len(cuts), largest / len(cuts))
        factor_of = factor_of * jnp.repeat(jnp.exp(steps), extent[position] // parts).reshape((-1,) + (1,) * (len(extent) - 1 - position))
    return factor_of


def gaussian(rng, extent, deviation, limit, pieces=(), kind=jnp.bfloat16):
    array = deviation * jax.random.normal(rng, extent, jnp.float32)
    if pieces:
        array = array * block_scale(rng, extent, pieces, -0.22, 0.18)
    return jnp.clip(array, -limit, limit).astype(kind)


def setup_inputs(seed: int = 0) -> dict:
    splits = jax.random.split(jax.random.key(seed), 6)
    return {
        "queries": draw_queries(jax.random.fold_in(splits[5], 71), 0),
        "kv_pool": draw_kv_pool(jax.random.fold_in(splits[5], 71), 0),
        "send_lists": draw_send_lists(jax.random.fold_in(splits[5], 71), 0),
        "block_slots": draw_block_slots(jax.random.fold_in(splits[5], 71), 0),
        "grad_context": gaussian(splits[4], (SEQS, SEQLEN, HEADS * DH), 4.0, 24.0, ((0, 8), (1, 4))),
    }


def move_up(row_data):
    filler = jnp.zeros((BLOCK - 1, row_data.shape[1]), row_data.dtype)
    return jnp.concatenate([row_data[BLOCK - 1:], filler], axis=0)


def move_down(row_data):
    filler = jnp.zeros((BLOCK - 1, row_data.shape[1]), row_data.dtype)
    return jnp.concatenate([filler, row_data[:row_data.shape[0] - BLOCK + 1]], axis=0)


def one_sequence(query_rows, received, block_use, grad_rows):
    head_width = query_rows.shape[1]
    heads_all = head_width // DH
    score_scale = DH ** -0.5
    best = lax.Precision.HIGHEST
    queries_moved = move_up(query_rows).reshape(BLOCKS, BLOCK, heads_all, DH).astype(jnp.float32)
    keys_used = received[block_use, 0].reshape(BLOCKS, 2 * NBLEN, heads_all, DH).astype(jnp.float32)
    values_used = received[block_use, 1].reshape(BLOCKS, 2 * NBLEN, heads_all, DH).astype(jnp.float32)
    scores = jnp.einsum("cihd,cjhd->chij", queries_moved, keys_used, precision=best) * score_scale
    row_peak = jnp.max(scores, axis=-1, keepdims=True)
    weights = jnp.exp(scores - row_peak)
    row_probs = weights / jnp.sum(weights, axis=-1, keepdims=True)
    probs_low = lax.optimization_barrier(row_probs.astype(jnp.bfloat16))
    out_blocks = jnp.einsum("chij,cjhd->cihd", probs_low.astype(jnp.float32), values_used, precision=best).astype(jnp.bfloat16)
    context = move_down(out_blocks.reshape(SEQLEN, head_width))
    grads_moved = move_up(grad_rows).reshape(BLOCKS, BLOCK, heads_all, DH).astype(jnp.float32)
    grad_probs = jnp.einsum("cihd,cjhd->chij", grads_moved, values_used, precision=best)
    row_inner = jnp.sum(row_probs * grad_probs, axis=-1, keepdims=True)
    grad_scores = lax.optimization_barrier((row_probs * (grad_probs - row_inner) * score_scale).astype(jnp.bfloat16))
    grad_wide = grad_scores.astype(jnp.float32)
    query_grads = jnp.einsum("chij,cjhd->cihd", grad_wide, keys_used, precision=best).astype(jnp.bfloat16)
    grad_queries = move_down(query_grads.reshape(SEQLEN, head_width))
    key_grads = jnp.einsum("chij,cihd->cjhd", grad_wide, queries_moved, precision=best)
    value_grads = jnp.einsum("chij,cihd->cjhd", probs_low.astype(jnp.float32), grads_moved, precision=best)
    use_grads = jnp.stack([key_grads.reshape(BLOCKS, 2, NBLEN, head_width), value_grads.reshape(BLOCKS, 2, NBLEN, head_width)], axis=2)
    use_grads = use_grads.reshape(BLOCKS * 2, 2, NBLEN, head_width)
    use_low = lax.optimization_barrier(use_grads.astype(jnp.bfloat16)).astype(jnp.float32)
    slot_grads = jax.ops.segment_sum(use_low, block_use.reshape(-1), num_segments=SLOTS).astype(jnp.bfloat16)
    return context, grad_queries, slot_grads


def reference(queries, kv_pool, send_lists, block_slots, grad_context):
    owner_base = jnp.arange(SEQS, dtype=jnp.int32)[:, None] * POOL

    def per_sequence(pool_sum, sequence):
        pool_rows = (owner_base + send_lists[:, sequence, :]).reshape(-1).astype(jnp.int32)
        received = kv_pool[pool_rows]
        context, grad_queries, slot_grads = one_sequence(queries[sequence], received, block_slots[sequence], grad_context[sequence])
        slot_wide = lax.optimization_barrier(slot_grads).astype(jnp.float32)
        pool_sum = pool_sum.at[pool_rows].add(slot_wide)
        return pool_sum, (context, grad_queries)

    start = jnp.zeros(kv_pool.shape, jnp.float32)
    pool_sum, outputs = lax.scan(per_sequence, start, jnp.arange(SEQS, dtype=jnp.int32))
    return outputs[0], outputs[1], pool_sum.astype(jnp.bfloat16)
```

```python
import functools

import jax
import jax.numpy as jnp
from jax import lax
from jax.experimental import pallas as pl
from jax.experimental.pallas import tpu as pltpu
from jax.sharding import PartitionSpec as P

DH = 128
BLOCK = 64
NBLEN = 128
CHUNKS = 2
F32 = jnp.float32
BF16 = jnp.bfloat16
VMEM_BYTES = 40 * 1024 * 1024


def partner(index, step, count):
    if count & (count - 1) == 0:
        return index ^ step
    return (step - index) % count


def exchange(array, axis, step, count):
    pairs = [(i, partner(i, step, count)) for i in range(count)]
    return lax.ppermute(array, axis, pairs)


def pack_kernel(width, chunk, chunks, count, place, q_ref, g_ref, *rest):
    outs, sems = rest[:-1], rest[-1]
    copies = []
    for h in range(chunks):
        for step in range(1, count):
            peer = partner(place[1], step, count)
            cols = pl.ds(pl.multiple_of(peer * width + h * chunk, 128), chunk)
            out = outs[h * (count - 1) + step - 1]
            for n, ref in enumerate((q_ref, g_ref)):
                copy = pltpu.make_async_copy(ref.at[0, :, cols], out.at[n], sems.at[len(copies)])
                copy.start()
                copies.append(copy)
    for copy in copies:
        copy.wait()


def pack(place, queries, grads, width, chunk, chunks, count):
    rows = queries.shape[1]
    total = chunks * (count - 1)
    anywhere = pl.BlockSpec(memory_space=pl.ANY)
    outs = pl.pallas_call(
        functools.partial(pack_kernel, width, chunk, chunks, count),
        grid_spec=pltpu.PrefetchScalarGridSpec(
            num_scalar_prefetch=1,
            grid=(1,),
            in_specs=[anywhere, anywhere],
            out_specs=[anywhere] * total,
            scratch_shapes=[pltpu.SemaphoreType.DMA((2 * total,))],
        ),
        out_shape=[jax.ShapeDtypeStruct((2, rows, chunk), BF16)] * total,
        cost_estimate=pl.CostEstimate(
            flops=0, bytes_accessed=8 * total * rows * chunk, transcendentals=0
        ),
        name="pack_rows",
    )(place, queries, grads)
    return [outs[h * (count - 1) : (h + 1) * (count - 1)] for h in range(chunks)]


def unpack_kernel(width, chunk, chunks, count, place, *rest):
    ins, (ctx_ref, gq_ref), sems = rest[: chunks * count], rest[chunks * count : -1], rest[-1]
    copies = []
    for h in range(chunks):
        for step in range(count):
            peer = partner(place[1], step, count)
            cols = pl.ds(pl.multiple_of(peer * width + h * chunk, 128), chunk)
            src = ins[h * count + step]
            for n, ref in enumerate((ctx_ref, gq_ref)):
                copy = pltpu.make_async_copy(src.at[n], ref.at[0, :, cols], sems.at[len(copies)])
                copy.start()
                copies.append(copy)
    for copy in copies:
        copy.wait()


def unpack(place, parts, shape, width, chunk, chunks, count):
    flat = [array for part in parts for array in part]
    anywhere = pl.BlockSpec(memory_space=pl.ANY)
    return pl.pallas_call(
        functools.partial(unpack_kernel, width, chunk, chunks, count),
        grid_spec=pltpu.PrefetchScalarGridSpec(
            num_scalar_prefetch=1,
            grid=(1,),
            in_specs=[anywhere] * len(flat),
            out_specs=[anywhere, anywhere],
            scratch_shapes=[pltpu.SemaphoreType.DMA((2 * len(flat),))],
        ),
        out_shape=[jax.ShapeDtypeStruct(shape, BF16)] * 2,
        cost_estimate=pl.CostEstimate(
            flops=0, bytes_accessed=8 * shape[1] * shape[2], transcendentals=0
        ),
        name="unpack_rows",
    )(place, *flat)


def dot(left, right, left_dim, right_dim):
    return lax.dot_general(
        left, right, (((left_dim,), (right_dim,)), ((), ())), preferred_element_type=F32
    )


def attend_kernel(seqs, parts, uses, place, q_ref, g_ref, kv_ref, *rest):
    rows_in, rest = rest[: parts - 1], rest[parts - 1 :]
    kv_in, rest = rest[: seqs - 1], rest[seqs - 1 :]
    rows_out, rest = rest[:parts], rest[parts:]
    kv_out, rest = rest[:seqs], rest[seqs:]
    held, rows, made, sums = rest
    scale = DH ** (-0.5)
    me, mine = place[0], place[1]

    held[me] = kv_ref[0]
    for step in range(1, seqs):
        held[partner(me, step, seqs)] = kv_in[step - 1][...]
    for n, ref in enumerate((q_ref, g_ref)):
        rows[mine, n] = pltpu.roll(ref[0].astype(F32), 1, 0)
    for step in range(1, parts):
        for n in range(2):
            piece = rows_in[step - 1][n].astype(F32)
            rows[partner(mine, step, parts), n] = pltpu.roll(piece, 1, 0)
    rows[parts] = jnp.zeros(rows.shape[1:], F32)
    made[0, :, :BLOCK] = jnp.zeros((2, BLOCK, DH), F32)
    sums[...] = jnp.zeros_like(sums)
    first_row = lax.broadcasted_iota(jnp.int32, (BLOCK, DH), 0) == 0

    def one_block(block, q, g):
        first, second = uses[2 * block], uses[2 * block + 1]
        keys = jnp.concatenate([held[first, 0], held[second, 0]], axis=0)
        values = jnp.concatenate([held[first, 1], held[second, 1]], axis=0)
        scores = dot(q, keys, 1, 1) * scale
        weights = jnp.exp(scores - jnp.max(scores, axis=1, keepdims=True))
        probs = weights / jnp.sum(weights, axis=1, keepdims=True)
        probs_low = probs.astype(BF16)
        out = dot(probs_low, values, 1, 0)
        grad_probs = dot(g, values, 1, 1)
        inner = jnp.sum(probs * grad_probs, axis=1, keepdims=True)
        grad_scores = (probs * (grad_probs - inner) * scale).astype(BF16)
        grad_q = dot(grad_scores, keys, 1, 0)
        grad_keys = dot(grad_scores, q, 0, 0)
        grad_values = dot(probs_low, g, 0, 0)
        sums[first, 0] += grad_keys[:NBLEN]
        sums[second, 0] += grad_keys[NBLEN:]
        sums[first, 1] += grad_values[:NBLEN]
        sums[second, 1] += grad_values[NBLEN:]
        return out, grad_q

    def one_part(part, carry):
        q, g = (rows[part, n, BLOCK:].astype(BF16) for n in range(2))
        for n, result in enumerate(one_block(2 * part, q, g)):
            made[part, n, BLOCK:] = result
        q, g = (
            jnp.where(first_row, rows[part, n, :BLOCK], rows[part + 1, n, :BLOCK]).astype(BF16)
            for n in range(2)
        )
        for n, result in enumerate(one_block(2 * part + 1, q, g)):
            made[part + 1, n, :BLOCK] = result
            made[part, n, :1] = result[:1]
        return carry

    if parts <= 4:
        for part in range(parts):
            one_part(part, 0)
    else:
        lax.fori_loop(0, parts, one_part, 0)

    for step in range(parts):
        for n in range(2):
            piece = made[partner(mine, step, parts), n]
            rows_out[step][n] = pltpu.roll(piece, 2 * BLOCK - 1, 0).astype(BF16)
    for step in range(seqs):
        kv_out[step][...] = sums[partner(me, step, seqs)].astype(BF16)


def attend(h, uses, place, queries, grads, kv_pool, rows_in, kv_in, chunk, seqs, parts):
    heads = chunk // DH
    width = kv_pool.shape[-1]
    blocks = uses.shape[0] // 2
    first = h * heads
    per_part = width // DH
    own_rows = pl.BlockSpec(
        (1, 2 * BLOCK, DH), lambda i, uses, place: (0, 0, place[1] * per_part + first + i)
    )
    own_kv = pl.BlockSpec(
        (1, 2, NBLEN, DH), lambda i, uses, place: (place[2], 0, 0, first + i)
    )
    rows_spec = pl.BlockSpec((2, 2 * BLOCK, DH), lambda i, uses, place: (0, 0, i))
    kv_spec = pl.BlockSpec((2, NBLEN, DH), lambda i, uses, place: (0, 0, i))
    outs = pl.pallas_call(
        functools.partial(attend_kernel, seqs, parts),
        grid_spec=pltpu.PrefetchScalarGridSpec(
            num_scalar_prefetch=2,
            grid=(heads,),
            in_specs=[own_rows, own_rows, own_kv]
            + [rows_spec] * (parts - 1)
            + [kv_spec] * (seqs - 1),
            out_specs=[rows_spec] * parts + [kv_spec] * seqs,
            scratch_shapes=[
                pltpu.VMEM((seqs, 2, NBLEN, DH), BF16),
                pltpu.VMEM((parts + 1, 2, 2 * BLOCK, DH), F32),
                pltpu.VMEM((parts + 1, 2, 2 * BLOCK, DH), F32),
                pltpu.VMEM((seqs, 2, NBLEN, DH), F32),
            ],
        ),
        out_shape=[jax.ShapeDtypeStruct((2, 2 * BLOCK, chunk), BF16)] * parts
        + [jax.ShapeDtypeStruct((2, NBLEN, chunk), BF16)] * seqs,
        compiler_params=pltpu.CompilerParams(vmem_limit_bytes=VMEM_BYTES),
        cost_estimate=pl.CostEstimate(
            flops=12 * heads * blocks * BLOCK * 2 * NBLEN * DH,
            bytes_accessed=8 * (seqs + parts) * NBLEN * chunk,
            transcendentals=heads * blocks * BLOCK * 2 * NBLEN,
        ),
        name="attend_blocks",
    )(uses, place, queries, grads, kv_pool, *rows_in, *kv_in)
    return outs[:parts], outs[parts:]


def owner_kernel(seqs, aliased, names, *rest):
    ins, out_ref, acc = rest[:seqs], rest[-2], rest[-1]
    acc[...] = jnp.zeros_like(acc)
    for step in range(seqs):
        acc[names[step]] += ins[step][...].astype(F32)
    out_ref[...] = acc[...].astype(BF16)


def owner_sum(h, names, parts, shape, so_far, chunk):
    seqs = len(parts)
    wide = min(chunk, 256)
    steps = chunk // wide
    spec = pl.BlockSpec((2, NBLEN, wide), lambda i, names: (0, 0, i))
    out_spec = pl.BlockSpec(
        (shape[0], 2, NBLEN, wide), lambda i, names: (0, 0, 0, h * steps + i)
    )
    extra = [] if so_far is None else [so_far]
    return pl.pallas_call(
        functools.partial(owner_kernel, seqs, bool(extra)),
        grid_spec=pltpu.PrefetchScalarGridSpec(
            num_scalar_prefetch=1,
            grid=(steps,),
            in_specs=[spec] * seqs + [pl.BlockSpec(memory_space=pl.ANY)] * len(extra),
            out_specs=out_spec,
            scratch_shapes=[pltpu.VMEM((shape[0], 2, NBLEN, wide), F32)],
        ),
        out_shape=jax.ShapeDtypeStruct(shape, BF16),
        input_output_aliases={seqs + 1: 0} if extra else {},
        compiler_params=pltpu.CompilerParams(vmem_limit_bytes=VMEM_BYTES),
        cost_estimate=pl.CostEstimate(
            flops=seqs * 2 * NBLEN * chunk,
            bytes_accessed=4 * (seqs + shape[0]) * NBLEN * chunk,
            transcendentals=0,
        ),
        name="owner_sum",
    )(names, *parts, *extra)


def far_first(count):
    return sorted(range(1, count), reverse=True)


def local(seqs, parts, queries, kv_pool, send_lists, block_slots, grad_context):
    width = kv_pool.shape[-1]
    chunks = min(CHUNKS, width // DH)
    chunk = width // chunks
    me, mine = lax.axis_index("enc"), lax.axis_index("seq")
    entries = send_lists[0, :, 0]
    names = jnp.stack([entries[partner(me, step, seqs)] for step in range(seqs)])
    uses = block_slots[0].reshape(-1)
    place = jnp.stack([me, mine, names[0]]).astype(jnp.int32)

    def fetch(h, source):
        got = [None] * (seqs - 1)
        for step in far_first(seqs):
            piece = lax.dynamic_slice(
                source, (names[step], 0, 0, h * chunk), (1, 2, NBLEN, chunk)
            )[0]
            got[step - 1] = exchange(piece, "enc", step, seqs)
        return got

    fetched = [fetch(0, kv_pool)]
    packed = pack(place, queries, grad_context, width, chunk, chunks, parts)
    heads = [
        [exchange(packed[h][step - 1], "seq", step, parts) for step in range(1, parts)]
        for h in range(chunks)
    ]
    pool_grads = None
    token_parts, returns = [], []
    for h in range(chunks):
        if h + 1 < chunks:
            fetched[h], source = lax.optimization_barrier((fetched[h], kv_pool))
            fetched.append(fetch(h + 1, source))
        rows_out, kv_out = attend(
            h, uses, place, queries, grad_context, kv_pool, heads[h], fetched[h], chunk, seqs, parts
        )
        returns.append(
            [kv_out[0]] + [exchange(kv_out[step], "enc", step, seqs) for step in range(1, seqs)]
        )
        token_parts.append(
            [rows_out[0]] + [exchange(rows_out[step], "seq", step, parts) for step in range(1, parts)]
        )
    context, grad_queries = unpack(
        place, token_parts, queries.shape, width, chunk, chunks, parts
    )
    for h in range(chunks):
        pool_grads = owner_sum(h, names, returns[h], kv_pool.shape, pool_grads, chunk)
    return (context, grad_queries, pool_grads)


def solution(mesh):
    in_specs = (
        P("enc", "seq", None),
        P("enc", None, None, "seq"),
        P("enc", None, None),
        P("enc", None, None),
        P("enc", "seq", None),
    )
    out_specs = (P("enc", "seq", None), P("enc", "seq", None), P("enc", None, None, "seq"))
    body = functools.partial(local, mesh.shape["enc"], mesh.shape["seq"])
    return jax.shard_map(body, mesh=mesh, in_specs=in_specs, out_specs=out_specs, check_vma=False)
```

```python
import functools

import jax
import jax.numpy as jnp
from jax import lax
from jax.experimental import pallas as pl
from jax.experimental.pallas import tpu as pltpu
from jax.sharding import PartitionSpec as P

DH = 128
BLOCK = 64
NBLEN = 128
CHUNKS = 2
F32 = jnp.float32
BF16 = jnp.bfloat16
VMEM_BYTES = 40 * 1024 * 1024


def partner(index, step, count):
    if count & (count - 1) == 0:
        return index ^ step
    return (step - index) % count


def exchange(array, axis, step, count):
    pairs = [(i, partner(i, step, count)) for i in range(count)]
    return lax.ppermute(array, axis, pairs)


def pack_kernel(width, chunk, chunks, count, place, q_ref, g_ref, *rest):
    outs, sems = rest[:-1], rest[-1]
    copies = []
    for h in range(chunks):
        for step in range(1, count):
            peer = partner(place[1], step, count)
            cols = pl.ds(pl.multiple_of(peer * width + h * chunk, 128), chunk)
            out = outs[h * (count - 1) + step - 1]
            for n, ref in enumerate((q_ref, g_ref)):
                copy = pltpu.make_async_copy(ref.at[0, :, cols], out.at[n], sems.at[len(copies)])
                copy.start()
                copies.append(copy)
    for copy in copies:
        copy.wait()


def pack(place, queries, grads, width, chunk, chunks, count):
    rows = queries.shape[1]
    total = chunks * (count - 1)
    anywhere = pl.BlockSpec(memory_space=pl.ANY)
    outs = pl.pallas_call(
        functools.partial(pack_kernel, width, chunk, chunks, count),
        grid_spec=pltpu.PrefetchScalarGridSpec(
            num_scalar_prefetch=1,
            grid=(1,),
            in_specs=[anywhere, anywhere],
            out_specs=[pl.BlockSpec((2, rows, chunk), lambda i, place: (0, 0, 0))] * total,
            scratch_shapes=[pltpu.SemaphoreType.DMA((2 * total,))],
        ),
        out_shape=[jax.ShapeDtypeStruct((2, rows, chunk), BF16)] * total,
        compiler_params=pltpu.CompilerParams(vmem_limit_bytes=VMEM_BYTES),
        cost_estimate=pl.CostEstimate(
            flops=0, bytes_accessed=8 * total * rows * chunk, transcendentals=0
        ),
        name="pack_rows",
    )(place, queries, grads)
    return [outs[h * (count - 1) : (h + 1) * (count - 1)] for h in range(chunks)]


def unpack_kernel(width, chunk, chunks, count, place, *rest):
    ins, (ctx_ref, gq_ref), sems = rest[: chunks * count], rest[chunks * count : -1], rest[-1]
    copies = []
    for h in range(chunks):
        for step in range(count):
            peer = partner(place[1], step, count)
            cols = pl.ds(pl.multiple_of(peer * width + h * chunk, 128), chunk)
            src = ins[h * count + step]
            for n, ref in enumerate((ctx_ref, gq_ref)):
                copy = pltpu.make_async_copy(src.at[n], ref.at[0, :, cols], sems.at[len(copies)])
                copy.start()
                copies.append(copy)
    for copy in copies:
        copy.wait()


def unpack(place, parts, shape, width, chunk, chunks, count):
    flat = [array for part in parts for array in part]
    anywhere = pl.BlockSpec(memory_space=pl.ANY)
    return pl.pallas_call(
        functools.partial(unpack_kernel, width, chunk, chunks, count),
        grid_spec=pltpu.PrefetchScalarGridSpec(
            num_scalar_prefetch=1,
            grid=(1,),
            in_specs=[pl.BlockSpec(array.shape, lambda i, place: (0, 0, 0)) for array in flat],
            out_specs=[anywhere, anywhere],
            scratch_shapes=[pltpu.SemaphoreType.DMA((2 * len(flat),))],
        ),
        out_shape=[jax.ShapeDtypeStruct(shape, BF16)] * 2,
        compiler_params=pltpu.CompilerParams(vmem_limit_bytes=VMEM_BYTES),
        cost_estimate=pl.CostEstimate(
            flops=0, bytes_accessed=8 * shape[1] * shape[2], transcendentals=0
        ),
        name="unpack_rows",
    )(place, *flat)


def dot(left, right, left_dim, right_dim):
    return lax.dot_general(
        left, right, (((left_dim,), (right_dim,)), ((), ())), preferred_element_type=F32
    )


def attend_kernel(seqs, parts, uses, place, q_ref, g_ref, held, *rest):
    rows_in, rest = rest[: parts - 1], rest[parts - 1 :]
    rows_out, rest = rest[:parts], rest[parts:]
    kv_out, rows, made, sums = rest
    scale = DH ** (-0.5)
    mine = place[1]

    for n, ref in enumerate((q_ref, g_ref)):
        rows[mine, n] = pltpu.roll(ref[0].astype(F32), 1, 0)
    for step in range(1, parts):
        for n in range(2):
            piece = rows_in[step - 1][n].astype(F32)
            rows[partner(mine, step, parts), n] = pltpu.roll(piece, 1, 0)
    rows[parts] = jnp.zeros(rows.shape[1:], F32)
    made[0, :, :BLOCK] = jnp.zeros((2, BLOCK, DH), F32)
    sums[...] = jnp.zeros_like(sums)
    first_row = lax.broadcasted_iota(jnp.int32, (BLOCK, DH), 0) == 0

    def one_block(block, q, g):
        first, second = uses[2 * block], uses[2 * block + 1]
        keys = jnp.concatenate([held[first, 0], held[second, 0]], axis=0)
        values = jnp.concatenate([held[first, 1], held[second, 1]], axis=0)
        scores = dot(q, keys, 1, 1) * scale
        weights = jnp.exp(scores - jnp.max(scores, axis=1, keepdims=True))
        probs = weights / jnp.sum(weights, axis=1, keepdims=True)
        probs_low = probs.astype(BF16)
        out = dot(probs_low, values, 1, 0)
        grad_probs = dot(g, values, 1, 1)
        inner = jnp.sum(probs * grad_probs, axis=1, keepdims=True)
        grad_scores = (probs * (grad_probs - inner) * scale).astype(BF16)
        grad_q = dot(grad_scores, keys, 1, 0)
        grad_keys = dot(grad_scores, q, 0, 0)
        grad_values = dot(probs_low, g, 0, 0)
        sums[first, 0] += grad_keys[:NBLEN]
        sums[second, 0] += grad_keys[NBLEN:]
        sums[first, 1] += grad_values[:NBLEN]
        sums[second, 1] += grad_values[NBLEN:]
        return out, grad_q

    def one_part(part, carry):
        q, g = (rows[part, n, BLOCK:].astype(BF16) for n in range(2))
        for n, result in enumerate(one_block(2 * part, q, g)):
            made[part, n, BLOCK:] = result
        q, g = (
            jnp.where(first_row, rows[part, n, :BLOCK], rows[part + 1, n, :BLOCK]).astype(BF16)
            for n in range(2)
        )
        for n, result in enumerate(one_block(2 * part + 1, q, g)):
            made[part + 1, n, :BLOCK] = result
            made[part, n, :1] = result[:1]
        return carry

    if parts <= 4:
        for part in range(parts):
            one_part(part, 0)
    else:
        lax.fori_loop(0, parts, one_part, 0)

    for step in range(parts):
        for n in range(2):
            piece = made[partner(mine, step, parts), n]
            rows_out[step][n] = pltpu.roll(piece, 2 * BLOCK - 1, 0).astype(BF16)
    kv_out[...] = sums[...].astype(BF16)


def attend(h, uses, place, queries, grads, rows_in, kv_in, width, chunk, seqs, parts):
    heads = chunk // DH
    blocks = uses.shape[0] // 2
    first = h * heads
    per_part = width // DH
    own_rows = pl.BlockSpec(
        (1, 2 * BLOCK, DH), lambda i, uses, place: (0, 0, place[1] * per_part + first + i)
    )
    rows_spec = pl.BlockSpec((2, 2 * BLOCK, DH), lambda i, uses, place: (0, 0, i))
    kv_spec = pl.BlockSpec((seqs, 2, NBLEN, DH), lambda i, uses, place: (0, 0, 0, i))
    outs = pl.pallas_call(
        functools.partial(attend_kernel, seqs, parts),
        grid_spec=pltpu.PrefetchScalarGridSpec(
            num_scalar_prefetch=2,
            grid=(heads,),
            in_specs=[own_rows, own_rows, kv_spec] + [rows_spec] * (parts - 1),
            out_specs=[rows_spec] * parts + [kv_spec],
            scratch_shapes=[
                pltpu.VMEM((parts + 1, 2, 2 * BLOCK, DH), F32),
                pltpu.VMEM((parts + 1, 2, 2 * BLOCK, DH), F32),
                pltpu.VMEM((seqs, 2, NBLEN, DH), F32),
            ],
        ),
        out_shape=[jax.ShapeDtypeStruct((2, 2 * BLOCK, chunk), BF16)] * parts
        + [jax.ShapeDtypeStruct((seqs, 2, NBLEN, chunk), BF16)],
        compiler_params=pltpu.CompilerParams(vmem_limit_bytes=VMEM_BYTES),
        cost_estimate=pl.CostEstimate(
            flops=12 * heads * blocks * BLOCK * 2 * NBLEN * DH,
            bytes_accessed=8 * (seqs + parts) * NBLEN * chunk,
            transcendentals=heads * blocks * BLOCK * 2 * NBLEN,
        ),
        name="attend_blocks",
    )(uses, place, queries, grads, kv_in, *rows_in)
    return outs[:parts], outs[parts]


def owner_kernel(seqs, names, back_ref, *rest):
    out_ref, acc = rest[-2], rest[-1]
    acc[...] = jnp.zeros_like(acc)
    for seq in range(seqs):
        acc[names[seq]] += back_ref[seq].astype(F32)
    out_ref[...] = acc[...].astype(BF16)


def owner_sum(h, names, back, shape, so_far, chunk):
    seqs = back.shape[0]
    wide = min(chunk, 256)
    steps = chunk // wide
    spec = pl.BlockSpec((seqs, 2, NBLEN, wide), lambda i, names: (0, 0, 0, i))
    out_spec = pl.BlockSpec(
        (shape[0], 2, NBLEN, wide), lambda i, names: (0, 0, 0, h * steps + i)
    )
    extra = [] if so_far is None else [so_far]
    return pl.pallas_call(
        functools.partial(owner_kernel, seqs),
        grid_spec=pltpu.PrefetchScalarGridSpec(
            num_scalar_prefetch=1,
            grid=(steps,),
            in_specs=[spec] + [pl.BlockSpec(memory_space=pl.ANY)] * len(extra),
            out_specs=out_spec,
            scratch_shapes=[pltpu.VMEM((shape[0], 2, NBLEN, wide), F32)],
        ),
        out_shape=jax.ShapeDtypeStruct(shape, BF16),
        input_output_aliases={2: 0} if extra else {},
        compiler_params=pltpu.CompilerParams(vmem_limit_bytes=VMEM_BYTES),
        cost_estimate=pl.CostEstimate(
            flops=seqs * 2 * NBLEN * chunk,
            bytes_accessed=4 * (seqs + shape[0]) * NBLEN * chunk,
            transcendentals=0,
        ),
        name="owner_sum",
    )(names, back, *extra)


def pick_kernel(names, pool_ref, out_ref):
    out_ref[...] = pool_ref[...]


def pick(h, names, kv_pool, chunk):
    seqs = names.shape[0]
    return pl.pallas_call(
        pick_kernel,
        grid_spec=pltpu.PrefetchScalarGridSpec(
            num_scalar_prefetch=1,
            grid=(seqs,),
            in_specs=[
                pl.BlockSpec((1, 2, NBLEN, chunk), lambda i, names: (names[i], 0, 0, h))
            ],
            out_specs=pl.BlockSpec((1, 2, NBLEN, chunk), lambda i, names: (i, 0, 0, 0)),
        ),
        out_shape=jax.ShapeDtypeStruct((seqs, 2, NBLEN, chunk), BF16),
        compiler_params=pltpu.CompilerParams(vmem_limit_bytes=VMEM_BYTES),
        cost_estimate=pl.CostEstimate(
            flops=0, bytes_accessed=8 * seqs * NBLEN * chunk, transcendentals=0
        ),
        name="pick_entries",
    )(names, kv_pool)


def swap(array):
    return lax.all_to_all(array, "enc", split_axis=0, concat_axis=0, tiled=True)


def local(seqs, parts, queries, kv_pool, send_lists, block_slots, grad_context):
    width = kv_pool.shape[-1]
    chunks = min(CHUNKS, width // DH)
    chunk = width // chunks
    mine = lax.axis_index("seq")
    names = send_lists.reshape(-1)
    uses = block_slots.reshape(-1)
    place = jnp.stack([mine, mine]).astype(jnp.int32)

    fetched = [swap(pick(h, names, kv_pool, chunk)) for h in range(chunks)]
    packed = pack(place, queries, grad_context, width, chunk, chunks, parts)
    heads = [
        [exchange(packed[h][step - 1], "seq", step, parts) for step in range(1, parts)]
        for h in range(chunks)
    ]
    pool_grads = None
    token_parts, returns = [], []
    for h in range(chunks):
        rows_out, kv_out = attend(
            h, uses, place, queries, grad_context, heads[h], fetched[h], width, chunk, seqs, parts
        )
        returns.append(swap(kv_out))
        token_parts.append(
            [rows_out[0]] + [exchange(rows_out[step], "seq", step, parts) for step in range(1, parts)]
        )
    context, grad_queries = unpack(
        place, token_parts, queries.shape, width, chunk, chunks, parts
    )
    for h in range(chunks):
        pool_grads = owner_sum(h, names, returns[h], kv_pool.shape, pool_grads, chunk)
    return (context, grad_queries, pool_grads)


def solution(mesh):
    in_specs = (
        P("enc", "seq", None),
        P("enc", None, None, "seq"),
        P("enc", None, None),
        P("enc", None, None),
        P("enc", "seq", None),
    )
    out_specs = (P("enc", "seq", None), P("enc", "seq", None), P("enc", None, None, "seq"))
    body = functools.partial(local, mesh.shape["enc"], mesh.shape["seq"])
    return jax.shard_map(body, mesh=mesh, in_specs=in_specs, out_specs=out_specs, check_vma=False)
```

```python
import functools

import jax
import jax.numpy as jnp
from jax import lax
from jax.experimental import pallas as pl
from jax.experimental.pallas import tpu as pltpu
from jax.sharding import PartitionSpec as P

DH = 128
BLOCK = 64
NBLEN = 128
CHUNKS = 2
FAR_DEPTH = 4
F32 = jnp.float32
BF16 = jnp.bfloat16
VMEM_BYTES = 40 * 1024 * 1024


def partner(index, step, count):
    if count & (count - 1) == 0:
        return index ^ step
    return (step - index) % count


def exchange(array, step, count):
    pairs = [(i, partner(i, step, count)) for i in range(count)]
    return lax.ppermute(array, "enc", pairs)


def swap_rows(array):
    return lax.all_to_all(array, "seq", split_axis=0, concat_axis=0, tiled=True)


def after(array, earlier):
    return lax.optimization_barrier((array, earlier))[0]


def cost(moved, flops=0, exps=0):
    return pl.CostEstimate(flops=flops, bytes_accessed=moved, transcendentals=exps)


PARAMS = pltpu.CompilerParams(vmem_limit_bytes=VMEM_BYTES)
SCALARS = pl.BlockSpec(memory_space=pltpu.SMEM)
ANYWHERE = pl.BlockSpec(memory_space=pl.ANY)


def pack_kernel(q_ref, g_ref, out_ref):
    out_ref[0, 0] = q_ref[0]
    out_ref[0, 1] = g_ref[0]


def pack(h, queries, grads, chunk, chunks, parts):
    rows = queries.shape[1]
    spec = pl.BlockSpec((1, rows, chunk), lambda i: (0, 0, i * chunks + h))
    return pl.pallas_call(
        pack_kernel,
        grid=(parts,),
        in_specs=[spec, spec],
        out_specs=pl.BlockSpec((1, 2, rows, chunk), lambda i: (i, 0, 0, 0)),
        out_shape=jax.ShapeDtypeStruct((parts, 2, rows, chunk), BF16),
        compiler_params=PARAMS,
        cost_estimate=cost(8 * parts * rows * chunk),
        name="pack_rows",
    )(queries, grads)


def unpack_kernel(chunks, *refs):
    ins, (ctx_ref, gq_ref) = refs[:chunks], refs[chunks:]
    chunk = ins[0].shape[-1]
    for h, ref in enumerate(ins):
        ctx_ref[0, :, h * chunk : (h + 1) * chunk] = ref[0, 0]
        gq_ref[0, :, h * chunk : (h + 1) * chunk] = ref[0, 1]


def unpack(pieces, shape):
    parts, _, rows, chunk = pieces[0].shape
    chunks = len(pieces)
    out_spec = pl.BlockSpec((1, rows, chunks * chunk), lambda i: (0, 0, i))
    return pl.pallas_call(
        functools.partial(unpack_kernel, chunks),
        grid=(parts,),
        in_specs=[pl.BlockSpec((1, 2, rows, chunk), lambda i: (i, 0, 0, 0))] * chunks,
        out_specs=[out_spec, out_spec],
        out_shape=[jax.ShapeDtypeStruct(shape, BF16)] * 2,
        compiler_params=PARAMS,
        cost_estimate=cost(8 * rows * shape[2]),
        name="unpack_rows",
    )(*pieces)


def pick_kernel(h, steps, seqs, lists, pool_ref, *rest):
    outs, sems = rest[:-1], rest[-1]
    me = lax.axis_index("enc")
    chunk = outs[0].shape[-1]
    copies = []
    for n, step in enumerate(steps):
        entry = lists[0, partner(me, step, seqs), 0]
        source = pool_ref.at[entry, :, :, h * chunk : (h + 1) * chunk]
        copies.append(pltpu.make_async_copy(source, outs[n], sems.at[n]))
        copies[-1].start()
    for copy in copies:
        copy.wait()


def pick(h, steps, send_lists, kv_pool, chunk):
    seqs = send_lists.shape[1]
    shape = (2, NBLEN, chunk)
    return pl.pallas_call(
        functools.partial(pick_kernel, h, steps, seqs),
        grid=(1,),
        in_specs=[SCALARS, ANYWHERE],
        out_specs=[pl.BlockSpec(shape, lambda i: (0, 0, 0))] * len(steps),
        out_shape=[jax.ShapeDtypeStruct(shape, BF16)] * len(steps),
        scratch_shapes=[pltpu.SemaphoreType.DMA((len(steps),))],
        compiler_params=PARAMS,
        cost_estimate=cost(8 * len(steps) * NBLEN * chunk),
        name="pick_entries",
    )(send_lists, kv_pool)


def dot(left, right, left_dim, right_dim):
    return lax.dot_general(
        left, right, (((left_dim,), (right_dim,)), ((), ())), preferred_element_type=F32
    )


def attend_kernel(seqs, parts, uses, rows_in, *rest):
    kv_in, rest = rest[:seqs], rest[seqs:]
    rows_out, rest = rest[0], rest[1:]
    kv_out, rest = rest[:seqs], rest[seqs:]
    held, rows, made, sums = rest
    scale = DH ** (-0.5)
    me = lax.axis_index("enc")

    for step in range(seqs):
        held[partner(me, step, seqs)] = kv_in[step][...]
    for part in range(parts):
        for n in range(2):
            rows[part, n] = pltpu.roll(rows_in[part, n].astype(F32), 1, 0)
    rows[parts] = jnp.zeros(rows.shape[1:], F32)
    made[0, :, :BLOCK] = jnp.zeros((2, BLOCK, DH), F32)
    sums[...] = jnp.zeros_like(sums)
    first_row = lax.broadcasted_iota(jnp.int32, (BLOCK, DH), 0) == 0

    def one_block(block, q, g):
        first, second = uses[0, block, 0], uses[0, block, 1]
        keys = jnp.concatenate([held[first, 0], held[second, 0]], axis=0)
        values = jnp.concatenate([held[first, 1], held[second, 1]], axis=0)
        scores = dot(q, keys, 1, 1) * scale
        weights = jnp.exp(scores - jnp.max(scores, axis=1, keepdims=True))
        probs = weights / jnp.sum(weights, axis=1, keepdims=True)
        probs_low = probs.astype(BF16)
        out = dot(probs_low, values, 1, 0)
        grad_probs = dot(g, values, 1, 1)
        inner = jnp.sum(probs * grad_probs, axis=1, keepdims=True)
        grad_scores = (probs * (grad_probs - inner) * scale).astype(BF16)
        grad_q = dot(grad_scores, keys, 1, 0)
        grad_keys = dot(grad_scores, q, 0, 0)
        grad_values = dot(probs_low, g, 0, 0)
        sums[first, 0] += grad_keys[:NBLEN]
        sums[second, 0] += grad_keys[NBLEN:]
        sums[first, 1] += grad_values[:NBLEN]
        sums[second, 1] += grad_values[NBLEN:]
        return out, grad_q

    def one_part(part, carry):
        q, g = (rows[part, n, BLOCK:].astype(BF16) for n in range(2))
        for n, result in enumerate(one_block(2 * part, q, g)):
            made[part, n, BLOCK:] = result
        q, g = (
            jnp.where(first_row, rows[part, n, :BLOCK], rows[part + 1, n, :BLOCK]).astype(BF16)
            for n in range(2)
        )
        for n, result in enumerate(one_block(2 * part + 1, q, g)):
            made[part + 1, n, :BLOCK] = result
            made[part, n, :1] = result[:1]
        return carry

    if parts <= 4:
        for part in range(parts):
            one_part(part, 0)
    else:
        lax.fori_loop(0, parts, one_part, 0)

    for part in range(parts):
        for n in range(2):
            rows_out[part, n] = pltpu.roll(made[part, n], 2 * BLOCK - 1, 0).astype(BF16)
    for step in range(seqs):
        kv_out[step][...] = sums[partner(me, step, seqs)].astype(BF16)


def attend(uses, rows_in, kv_in):
    parts, _, part_rows, chunk = rows_in.shape
    seqs = len(kv_in)
    heads = chunk // DH
    rows_spec = pl.BlockSpec((parts, 2, part_rows, DH), lambda i: (0, 0, 0, i))
    kv_spec = pl.BlockSpec((2, NBLEN, DH), lambda i: (0, 0, i))
    pairs = heads * parts * part_rows * 2 * NBLEN
    outs = pl.pallas_call(
        functools.partial(attend_kernel, seqs, parts),
        grid=(heads,),
        in_specs=[SCALARS, rows_spec] + [kv_spec] * seqs,
        out_specs=[rows_spec] + [kv_spec] * seqs,
        scratch_shapes=[
            pltpu.VMEM((seqs, 2, NBLEN, DH), BF16),
            pltpu.VMEM((parts + 1, 2, part_rows, DH), F32),
            pltpu.VMEM((parts + 1, 2, part_rows, DH), F32),
            pltpu.VMEM((seqs, 2, NBLEN, DH), F32),
        ],
        out_shape=[jax.ShapeDtypeStruct(rows_in.shape, BF16)]
        + [jax.ShapeDtypeStruct((2, NBLEN, chunk), BF16)] * seqs,
        compiler_params=PARAMS,
        cost_estimate=cost(8 * (seqs + parts) * NBLEN * chunk, 12 * DH * pairs, pairs),
        name="attend_blocks",
    )(uses, rows_in, *kv_in)
    return outs[0], outs[1:]


def owner_kernel(seqs, lists, *rest):
    ins, out_ref, acc = rest[:seqs], rest[-2], rest[-1]
    me = lax.axis_index("enc")
    acc[...] = jnp.zeros_like(acc)
    for step in range(seqs):
        acc[lists[0, partner(me, step, seqs), 0]] += ins[step][...].astype(F32)
    out_ref[...] = acc[...].astype(BF16)


def owner_sum(h, send_lists, returned, shape, so_far):
    seqs = len(returned)
    chunk = returned[0].shape[-1]
    wide = min(chunk, 256)
    steps = chunk // wide
    extra = [] if so_far is None else [so_far]
    return pl.pallas_call(
        functools.partial(owner_kernel, seqs),
        grid=(steps,),
        in_specs=[SCALARS]
        + [pl.BlockSpec((2, NBLEN, wide), lambda i: (0, 0, i))] * seqs
        + [ANYWHERE] * len(extra),
        out_specs=pl.BlockSpec(
            (shape[0], 2, NBLEN, wide), lambda i: (0, 0, 0, h * steps + i)
        ),
        scratch_shapes=[pltpu.VMEM((shape[0], 2, NBLEN, wide), F32)],
        out_shape=jax.ShapeDtypeStruct(shape, BF16),
        input_output_aliases={seqs + 1: 0} if extra else {},
        compiler_params=PARAMS,
        cost_estimate=cost(4 * (seqs + shape[0]) * NBLEN * chunk, seqs * 2 * NBLEN * chunk),
        name="owner_sum",
    )(send_lists, *returned, *extra)


class Exchanges:
    def __init__(self, count, depth):
        self.count, self.depth = count, depth
        self.far, self.near = [], []
        half = count // 2
        self.far_steps = list(range(half, count))
        self.near_steps = list(range(1, half))

    def run(self, pieces):
        got = [pieces[0]] + [None] * (self.count - 1)
        for steps, done, depth in (
            (self.far_steps, self.far, self.depth),
            (self.near_steps, self.near, 1),
        ):
            for step in steps:
                piece = pieces[step]
                if len(done) >= depth:
                    piece = after(piece, done[-depth])
                got[step] = exchange(piece, step, self.count)
                done.append(got[step])
        return got


def local(seqs, parts, queries, kv_pool, send_lists, block_slots, grad_context):
    width = kv_pool.shape[-1]
    chunks = min(CHUNKS, width // DH)
    chunk = width // chunks
    links = Exchanges(seqs, FAR_DEPTH)
    half = seqs // 2

    fetched, arrived = [], []
    for h in range(chunks):
        far = pick(h, range(half, seqs), send_lists, kv_pool, chunk)
        send_lists = after(send_lists, far[0])
        near = pick(h, range(half), send_lists, kv_pool, chunk)
        queries = after(queries, near[0])
        fetched.append(links.run(list(near) + list(far)))
        packed = pack(h, queries, grad_context, chunk, chunks, parts)
        send_lists = after(send_lists, packed)
        arrived.append(swap_rows(packed))
    pool_grads = None
    token_parts, returns = [], []
    for h in range(chunks):
        rows_out, kv_out = attend(block_slots, arrived[h], fetched[h])
        returns.append(links.run(kv_out))
        token_parts.append(swap_rows(rows_out))
    context, grad_queries = unpack(token_parts, queries.shape)
    for h in range(chunks):
        pool_grads = owner_sum(h, send_lists, returns[h], kv_pool.shape, pool_grads)
    return (context, grad_queries, pool_grads)


def solution(mesh):
    in_specs = (
        P("enc", "seq", None),
        P("enc", None, None, "seq"),
        P("enc", None, None),
        P("enc", None, None),
        P("enc", "seq", None),
    )
    out_specs = (P("enc", "seq", None), P("enc", "seq", None), P("enc", None, None, "seq"))
    body = functools.partial(local, mesh.shape["enc"], mesh.shape["seq"])
    return jax.shard_map(body, mesh=mesh, in_specs=in_specs, out_specs=out_specs, check_vma=False)
```

```python
import functools

import jax
import jax.numpy as jnp
from jax import lax
from jax.experimental import pallas as pl
from jax.experimental.pallas import tpu as pltpu
from jax.sharding import PartitionSpec as P

DH = 128
BLOCK = 64
NBLEN = 128
CHUNKS = 2
FAR_DEPTH = 4
F32 = jnp.float32
BF16 = jnp.bfloat16
VMEM_BYTES = 40 * 1024 * 1024


def partner(index, step, count):
    half = count // 2
    below = jnp.asarray(index) < half
    return jnp.where(below, half + (index + step) % half, (index - step) % half)


def exchange(array, step, count):
    half = count // 2
    there = [half + (i + step) % half for i in range(half)]
    pairs = list(enumerate(there)) + [(peer, i) for i, peer in enumerate(there)]
    return lax.ppermute(array, "enc", pairs)


def swap_near(array, count):
    half = count // 2
    groups = [list(range(half)), list(range(half, count))]
    return lax.all_to_all(
        array, "enc", split_axis=0, concat_axis=0, axis_index_groups=groups, tiled=True
    )


def swap_rows(array):
    return lax.all_to_all(array, "seq", split_axis=0, concat_axis=0, tiled=True)


def after(array, earlier):
    return lax.optimization_barrier((array, earlier))[0]


def in_hbm(shape):
    return pltpu.HBM(shape, BF16)


def cost(moved, flops=0, exps=0):
    return pl.CostEstimate(flops=flops, bytes_accessed=moved, transcendentals=exps)


PARAMS = pltpu.CompilerParams(vmem_limit_bytes=VMEM_BYTES)
SCALARS = pl.BlockSpec(memory_space=pltpu.SMEM)
ANYWHERE = pl.BlockSpec(memory_space=pl.ANY)


def pack_kernel(q_ref, g_ref, out_ref):
    out_ref[0, 0] = q_ref[0]
    out_ref[0, 1] = g_ref[0]


def pack(h, queries, grads, chunk, chunks, parts):
    rows = queries.shape[1]
    spec = pl.BlockSpec((1, rows, chunk), lambda i: (0, 0, i * chunks + h))
    return pl.pallas_call(
        pack_kernel,
        grid=(parts,),
        in_specs=[spec, spec],
        out_specs=pl.BlockSpec((1, 2, rows, chunk), lambda i: (i, 0, 0, 0)),
        out_shape=in_hbm((parts, 2, rows, chunk)),
        compiler_params=PARAMS,
        cost_estimate=cost(8 * parts * rows * chunk),
        name="pack_rows",
    )(queries, grads)


def unpack_kernel(chunks, *refs):
    ins, (ctx_ref, gq_ref) = refs[:chunks], refs[chunks:]
    chunk = ins[0].shape[-1]
    for h, ref in enumerate(ins):
        ctx_ref[0, :, h * chunk : (h + 1) * chunk] = ref[0, 0]
        gq_ref[0, :, h * chunk : (h + 1) * chunk] = ref[0, 1]


def unpack(pieces, shape):
    parts, _, rows, chunk = pieces[0].shape
    chunks = len(pieces)
    out_spec = pl.BlockSpec((1, rows, chunks * chunk), lambda i: (0, 0, i))
    return pl.pallas_call(
        functools.partial(unpack_kernel, chunks),
        grid=(parts,),
        in_specs=[pl.BlockSpec((1, 2, rows, chunk), lambda i: (i, 0, 0, 0))] * chunks,
        out_specs=[out_spec, out_spec],
        out_shape=[jax.ShapeDtypeStruct(shape, BF16)] * 2,
        compiler_params=PARAMS,
        cost_estimate=cost(8 * rows * shape[2]),
        name="unpack_rows",
    )(*pieces)


def pick_kernel(h, far, seqs, lists, pool_ref, *rest):
    outs, sems = rest[:-1], rest[-1]
    half = seqs // 2
    me = lax.axis_index("enc")
    copies = []
    for step in range(half):
        if far:
            peer, out = partner(me, step, seqs), outs[step]
        else:
            peer, out = me - me % half + step, outs[0].at[step]
        chunk = out.shape[-1]
        source = pool_ref.at[lists[0, peer, 0], :, :, h * chunk : (h + 1) * chunk]
        copies.append(pltpu.make_async_copy(source, out, sems.at[step]))
        copies[-1].start()
    for copy in copies:
        copy.wait()


def pick(h, far, send_lists, kv_pool, chunk):
    seqs = send_lists.shape[1]
    half = seqs // 2
    shapes = [(2, NBLEN, chunk)] * half if far else [(half, 2, NBLEN, chunk)]
    return pl.pallas_call(
        functools.partial(pick_kernel, h, far, seqs),
        grid=(1,),
        in_specs=[SCALARS, ANYWHERE],
        out_specs=[pl.BlockSpec(shape, lambda i, n=len(shape): (0,) * n) for shape in shapes],
        out_shape=[in_hbm(shape) for shape in shapes],
        scratch_shapes=[pltpu.SemaphoreType.DMA((half,))],
        compiler_params=PARAMS,
        cost_estimate=cost(8 * half * NBLEN * chunk),
        name="pick_far" if far else "pick_near",
    )(send_lists, kv_pool)


def dot(left, right, left_dim, right_dim):
    return lax.dot_general(
        left, right, (((left_dim,), (right_dim,)), ((), ())), preferred_element_type=F32
    )


def attend_kernel(seqs, parts, uses, rows_in, *rest):
    half = seqs // 2
    near_in, far_in, rest = rest[0], rest[1 : 1 + half], rest[1 + half :]
    rows_out, near_out, far_out, rest = rest[0], rest[1], rest[2 : 2 + half], rest[2 + half :]
    held, rows, made, sums = rest
    scale = DH ** (-0.5)
    me = lax.axis_index("enc")

    base = me - me % half
    for step in range(half):
        held[base + step] = near_in[step]
        held[partner(me, step, seqs)] = far_in[step][...]
    for part in range(parts):
        for n in range(2):
            rows[part, n] = pltpu.roll(rows_in[part, n].astype(F32), 1, 0)
    rows[parts] = jnp.zeros(rows.shape[1:], F32)
    made[0, :, :BLOCK] = jnp.zeros((2, BLOCK, DH), F32)
    sums[...] = jnp.zeros_like(sums)
    first_row = lax.broadcasted_iota(jnp.int32, (BLOCK, DH), 0) == 0

    def one_block(block, q, g):
        first, second = uses[0, block, 0], uses[0, block, 1]
        keys = jnp.concatenate([held[first, 0], held[second, 0]], axis=0)
        values = jnp.concatenate([held[first, 1], held[second, 1]], axis=0)
        scores = dot(q, keys, 1, 1) * scale
        weights = jnp.exp(scores - jnp.max(scores, axis=1, keepdims=True))
        probs = weights / jnp.sum(weights, axis=1, keepdims=True)
        probs_low = probs.astype(BF16)
        out = dot(probs_low, values, 1, 0)
        grad_probs = dot(g, values, 1, 1)
        inner = jnp.sum(probs * grad_probs, axis=1, keepdims=True)
        grad_scores = (probs * (grad_probs - inner) * scale).astype(BF16)
        grad_q = dot(grad_scores, keys, 1, 0)
        grad_keys = dot(grad_scores, q, 0, 0)
        grad_values = dot(probs_low, g, 0, 0)
        sums[first, 0] += grad_keys[:NBLEN]
        sums[second, 0] += grad_keys[NBLEN:]
        sums[first, 1] += grad_values[:NBLEN]
        sums[second, 1] += grad_values[NBLEN:]
        return out, grad_q

    def one_part(part, carry):
        q, g = (rows[part, n, BLOCK:].astype(BF16) for n in range(2))
        for n, result in enumerate(one_block(2 * part, q, g)):
            made[part, n, BLOCK:] = result
        q, g = (
            jnp.where(first_row, rows[part, n, :BLOCK], rows[part + 1, n, :BLOCK]).astype(BF16)
            for n in range(2)
        )
        for n, result in enumerate(one_block(2 * part + 1, q, g)):
            made[part + 1, n, :BLOCK] = result
            made[part, n, :1] = result[:1]
        return carry

    if parts <= 4:
        for part in range(parts):
            one_part(part, 0)
    else:
        lax.fori_loop(0, parts, one_part, 0)

    for part in range(parts):
        for n in range(2):
            rows_out[part, n] = pltpu.roll(made[part, n], 2 * BLOCK - 1, 0).astype(BF16)
    for step in range(half):
        near_out[step] = sums[base + step].astype(BF16)
        far_out[step][...] = sums[partner(me, step, seqs)].astype(BF16)


def attend(uses, rows_in, near_in, far_in):
    parts, _, part_rows, chunk = rows_in.shape
    half = len(far_in)
    seqs = 2 * half
    heads = chunk // DH
    rows_spec = pl.BlockSpec((parts, 2, part_rows, DH), lambda i: (0, 0, 0, i))
    near_spec = pl.BlockSpec((half, 2, NBLEN, DH), lambda i: (0, 0, 0, i))
    far_spec = pl.BlockSpec((2, NBLEN, DH), lambda i: (0, 0, i))
    pairs = heads * parts * part_rows * 2 * NBLEN
    outs = pl.pallas_call(
        functools.partial(attend_kernel, seqs, parts),
        grid=(heads,),
        in_specs=[SCALARS, rows_spec, near_spec] + [far_spec] * half,
        out_specs=[rows_spec, near_spec] + [far_spec] * half,
        scratch_shapes=[
            pltpu.VMEM((seqs, 2, NBLEN, DH), BF16),
            pltpu.VMEM((parts + 1, 2, part_rows, DH), F32),
            pltpu.VMEM((parts + 1, 2, part_rows, DH), F32),
            pltpu.VMEM((seqs, 2, NBLEN, DH), F32),
        ],
        out_shape=[in_hbm(rows_in.shape), in_hbm(near_in.shape)]
        + [in_hbm(array.shape) for array in far_in],
        compiler_params=PARAMS,
        cost_estimate=cost(8 * (seqs + parts) * NBLEN * chunk, 12 * DH * pairs, pairs),
        name="attend_blocks",
    )(uses, rows_in, near_in, *far_in)
    return outs[0], outs[1], outs[2:]


def owner_kernel(seqs, lists, near_ref, *rest):
    half = seqs // 2
    far_refs, out_ref, acc = rest[:half], rest[-2], rest[-1]
    me = lax.axis_index("enc")
    base = me - me % half
    acc[...] = jnp.zeros_like(acc)
    for step in range(half):
        acc[lists[0, base + step, 0]] += near_ref[step].astype(F32)
        acc[lists[0, partner(me, step, seqs), 0]] += far_refs[step][...].astype(F32)
    out_ref[...] = acc[...].astype(BF16)


def owner_sum(h, send_lists, near, far, shape, so_far):
    half = len(far)
    chunk = near.shape[-1]
    wide = min(chunk, 256)
    steps = chunk // wide
    extra = [] if so_far is None else [so_far]
    return pl.pallas_call(
        functools.partial(owner_kernel, 2 * half),
        grid=(steps,),
        in_specs=[SCALARS, pl.BlockSpec((half, 2, NBLEN, wide), lambda i: (0, 0, 0, i))]
        + [pl.BlockSpec((2, NBLEN, wide), lambda i: (0, 0, i))] * half
        + [ANYWHERE] * len(extra),
        out_specs=pl.BlockSpec(
            (shape[0], 2, NBLEN, wide), lambda i: (0, 0, 0, h * steps + i)
        ),
        scratch_shapes=[pltpu.VMEM((shape[0], 2, NBLEN, wide), F32)],
        out_shape=in_hbm(shape),
        input_output_aliases={half + 2: 0} if extra else {},
        compiler_params=PARAMS,
        cost_estimate=cost(4 * (2 * half + shape[0]) * NBLEN * chunk, 4 * half * NBLEN * chunk),
        name="owner_sum",
    )(send_lists, near, *far, *extra)


class FarExchanges:
    def __init__(self, count, depth):
        self.count, self.depth, self.done = count, depth, []

    def run(self, pieces):
        got = []
        for step, piece in enumerate(pieces):
            if len(self.done) >= self.depth:
                piece = after(piece, self.done[-self.depth])
            got.append(exchange(piece, step, self.count))
            self.done.append(got[-1])
        return got


def local(seqs, parts, queries, kv_pool, send_lists, block_slots, grad_context):
    width = kv_pool.shape[-1]
    chunks = min(CHUNKS, width // DH)
    chunk = width // chunks
    links = FarExchanges(seqs, FAR_DEPTH)

    arrived = []
    for h in range(chunks):
        far = links.run(pick(h, True, send_lists, kv_pool, chunk))
        near = swap_near(pick(h, False, send_lists, kv_pool, chunk)[0], seqs)
        rows = swap_rows(pack(h, queries, grad_context, chunk, chunks, parts))
        arrived.append((rows, near, far))
    pool_grads = None
    token_parts, returns = [], []
    for h in range(chunks):
        rows, near, far = attend(block_slots, *arrived[h])
        far = links.run(far)
        near = swap_near(near, seqs)
        returns.append((near, far))
        token_parts.append(swap_rows(rows))
    context, grad_queries = unpack(token_parts, queries.shape)
    for h in range(chunks):
        pool_grads = owner_sum(h, send_lists, *returns[h], kv_pool.shape, pool_grads)
    return (context, grad_queries, pool_grads)


def solution(mesh):
    in_specs = (
        P("enc", "seq", None),
        P("enc", None, None, "seq"),
        P("enc", None, None),
        P("enc", None, None),
        P("enc", "seq", None),
    )
    out_specs = (P("enc", "seq", None), P("enc", "seq", None), P("enc", None, None, "seq"))
    body = functools.partial(local, mesh.shape["enc"], mesh.shape["seq"])
    return jax.shard_map(body, mesh=mesh, in_specs=in_specs, out_specs=out_specs, check_vma=False)
```

```python
import functools

import jax
import jax.numpy as jnp
from jax import lax
from jax.experimental import pallas as pl
from jax.experimental.pallas import tpu as pltpu
from jax.sharding import PartitionSpec as P

DH = 128
BLOCK = 64
NBLEN = 128
GROUPS = 4
DEPTH = 2
F32 = jnp.float32
BF16 = jnp.bfloat16
VMEM_BYTES = 40 * 1024 * 1024


def partner(index, step, count):
    if count & (count - 1) == 0:
        return index ^ step
    return (step - index) % count


def exchange(array, axis, step, count):
    pairs = [(i, partner(i, step, count)) for i in range(count)]
    return lax.ppermute(array, axis, pairs)


def swap_rows(pieces):
    count = len(pieces)
    return [pieces[0]] + [exchange(pieces[step], "seq", step, count) for step in range(1, count)]


def swap_pool(array):
    return lax.all_to_all(array, "enc", split_axis=0, concat_axis=0, tiled=True)


def after(array, earlier):
    return lax.optimization_barrier((array, earlier))[0]


def in_hbm(shape):
    return pltpu.HBM(shape, BF16)


def cost(moved, flops=0, exps=0):
    return pl.CostEstimate(flops=flops, bytes_accessed=moved, transcendentals=exps)


PARAMS = pltpu.CompilerParams(vmem_limit_bytes=VMEM_BYTES)
SCALARS = pl.BlockSpec(memory_space=pltpu.SMEM)
ANYWHERE = pl.BlockSpec(memory_space=pl.ANY)
IN_HBM = pl.BlockSpec(memory_space=pltpu.HBM)


def pack_kernel(first, width, q_ref, g_ref, *rest):
    outs, sems = rest[:-1], rest[-1]
    parts, chunk = len(outs), outs[0].shape[-1]
    me = lax.axis_index("seq")
    copies = []
    for step, out in enumerate(outs):
        start = pl.multiple_of(partner(me, step, parts) * width + first, DH)
        for n, ref in enumerate((q_ref, g_ref)):
            source = ref.at[0, :, pl.ds(start, chunk)]
            copies.append(pltpu.make_async_copy(source, out.at[n], sems.at[2 * step + n]))
            copies[-1].start()
    for copy in copies:
        copy.wait()


def pack(first, chunk, queries, grads, width, parts):
    shape = (2, queries.shape[1], chunk)
    return pl.pallas_call(
        functools.partial(pack_kernel, first, width),
        grid=(1,),
        in_specs=[IN_HBM, IN_HBM],
        out_specs=[pl.BlockSpec(shape, lambda i: (0, 0, 0))] * parts,
        out_shape=[in_hbm(shape)] * parts,
        scratch_shapes=[pltpu.SemaphoreType.DMA((2 * parts,))],
        compiler_params=PARAMS,
        cost_estimate=cost(8 * parts * queries.shape[1] * chunk),
        name="pack_rows",
    )(queries, grads)


def unpack_kernel(firsts, width, *refs):
    ins, (ctx_ref, gq_ref, sems) = refs[:-3], refs[-3:]
    parts = len(ins) // len(firsts)
    me = lax.axis_index("seq")
    copies = []
    for n, src in enumerate(ins):
        first, step = firsts[n // parts], n % parts
        start = pl.multiple_of(partner(me, step, parts) * width + first, DH)
        for k, ref in enumerate((ctx_ref, gq_ref)):
            target = ref.at[0, :, pl.ds(start, src.shape[-1])]
            copies.append(pltpu.make_async_copy(src.at[k], target, sems.at[2 * n + k]))
            copies[-1].start()
    for copy in copies:
        copy.wait()


def unpack(pieces, firsts, width, shape):
    flat = [array for piece in pieces for array in piece]
    return pl.pallas_call(
        functools.partial(unpack_kernel, firsts, width),
        grid=(1,),
        in_specs=[pl.BlockSpec(array.shape, lambda i: (0, 0, 0)) for array in flat],
        out_specs=[IN_HBM, IN_HBM],
        out_shape=[in_hbm(shape)] * 2,
        scratch_shapes=[pltpu.SemaphoreType.DMA((2 * len(flat),))],
        compiler_params=PARAMS,
        cost_estimate=cost(8 * shape[1] * shape[2]),
        name="unpack_rows",
    )(*flat)


def pick_kernel(first, split, seqs, lists, pool_ref, *rest):
    outs, sems = rest[:-1], rest[-1]
    me = lax.axis_index("enc")
    copies = []
    for step in range(seqs):
        if split:
            peer, out = partner(me, step, seqs), outs[step]
        else:
            peer, out = step, outs[0].at[step]
        chunk = out.shape[-1]
        source = pool_ref.at[lists[0, peer, 0], :, :, first : first + chunk]
        copies.append(pltpu.make_async_copy(source, out, sems.at[step]))
        copies[-1].start()
    for copy in copies:
        copy.wait()


def pick(first, chunk, split, send_lists, kv_pool):
    seqs = send_lists.shape[1]
    shapes = [(2, NBLEN, chunk)] * seqs if split else [(seqs, 2, NBLEN, chunk)]
    return pl.pallas_call(
        functools.partial(pick_kernel, first, split, seqs),
        grid=(1,),
        in_specs=[SCALARS, IN_HBM],
        out_specs=[pl.BlockSpec(shape, lambda i, n=len(shape): (0,) * n) for shape in shapes],
        out_shape=[in_hbm(shape) for shape in shapes],
        scratch_shapes=[pltpu.SemaphoreType.DMA((seqs,))],
        compiler_params=PARAMS,
        cost_estimate=cost(8 * seqs * NBLEN * chunk),
        name="pick_split" if split else "pick_whole",
    )(send_lists, kv_pool)


def dot(left, right, left_dim, right_dim):
    return lax.dot_general(
        left, right, (((left_dim,), (right_dim,)), ((), ())), preferred_element_type=F32
    )


def attend_kernel(seqs, parts, split, uses, *rest):
    pieces = seqs if split else 1
    rows_in, rest = rest[:parts], rest[parts:]
    kv_in, rest = rest[:pieces], rest[pieces:]
    rows_out, rest = rest[:parts], rest[parts:]
    kv_out, rest = rest[:pieces], rest[pieces:]
    held, rows, made, sums = rest if split else (kv_in[0], *rest)
    scale = DH ** (-0.5)
    me, mine = lax.axis_index("enc"), lax.axis_index("seq")

    if split:
        for step in range(seqs):
            held[partner(me, step, seqs)] = kv_in[step][...]
    for step in range(parts):
        for n in range(2):
            piece = rows_in[step][n].astype(F32)
            rows[partner(mine, step, parts), n] = pltpu.roll(piece, 1, 0)
    rows[parts] = jnp.zeros(rows.shape[1:], F32)
    made[0, :, :BLOCK] = jnp.zeros((2, BLOCK, DH), F32)
    sums[...] = jnp.zeros_like(sums)
    first_row = lax.broadcasted_iota(jnp.int32, (BLOCK, DH), 0) == 0

    def one_block(block, q, g):
        first, second = uses[0, block, 0], uses[0, block, 1]
        keys = jnp.concatenate([held[first, 0], held[second, 0]], axis=0)
        values = jnp.concatenate([held[first, 1], held[second, 1]], axis=0)
        scores = dot(q, keys, 1, 1) * scale
        weights = jnp.exp(scores - jnp.max(scores, axis=1, keepdims=True))
        probs = weights / jnp.sum(weights, axis=1, keepdims=True)
        probs_low = probs.astype(BF16)
        out = dot(probs_low, values, 1, 0)
        grad_probs = dot(g, values, 1, 1)
        inner = jnp.sum(probs * grad_probs, axis=1, keepdims=True)
        grad_scores = (probs * (grad_probs - inner) * scale).astype(BF16)
        grad_q = dot(grad_scores, keys, 1, 0)
        grad_keys = dot(grad_scores, q, 0, 0)
        grad_values = dot(probs_low, g, 0, 0)
        sums[first, 0] += grad_keys[:NBLEN]
        sums[second, 0] += grad_keys[NBLEN:]
        sums[first, 1] += grad_values[:NBLEN]
        sums[second, 1] += grad_values[NBLEN:]
        return out, grad_q

    def one_part(part, carry):
        q, g = (rows[part, n, BLOCK:].astype(BF16) for n in range(2))
        for n, result in enumerate(one_block(2 * part, q, g)):
            made[part, n, BLOCK:] = result
        q, g = (
            jnp.where(first_row, rows[part, n, :BLOCK], rows[part + 1, n, :BLOCK]).astype(BF16)
            for n in range(2)
        )
        for n, result in enumerate(one_block(2 * part + 1, q, g)):
            made[part + 1, n, :BLOCK] = result
            made[part, n, :1] = result[:1]
        return carry

    if parts <= 4:
        for part in range(parts):
            one_part(part, 0)
    else:
        lax.fori_loop(0, parts, one_part, 0)

    for step in range(parts):
        for n in range(2):
            piece = made[partner(mine, step, parts), n]
            rows_out[step][n] = pltpu.roll(piece, 2 * BLOCK - 1, 0).astype(BF16)
    if split:
        for step in range(seqs):
            kv_out[step][...] = sums[partner(me, step, seqs)].astype(BF16)
    else:
        kv_out[0][...] = sums[...].astype(BF16)


def attend(first, uses, rows_in, kv_in):
    parts, part_rows = len(rows_in), rows_in[0].shape[1]
    split = len(kv_in) > 1
    seqs = len(kv_in) if split else kv_in[0].shape[0]
    chunk = kv_in[0].shape[-1]
    heads = chunk // DH
    skip = first // DH
    rows_block = (2, part_rows, DH)
    if split:
        kv_spec = pl.BlockSpec((2, NBLEN, DH), lambda i: (0, 0, i))
    else:
        kv_spec = pl.BlockSpec((seqs, 2, NBLEN, DH), lambda i: (0, 0, 0, i))
    held = [pltpu.VMEM((seqs, 2, NBLEN, DH), BF16)] if split else []
    pairs = heads * parts * part_rows * 2 * NBLEN
    outs = pl.pallas_call(
        functools.partial(attend_kernel, seqs, parts, split),
        grid=(heads,),
        in_specs=[SCALARS]
        + [pl.BlockSpec(rows_block, lambda i: (0, 0, skip + i))] * parts
        + [kv_spec] * len(kv_in),
        out_specs=[pl.BlockSpec(rows_block, lambda i: (0, 0, i))] * parts
        + [kv_spec] * len(kv_in),
        scratch_shapes=held
        + [
            pltpu.VMEM((parts + 1, 2, part_rows, DH), F32),
            pltpu.VMEM((parts + 1, 2, part_rows, DH), F32),
            pltpu.VMEM((seqs, 2, NBLEN, DH), F32),
        ],
        out_shape=[in_hbm((2, part_rows, chunk))] * parts
        + [in_hbm(array.shape) for array in kv_in],
        compiler_params=PARAMS,
        cost_estimate=cost(8 * (seqs + parts) * NBLEN * chunk, 12 * DH * pairs, pairs),
        name="attend_blocks",
    )(uses, *rows_in, *kv_in)
    return outs[:parts], outs[parts:]


def owner_kernel(seqs, pieces, lists, *rest):
    ins, out_ref, acc = rest[:pieces], rest[-2], rest[-1]
    me = lax.axis_index("enc")
    acc[...] = jnp.zeros_like(acc)
    for step in range(seqs):
        if pieces > 1:
            acc[lists[0, partner(me, step, seqs), 0]] += ins[step][...].astype(F32)
        else:
            acc[lists[0, step, 0]] += ins[0][step].astype(F32)
    out_ref[...] = acc[...].astype(BF16)


def owner_sum(first, send_lists, back, shape, so_far):
    seqs = send_lists.shape[1]
    pieces, chunk = len(back), back[0].shape[-1]
    wide = min(chunk, 256)
    skip, steps = first // wide, chunk // wide
    extra = [] if so_far is None else [so_far]
    if pieces > 1:
        spec = pl.BlockSpec((2, NBLEN, wide), lambda i: (0, 0, i))
    else:
        spec = pl.BlockSpec((seqs, 2, NBLEN, wide), lambda i: (0, 0, 0, i))
    return pl.pallas_call(
        functools.partial(owner_kernel, seqs, pieces),
        grid=(steps,),
        in_specs=[SCALARS] + [spec] * pieces + [ANYWHERE] * len(extra),
        out_specs=pl.BlockSpec(
            (shape[0], 2, NBLEN, wide), lambda i: (0, 0, 0, skip + i)
        ),
        scratch_shapes=[pltpu.VMEM((shape[0], 2, NBLEN, wide), F32)],
        out_shape=in_hbm(shape),
        input_output_aliases={pieces + 1: 0} if extra else {},
        compiler_params=PARAMS,
        cost_estimate=cost(4 * (seqs + shape[0]) * NBLEN * chunk, seqs * 2 * NBLEN * chunk),
        name="owner_sum",
    )(send_lists, *back, *extra)


class Chain:
    def __init__(self, count):
        self.count, self.done = count, []

    def swap(self, pieces):
        got = [pieces[0]] + [None] * (self.count - 1)
        half = self.count // 2
        for step in list(range(half, self.count)) + list(range(1, half)):
            piece = pieces[step]
            if len(self.done) >= DEPTH:
                piece = after(piece, self.done[-DEPTH])
            got[step] = exchange(piece, "enc", step, self.count)
            self.done.append(got[step])
        return got


def local(seqs, parts, queries, kv_pool, send_lists, block_slots, grad_context):
    width = kv_pool.shape[-1]
    groups = min(GROUPS, width // DH)
    chunk = width // groups
    chain = Chain(seqs)

    def swap(split, pieces):
        return chain.swap(pieces) if split else [swap_pool(pieces[0])]

    fetched, rows = [], []
    for group in range(groups):
        split = group % 2 == 1
        picked = pick(group * chunk, chunk, split, send_lists, kv_pool)
        send_lists = after(send_lists, picked[0])
        if group == 3:
            picked = after(picked, fetched[0])
        fetched.append(swap(split, picked))
        rows.append(swap_rows(pack(group * chunk, chunk, queries, grad_context, width, parts)))
    pool_grads = None
    token_parts, returns = [], []
    for group in range(groups):
        rows_out, kv_out = attend(0, block_slots, rows[group], fetched[group])
        block_slots = after(block_slots, rows_out[0])
        returns.append(swap(group % 2 == 1, kv_out))
        token_parts.append(swap_rows(rows_out))
    firsts = [group * chunk for group in range(groups)]
    context, grad_queries = unpack(token_parts, firsts, width, queries.shape)
    for group in range(groups):
        pool_grads = owner_sum(
            group * chunk, send_lists, returns[group], kv_pool.shape, pool_grads
        )
    return (context, grad_queries, pool_grads)


def solution(mesh):
    in_specs = (
        P("enc", "seq", None),
        P("enc", None, None, "seq"),
        P("enc", None, None),
        P("enc", None, None),
        P("enc", "seq", None),
    )
    out_specs = (P("enc", "seq", None), P("enc", "seq", None), P("enc", None, None, "seq"))
    body = functools.partial(local, mesh.shape["enc"], mesh.shape["seq"])
    return jax.shard_map(body, mesh=mesh, in_specs=in_specs, out_specs=out_specs, check_vma=False)
```

```python
import functools
import math

import jax
import jax.numpy as jnp
from jax import lax
from jax.experimental import pallas as pl
from jax.experimental.pallas import tpu as pltpu
from jax.sharding import PartitionSpec as P

DH = 128
BLOCK = 64
NBLEN = 128
F32 = jnp.float32
BF16 = jnp.bfloat16
VMEM_BYTES = 40 * 1024 * 1024


def partner(index, step, count):
    if count & (count - 1) == 0:
        return index ^ step
    return (step - index) % count


def exchange(array, axis, step, count):
    pairs = [(i, partner(i, step, count)) for i in range(count)]
    return lax.ppermute(array, axis, pairs)


def swap_rows(pieces):
    count = len(pieces)
    return [pieces[0]] + [exchange(pieces[step], "seq", step, count) for step in range(1, count)]


def swap_pool(array):
    return lax.all_to_all(array, "enc", split_axis=0, concat_axis=0, tiled=True)


def after(array, earlier):
    return lax.optimization_barrier((array, earlier))[0]


def in_hbm(shape):
    return pltpu.HBM(shape, BF16)


def cost(moved, flops=0, exps=0):
    return pl.CostEstimate(flops=flops, bytes_accessed=moved, transcendentals=exps)


PARAMS = pltpu.CompilerParams(vmem_limit_bytes=VMEM_BYTES)
SCALARS = pl.BlockSpec(memory_space=pltpu.SMEM)
ANYWHERE = pl.BlockSpec(memory_space=pl.ANY)
IN_HBM = pl.BlockSpec(memory_space=pltpu.HBM)


def pack_kernel(first, width, q_ref, g_ref, *rest):
    outs, sems = rest[:-1], rest[-1]
    parts, chunk = len(outs), outs[0].shape[-1]
    me = lax.axis_index("seq")
    copies = []
    for step, out in enumerate(outs):
        start = pl.multiple_of(partner(me, step, parts) * width + first, DH)
        for n, ref in enumerate((q_ref, g_ref)):
            source = ref.at[0, :, pl.ds(start, chunk)]
            copies.append(pltpu.make_async_copy(source, out.at[n], sems.at[2 * step + n]))
            copies[-1].start()
    for copy in copies:
        copy.wait()


def pack(first, chunk, queries, grads, width, parts):
    shape = (2, queries.shape[1], chunk)
    return pl.pallas_call(
        functools.partial(pack_kernel, first, width),
        grid=(1,),
        in_specs=[IN_HBM, IN_HBM],
        out_specs=[pl.BlockSpec(shape, lambda i: (0, 0, 0))] * parts,
        out_shape=[in_hbm(shape)] * parts,
        scratch_shapes=[pltpu.SemaphoreType.DMA((2 * parts,))],
        compiler_params=PARAMS,
        cost_estimate=cost(8 * parts * queries.shape[1] * chunk),
        name="pack_rows",
    )(queries, grads)


def unpack_kernel(firsts, width, *refs):
    ins, (ctx_ref, gq_ref, sems) = refs[:-3], refs[-3:]
    parts = len(ins) // len(firsts)
    me = lax.axis_index("seq")
    copies = []
    for n, src in enumerate(ins):
        first, step = firsts[n // parts], n % parts
        start = pl.multiple_of(partner(me, step, parts) * width + first, DH)
        for k, ref in enumerate((ctx_ref, gq_ref)):
            target = ref.at[0, :, pl.ds(start, src.shape[-1])]
            copies.append(pltpu.make_async_copy(src.at[k], target, sems.at[2 * n + k]))
            copies[-1].start()
    for copy in copies:
        copy.wait()


def unpack(pieces, firsts, width, shape):
    flat = [array for piece in pieces for array in piece]
    return pl.pallas_call(
        functools.partial(unpack_kernel, firsts, width),
        grid=(1,),
        in_specs=[pl.BlockSpec(array.shape, lambda i: (0, 0, 0)) for array in flat],
        out_specs=[IN_HBM, IN_HBM],
        out_shape=[in_hbm(shape)] * 2,
        scratch_shapes=[pltpu.SemaphoreType.DMA((2 * len(flat),))],
        compiler_params=PARAMS,
        cost_estimate=cost(8 * shape[1] * shape[2]),
        name="unpack_rows",
    )(*flat)


def pick_kernel(first, split, seqs, lists, pool_ref, *rest):
    outs, sems = rest[:-1], rest[-1]
    me = lax.axis_index("enc")
    copies = []
    for step in range(seqs):
        if split:
            peer, out = partner(me, step, seqs), outs[step]
        else:
            peer, out = step, outs[0].at[step]
        chunk = out.shape[-1]
        source = pool_ref.at[lists[0, peer, 0], :, :, first : first + chunk]
        copies.append(pltpu.make_async_copy(source, out, sems.at[step]))
        copies[-1].start()
    for copy in copies:
        copy.wait()


def pick(first, chunk, split, send_lists, kv_pool):
    seqs = send_lists.shape[1]
    shapes = [(2, NBLEN, chunk)] * seqs if split else [(seqs, 2, NBLEN, chunk)]
    return pl.pallas_call(
        functools.partial(pick_kernel, first, split, seqs),
        grid=(1,),
        in_specs=[SCALARS, IN_HBM],
        out_specs=[pl.BlockSpec(shape, lambda i, n=len(shape): (0,) * n) for shape in shapes],
        out_shape=[in_hbm(shape) for shape in shapes],
        scratch_shapes=[pltpu.SemaphoreType.DMA((seqs,))],
        compiler_params=PARAMS,
        cost_estimate=cost(8 * seqs * NBLEN * chunk),
        name="pick_split" if split else "pick_whole",
    )(send_lists, kv_pool)


def dot(left, right, left_dim, right_dim):
    return lax.dot_general(
        left, right, (((left_dim,), (right_dim,)), ((), ())), preferred_element_type=F32
    )


def attend_kernel(seqs, parts, split, uses, *rest):
    pieces = seqs if split else 1
    rows_in, rest = rest[:parts], rest[parts:]
    kv_in, rest = rest[:pieces], rest[pieces:]
    rows_out, rest = rest[:parts], rest[parts:]
    kv_out, rest = rest[:pieces], rest[pieces:]
    held, rows, made, sums = rest if split else (kv_in[0], *rest)
    scale = DH ** (-0.5)
    me, mine = lax.axis_index("enc"), lax.axis_index("seq")

    if split:
        for step in range(seqs):
            held[partner(me, step, seqs)] = kv_in[step][...]
    for step in range(parts):
        for n in range(2):
            piece = rows_in[step][n].astype(F32)
            rows[partner(mine, step, parts), n] = pltpu.roll(piece, 1, 0)
    rows[parts] = jnp.zeros(rows.shape[1:], F32)
    made[0, :, :BLOCK] = jnp.zeros((2, BLOCK, DH), F32)
    sums[...] = jnp.zeros_like(sums)
    first_row = lax.broadcasted_iota(jnp.int32, (BLOCK, DH), 0) == 0

    def one_block(block, q, g):
        first, second = uses[0, block, 0], uses[0, block, 1]
        keys = jnp.concatenate([held[first, 0], held[second, 0]], axis=0)
        values = jnp.concatenate([held[first, 1], held[second, 1]], axis=0)
        scores = dot(q, keys, 1, 1) * scale
        weights = jnp.exp(scores - jnp.max(scores, axis=1, keepdims=True))
        probs = weights / jnp.sum(weights, axis=1, keepdims=True)
        probs_low = probs.astype(BF16)
        out = dot(probs_low, values, 1, 0)
        grad_probs = dot(g, values, 1, 1)
        inner = jnp.sum(probs * grad_probs, axis=1, keepdims=True)
        grad_scores = (probs * (grad_probs - inner) * scale).astype(BF16)
        grad_q = dot(grad_scores, keys, 1, 0)
        grad_keys = dot(grad_scores, q, 0, 0)
        grad_values = dot(probs_low, g, 0, 0)
        sums[first, 0] += grad_keys[:NBLEN]
        sums[second, 0] += grad_keys[NBLEN:]
        sums[first, 1] += grad_values[:NBLEN]
        sums[second, 1] += grad_values[NBLEN:]
        return out, grad_q

    def one_part(part, carry):
        q, g = (rows[part, n, BLOCK:].astype(BF16) for n in range(2))
        for n, result in enumerate(one_block(2 * part, q, g)):
            made[part, n, BLOCK:] = result
        q, g = (
            jnp.where(first_row, rows[part, n, :BLOCK], rows[part + 1, n, :BLOCK]).astype(BF16)
            for n in range(2)
        )
        for n, result in enumerate(one_block(2 * part + 1, q, g)):
            made[part + 1, n, :BLOCK] = result
            made[part, n, :1] = result[:1]
        return carry

    if parts <= 4:
        for part in range(parts):
            one_part(part, 0)
    else:
        lax.fori_loop(0, parts, one_part, 0)

    for step in range(parts):
        for n in range(2):
            piece = made[partner(mine, step, parts), n]
            rows_out[step][n] = pltpu.roll(piece, 2 * BLOCK - 1, 0).astype(BF16)
    if split:
        for step in range(seqs):
            kv_out[step][...] = sums[partner(me, step, seqs)].astype(BF16)
    else:
        kv_out[0][...] = sums[...].astype(BF16)


def attend(first, uses, rows_in, kv_in):
    parts, part_rows = len(rows_in), rows_in[0].shape[1]
    split = len(kv_in) > 1
    seqs = len(kv_in) if split else kv_in[0].shape[0]
    chunk = kv_in[0].shape[-1]
    heads = chunk // DH
    skip = first // DH
    rows_block = (2, part_rows, DH)
    if split:
        kv_spec = pl.BlockSpec((2, NBLEN, DH), lambda i: (0, 0, i))
    else:
        kv_spec = pl.BlockSpec((seqs, 2, NBLEN, DH), lambda i: (0, 0, 0, i))
    held = [pltpu.VMEM((seqs, 2, NBLEN, DH), BF16)] if split else []
    pairs = heads * parts * part_rows * 2 * NBLEN
    outs = pl.pallas_call(
        functools.partial(attend_kernel, seqs, parts, split),
        grid=(heads,),
        in_specs=[SCALARS]
        + [pl.BlockSpec(rows_block, lambda i: (0, 0, skip + i))] * parts
        + [kv_spec] * len(kv_in),
        out_specs=[pl.BlockSpec(rows_block, lambda i: (0, 0, i))] * parts
        + [kv_spec] * len(kv_in),
        scratch_shapes=held
        + [
            pltpu.VMEM((parts + 1, 2, part_rows, DH), F32),
            pltpu.VMEM((parts + 1, 2, part_rows, DH), F32),
            pltpu.VMEM((seqs, 2, NBLEN, DH), F32),
        ],
        out_shape=[in_hbm((2, part_rows, chunk))] * parts
        + [in_hbm(array.shape) for array in kv_in],
        compiler_params=PARAMS,
        cost_estimate=cost(8 * (seqs + parts) * NBLEN * chunk, 12 * DH * pairs, pairs),
        name="attend_blocks",
    )(uses, *rows_in, *kv_in)
    return outs[:parts], outs[parts:]


def owner_kernel(seqs, pieces, lists, *rest):
    ins, out_ref, acc = rest[:pieces], rest[-2], rest[-1]
    me = lax.axis_index("enc")
    acc[...] = jnp.zeros_like(acc)
    for step in range(seqs):
        if pieces > 1:
            acc[lists[0, partner(me, step, seqs), 0]] += ins[step][...].astype(F32)
        else:
            acc[lists[0, step, 0]] += ins[0][step].astype(F32)
    out_ref[...] = acc[...].astype(BF16)


def owner_sum(first, send_lists, back, shape, so_far):
    seqs = send_lists.shape[1]
    pieces, chunk = len(back), back[0].shape[-1]
    wide = math.gcd(math.gcd(first, chunk), 256)
    skip, steps = first // wide, chunk // wide
    extra = [] if so_far is None else [so_far]
    if pieces > 1:
        spec = pl.BlockSpec((2, NBLEN, wide), lambda i: (0, 0, i))
    else:
        spec = pl.BlockSpec((seqs, 2, NBLEN, wide), lambda i: (0, 0, 0, i))
    return pl.pallas_call(
        functools.partial(owner_kernel, seqs, pieces),
        grid=(steps,),
        in_specs=[SCALARS] + [spec] * pieces + [ANYWHERE] * len(extra),
        out_specs=pl.BlockSpec(
            (shape[0], 2, NBLEN, wide), lambda i: (0, 0, 0, skip + i)
        ),
        scratch_shapes=[pltpu.VMEM((shape[0], 2, NBLEN, wide), F32)],
        out_shape=in_hbm(shape),
        input_output_aliases={pieces + 1: 0} if extra else {},
        compiler_params=PARAMS,
        cost_estimate=cost(4 * (seqs + shape[0]) * NBLEN * chunk, seqs * 2 * NBLEN * chunk),
        name="owner_sum",
    )(send_lists, *back, *extra)


def swap_split(pieces, depth):
    count = len(pieces)
    half = count // 2
    got = [pieces[0]] + [None] * (count - 1)
    for step in list(range(half, count)) + list(range(1, half)):
        piece = pieces[step]
        if step >= half + depth:
            piece = after(piece, got[step - depth])
        got[step] = exchange(piece, "enc", step, count)
    return got


def local(seqs, parts, queries, kv_pool, send_lists, block_slots, grad_context):
    width = kv_pool.shape[-1]
    heads = width // DH
    half = seqs // 2
    cut = [heads // 4, heads // 4 + max(1, 3 * heads // 8)]
    firsts = [0, cut[0] * DH, cut[1] * DH]
    sizes = [cut[0] * DH, (cut[1] - cut[0]) * DH, width - cut[1] * DH]

    def choose(group):
        return pick(firsts[group], sizes[group], group == 1, send_lists, kv_pool)

    def rows_of(group):
        return swap_rows(pack(firsts[group], sizes[group], queries, grad_context, width, parts))

    picked = choose(0)
    send_lists = after(send_lists, picked[0])
    early = [swap_pool(picked[0])]
    picked = choose(1)
    send_lists, queries = after((send_lists, queries), picked[0])
    split = swap_split(picked, half)
    rows = [rows_of(0), rows_of(1)]
    late = [swap_pool(choose(2)[0])]
    rows.append(rows_of(2))

    early, split = lax.optimization_barrier((early, split))
    early_rows, early_back = attend(0, block_slots, rows[0], early)
    block_slots = after(block_slots, early_rows[0])
    split_rows, split_back = attend(0, block_slots, rows[1], split)
    block_slots = after(block_slots, split_rows[0])
    early_back = [swap_pool(early_back[0])]
    split_back = swap_split(split_back, 2)
    late = after(late, split_back[half : half + 2])
    late_rows, late_back = attend(0, block_slots, rows[2], late)
    late_back = [swap_pool(late_back[0])]

    token_parts = [swap_rows(piece) for piece in (early_rows, split_rows, late_rows)]
    context, grad_queries = unpack(token_parts, firsts, width, queries.shape)
    pool_grads = None
    for first, back in zip(firsts, (early_back, split_back, late_back)):
        pool_grads = owner_sum(first, send_lists, back, kv_pool.shape, pool_grads)
    return (context, grad_queries, pool_grads)


def solution(mesh):
    in_specs = (
        P("enc", "seq", None),
        P("enc", None, None, "seq"),
        P("enc", None, None),
        P("enc", None, None),
        P("enc", "seq", None),
    )
    out_specs = (P("enc", "seq", None), P("enc", "seq", None), P("enc", None, None, "seq"))
    body = functools.partial(local, mesh.shape["enc"], mesh.shape["seq"])
    return jax.shard_map(body, mesh=mesh, in_specs=in_specs, out_specs=out_specs, check_vma=False)
```

```python
import functools

import jax
import jax.numpy as jnp
from jax import lax
from jax.experimental import pallas as pl
from jax.experimental.pallas import tpu as pltpu
from jax.sharding import PartitionSpec as P

DH = 128
BLOCK = 64
NBLEN = 128
CHUNKS = 2
DEPTH = 4
ATTEND_WEIGHT = 24
F32 = jnp.float32
BF16 = jnp.bfloat16
VMEM_BYTES = 40 * 1024 * 1024


def partner(index, step, count):
    if count & (count - 1) == 0:
        return index ^ step
    return (step - index) % count


def exchange(array, axis, step, count):
    pairs = [(i, partner(i, step, count)) for i in range(count)]
    return lax.ppermute(array, axis, pairs)


def across(index, step, count):
    half = count // 2
    there = half + (index + step) % half
    return jnp.where(index < half, there, (index - step) % half)


def swap_near(array, count):
    half = count // 2
    groups = [list(range(half)), list(range(half, count))]
    return lax.all_to_all(
        array, "enc", split_axis=0, concat_axis=0, axis_index_groups=groups, tiled=True
    )


def swap_rows(pieces):
    count = len(pieces)
    return [pieces[0]] + [exchange(pieces[step], "seq", step, count) for step in range(1, count)]


def swap_pool(array):
    return lax.all_to_all(array, "enc", split_axis=0, concat_axis=0, tiled=True)


def after(array, earlier):
    return lax.optimization_barrier((array, earlier))[0]


def in_hbm(shape):
    return pltpu.HBM(shape, BF16)


def cost(moved, flops=0, exps=0):
    return pl.CostEstimate(flops=flops, bytes_accessed=moved, transcendentals=exps)


PARAMS = pltpu.CompilerParams(vmem_limit_bytes=VMEM_BYTES)
SCALARS = pl.BlockSpec(memory_space=pltpu.SMEM)
ANYWHERE = pl.BlockSpec(memory_space=pl.ANY)
IN_HBM = pl.BlockSpec(memory_space=pltpu.HBM)


def pack_kernel(first, width, q_ref, g_ref, *rest):
    outs, sems = rest[:-1], rest[-1]
    parts, chunk = len(outs), outs[0].shape[-1]
    me = lax.axis_index("seq")
    copies = []
    for step, out in enumerate(outs):
        start = pl.multiple_of(partner(me, step, parts) * width + first, DH)
        for n, ref in enumerate((q_ref, g_ref)):
            source = ref.at[0, :, pl.ds(start, chunk)]
            copies.append(pltpu.make_async_copy(source, out.at[n], sems.at[2 * step + n]))
            copies[-1].start()
    for copy in copies:
        copy.wait()


def pack(first, chunk, queries, grads, width, parts):
    shape = (2, queries.shape[1], chunk)
    return pl.pallas_call(
        functools.partial(pack_kernel, first, width),
        grid=(1,),
        in_specs=[IN_HBM, IN_HBM],
        out_specs=[pl.BlockSpec(shape, lambda i: (0, 0, 0))] * parts,
        out_shape=[in_hbm(shape)] * parts,
        scratch_shapes=[pltpu.SemaphoreType.DMA((2 * parts,))],
        compiler_params=PARAMS,
        cost_estimate=cost(8 * parts * queries.shape[1] * chunk),
        name="pack_rows",
    )(queries, grads)


def unpack_kernel(firsts, width, *refs):
    ins, (ctx_ref, gq_ref, sems) = refs[:-3], refs[-3:]
    parts = len(ins) // len(firsts)
    me = lax.axis_index("seq")
    copies = []
    for n, src in enumerate(ins):
        first, step = firsts[n // parts], n % parts
        start = pl.multiple_of(partner(me, step, parts) * width + first, DH)
        for k, ref in enumerate((ctx_ref, gq_ref)):
            target = ref.at[0, :, pl.ds(start, src.shape[-1])]
            copies.append(pltpu.make_async_copy(src.at[k], target, sems.at[2 * n + k]))
            copies[-1].start()
    for copy in copies:
        copy.wait()


def unpack(pieces, firsts, width, shape):
    flat = [array for piece in pieces for array in piece]
    return pl.pallas_call(
        functools.partial(unpack_kernel, firsts, width),
        grid=(1,),
        in_specs=[pl.BlockSpec(array.shape, lambda i: (0, 0, 0)) for array in flat],
        out_specs=[IN_HBM, IN_HBM],
        out_shape=[in_hbm(shape)] * 2,
        scratch_shapes=[pltpu.SemaphoreType.DMA((2 * len(flat),))],
        compiler_params=PARAMS,
        cost_estimate=cost(8 * shape[1] * shape[2]),
        name="unpack_rows",
    )(*flat)


def pick_kernel(first, lists, pool_ref, out_ref, sems):
    copies = []
    for seq in range(out_ref.shape[0]):
        source = pool_ref.at[lists[0, seq, 0], :, :, first : first + out_ref.shape[-1]]
        copies.append(pltpu.make_async_copy(source, out_ref.at[seq], sems.at[seq]))
        copies[-1].start()
    for copy in copies:
        copy.wait()


def pick(first, chunk, send_lists, kv_pool):
    shape = (send_lists.shape[1], 2, NBLEN, chunk)
    return pl.pallas_call(
        functools.partial(pick_kernel, first),
        grid=(1,),
        in_specs=[SCALARS, IN_HBM],
        out_specs=pl.BlockSpec(shape, lambda i: (0, 0, 0, 0)),
        out_shape=in_hbm(shape),
        scratch_shapes=[pltpu.SemaphoreType.DMA((shape[0],))],
        compiler_params=PARAMS,
        cost_estimate=cost(8 * shape[0] * NBLEN * chunk),
        name="pick_entries",
    )(send_lists, kv_pool)


def dot(left, right, left_dim, right_dim):
    return lax.dot_general(
        left, right, (((left_dim,), (right_dim,)), ((), ())), preferred_element_type=F32
    )


def attend_kernel(seqs, parts, uses, *rest):
    half = seqs // 2
    rows_in, held, rest = rest[:parts], rest[parts], rest[parts + 1 :]
    rows_out, near_out, rest = rest[:parts], rest[parts], rest[parts + 1 :]
    far_out, (rows, made, sums) = rest[:half], rest[half:]
    scale = DH ** (-0.5)
    me, mine = lax.axis_index("enc"), lax.axis_index("seq")

    for step in range(parts):
        for n in range(2):
            piece = rows_in[step][n].astype(F32)
            rows[partner(mine, step, parts), n] = pltpu.roll(piece, 1, 0)
    rows[parts] = jnp.zeros(rows.shape[1:], F32)
    made[0, :, :BLOCK] = jnp.zeros((2, BLOCK, DH), F32)
    sums[...] = jnp.zeros_like(sums)
    first_row = lax.broadcasted_iota(jnp.int32, (BLOCK, DH), 0) == 0

    def one_block(block, q, g):
        first, second = uses[0, block, 0], uses[0, block, 1]
        keys = jnp.concatenate([held[first, 0], held[second, 0]], axis=0)
        values = jnp.concatenate([held[first, 1], held[second, 1]], axis=0)
        scores = dot(q, keys, 1, 1) * scale
        weights = jnp.exp(scores - jnp.max(scores, axis=1, keepdims=True))
        probs = weights / jnp.sum(weights, axis=1, keepdims=True)
        probs_low = probs.astype(BF16)
        out = dot(probs_low, values, 1, 0)
        grad_probs = dot(g, values, 1, 1)
        inner = jnp.sum(probs * grad_probs, axis=1, keepdims=True)
        grad_scores = (probs * (grad_probs - inner) * scale).astype(BF16)
        grad_q = dot(grad_scores, keys, 1, 0)
        grad_keys = dot(grad_scores, q, 0, 0)
        grad_values = dot(probs_low, g, 0, 0)
        sums[first, 0] += grad_keys[:NBLEN]
        sums[second, 0] += grad_keys[NBLEN:]
        sums[first, 1] += grad_values[:NBLEN]
        sums[second, 1] += grad_values[NBLEN:]
        return out, grad_q

    def one_part(part, carry):
        q, g = (rows[part, n, BLOCK:].astype(BF16) for n in range(2))
        for n, result in enumerate(one_block(2 * part, q, g)):
            made[part, n, BLOCK:] = result
        q, g = (
            jnp.where(first_row, rows[part, n, :BLOCK], rows[part + 1, n, :BLOCK]).astype(BF16)
            for n in range(2)
        )
        for n, result in enumerate(one_block(2 * part + 1, q, g)):
            made[part + 1, n, :BLOCK] = result
            made[part, n, :1] = result[:1]
        return carry

    if parts <= 4:
        for part in range(parts):
            one_part(part, 0)
    else:
        lax.fori_loop(0, parts, one_part, 0)

    for step in range(parts):
        for n in range(2):
            piece = made[partner(mine, step, parts), n]
            rows_out[step][n] = pltpu.roll(piece, 2 * BLOCK - 1, 0).astype(BF16)
    base = me - me % half
    for step in range(half):
        near_out[step] = sums[base + step].astype(BF16)
        far_out[step][...] = sums[across(me, step, seqs)].astype(BF16)


def attend(uses, rows_in, arrived):
    parts, part_rows = len(rows_in), rows_in[0].shape[1]
    seqs, _, _, chunk = arrived.shape
    half, heads = seqs // 2, chunk // DH
    rows_spec = pl.BlockSpec((2, part_rows, DH), lambda i: (0, 0, i))
    far_spec = pl.BlockSpec((2, NBLEN, DH), lambda i: (0, 0, i))
    pairs = heads * parts * part_rows * 2 * NBLEN
    outs = pl.pallas_call(
        functools.partial(attend_kernel, seqs, parts),
        grid=(heads,),
        in_specs=[SCALARS]
        + [rows_spec] * parts
        + [pl.BlockSpec((seqs, 2, NBLEN, DH), lambda i: (0, 0, 0, i))],
        out_specs=[rows_spec] * parts
        + [pl.BlockSpec((half, 2, NBLEN, DH), lambda i: (0, 0, 0, i))]
        + [far_spec] * half,
        scratch_shapes=[
            pltpu.VMEM((parts + 1, 2, part_rows, DH), F32),
            pltpu.VMEM((parts + 1, 2, part_rows, DH), F32),
            pltpu.VMEM((seqs, 2, NBLEN, DH), F32),
        ],
        out_shape=[in_hbm((2, part_rows, chunk))] * parts
        + [in_hbm((half, 2, NBLEN, chunk))]
        + [in_hbm((2, NBLEN, chunk))] * half,
        compiler_params=PARAMS,
        cost_estimate=cost(
            8 * (seqs + parts) * NBLEN * chunk, ATTEND_WEIGHT * 12 * DH * pairs, pairs
        ),
        name="attend_blocks",
    )(uses, *rows_in, arrived)
    return outs[:parts], outs[parts], outs[parts + 1 :]


def owner_kernel(seqs, lists, near_ref, *rest):
    half = seqs // 2
    far_refs, out_ref, acc = rest[:half], rest[-2], rest[-1]
    me = lax.axis_index("enc")
    base = me - me % half
    acc[...] = jnp.zeros_like(acc)
    for step in range(half):
        acc[lists[0, base + step, 0]] += near_ref[step].astype(F32)
        acc[lists[0, across(me, step, seqs), 0]] += far_refs[step][...].astype(F32)
    out_ref[...] = acc[...].astype(BF16)


def owner_sum(h, send_lists, near, far, shape, so_far):
    half = len(far)
    chunk = near.shape[-1]
    wide = min(chunk, 256)
    steps = chunk // wide
    extra = [] if so_far is None else [so_far]
    return pl.pallas_call(
        functools.partial(owner_kernel, 2 * half),
        grid=(steps,),
        in_specs=[SCALARS, pl.BlockSpec((half, 2, NBLEN, wide), lambda i: (0, 0, 0, i))]
        + [pl.BlockSpec((2, NBLEN, wide), lambda i: (0, 0, i))] * half
        + [ANYWHERE] * len(extra),
        out_specs=pl.BlockSpec(
            (shape[0], 2, NBLEN, wide), lambda i: (0, 0, 0, h * steps + i)
        ),
        scratch_shapes=[pltpu.VMEM((shape[0], 2, NBLEN, wide), F32)],
        out_shape=in_hbm(shape),
        input_output_aliases={half + 2: 0} if extra else {},
        compiler_params=PARAMS,
        cost_estimate=cost(4 * (2 * half + shape[0]) * NBLEN * chunk, 4 * half * NBLEN * chunk),
        name="owner_sum",
    )(send_lists, near, *far, *extra)


def swap_far(pieces, done):
    half = len(pieces)
    there = [[half + (i + step) % half for i in range(half)] for step in range(half)]
    got = []
    for step, piece in enumerate(pieces):
        if len(done) >= DEPTH:
            piece = after(piece, done[-DEPTH])
        pairs = list(enumerate(there[step])) + [(peer, i) for i, peer in enumerate(there[step])]
        got.append(lax.ppermute(piece, "enc", pairs))
        done.append(got[-1])
    return got


def local(seqs, parts, queries, kv_pool, send_lists, block_slots, grad_context):
    width = kv_pool.shape[-1]
    chunks = min(CHUNKS, width // DH)
    chunk = width // chunks
    firsts = [h * chunk for h in range(chunks)]

    arrived, rows = [], []
    for first in firsts:
        picked = pick(first, chunk, send_lists, kv_pool)
        send_lists, queries = after((send_lists, queries), picked)
        arrived.append(swap_pool(picked))
        rows.append(swap_rows(pack(first, chunk, queries, grad_context, width, parts)))
    done, returns, token_parts = [], [], []
    for h in range(chunks):
        rows_out, near, far = attend(block_slots, rows[h], arrived[h])
        far = swap_far(far, done)
        if h > 0:
            near, rows_out = after((near, rows_out), done[:DEPTH])
        returns.append((swap_near(near, seqs), far))
        token_parts.append(swap_rows(rows_out))
    context, grad_queries = unpack(token_parts, firsts, width, queries.shape)
    pool_grads = None
    for h in range(chunks):
        pool_grads = owner_sum(h, send_lists, *returns[h], kv_pool.shape, pool_grads)
    return (context, grad_queries, pool_grads)


def solution(mesh):
    in_specs = (
        P("enc", "seq", None),
        P("enc", None, None, "seq"),
        P("enc", None, None),
        P("enc", None, None),
        P("enc", "seq", None),
    )
    out_specs = (P("enc", "seq", None), P("enc", "seq", None), P("enc", None, None, "seq"))
    body = functools.partial(local, mesh.shape["enc"], mesh.shape["seq"])
    return jax.shard_map(body, mesh=mesh, in_specs=in_specs, out_specs=out_specs, check_vma=False)
```

```python
import functools

import jax
import jax.numpy as jnp
from jax import lax
from jax.experimental import pallas as pl
from jax.experimental.pallas import tpu as pltpu
from jax.sharding import PartitionSpec as P

DH = 128
BLOCK = 64
NBLEN = 128
CHUNKS = 2
DEPTH = 4
ATTEND_WEIGHT = 24
F32 = jnp.float32
BF16 = jnp.bfloat16
VMEM_BYTES = 40 * 1024 * 1024


def partner(index, step, count):
    if count & (count - 1) == 0:
        return index ^ step
    return (step - index) % count


def exchange(array, axis, step, count):
    pairs = [(i, partner(i, step, count)) for i in range(count)]
    return lax.ppermute(array, axis, pairs)


def across(index, step, count):
    half = count // 2
    there = half + (index + step) % half
    return jnp.where(index < half, there, (index - step) % half)


def swap_near(array, count):
    half = count // 2
    groups = [list(range(half)), list(range(half, count))]
    return lax.all_to_all(
        array, "enc", split_axis=0, concat_axis=0, axis_index_groups=groups, tiled=True
    )


def swap_rows(pieces):
    count = len(pieces)
    got = [pieces[0]]
    for step in range(1, count):
        piece = pieces[step]
        if step > 1:
            piece = after(piece, got[-1])
        got.append(exchange(piece, "seq", step, count))
    return got


def swap_pool(array):
    return lax.all_to_all(array, "enc", split_axis=0, concat_axis=0, tiled=True)


def after(array, earlier):
    return lax.optimization_barrier((array, earlier))[0]


def in_hbm(shape):
    return pltpu.HBM(shape, BF16)


def cost(moved, flops=0, exps=0):
    return pl.CostEstimate(flops=flops, bytes_accessed=moved, transcendentals=exps)


PARAMS = pltpu.CompilerParams(vmem_limit_bytes=VMEM_BYTES)
SCALARS = pl.BlockSpec(memory_space=pltpu.SMEM)
ANYWHERE = pl.BlockSpec(memory_space=pl.ANY)
IN_HBM = pl.BlockSpec(memory_space=pltpu.HBM)


def pack_kernel(first, width, q_ref, g_ref, *rest):
    outs, sems = rest[:-1], rest[-1]
    parts, chunk = len(outs), outs[0].shape[-1]
    me = lax.axis_index("seq")
    copies = []
    for step, out in enumerate(outs):
        start = pl.multiple_of(partner(me, step, parts) * width + first, DH)
        for n, ref in enumerate((q_ref, g_ref)):
            source = ref.at[0, :, pl.ds(start, chunk)]
            copies.append(pltpu.make_async_copy(source, out.at[n], sems.at[2 * step + n]))
            copies[-1].start()
    for copy in copies:
        copy.wait()


def pack(first, chunk, queries, grads, width, parts):
    shape = (2, queries.shape[1], chunk)
    return pl.pallas_call(
        functools.partial(pack_kernel, first, width),
        grid=(1,),
        in_specs=[IN_HBM, IN_HBM],
        out_specs=[pl.BlockSpec(shape, lambda i: (0, 0, 0))] * parts,
        out_shape=[in_hbm(shape)] * parts,
        scratch_shapes=[pltpu.SemaphoreType.DMA((2 * parts,))],
        compiler_params=PARAMS,
        cost_estimate=cost(8 * parts * queries.shape[1] * chunk),
        name="pack_rows",
    )(queries, grads)


def unpack_kernel(firsts, width, *refs):
    ins, (ctx_ref, gq_ref, sems) = refs[:-3], refs[-3:]
    parts = len(ins) // len(firsts)
    me = lax.axis_index("seq")
    copies = []
    for n, src in enumerate(ins):
        first, step = firsts[n // parts], n % parts
        start = pl.multiple_of(partner(me, step, parts) * width + first, DH)
        for k, ref in enumerate((ctx_ref, gq_ref)):
            target = ref.at[0, :, pl.ds(start, src.shape[-1])]
            copies.append(pltpu.make_async_copy(src.at[k], target, sems.at[2 * n + k]))
            copies[-1].start()
    for copy in copies:
        copy.wait()


def unpack(pieces, firsts, width, shape):
    flat = [array for piece in pieces for array in piece]
    return pl.pallas_call(
        functools.partial(unpack_kernel, firsts, width),
        grid=(1,),
        in_specs=[pl.BlockSpec(array.shape, lambda i: (0, 0, 0)) for array in flat],
        out_specs=[IN_HBM, IN_HBM],
        out_shape=[in_hbm(shape)] * 2,
        scratch_shapes=[pltpu.SemaphoreType.DMA((2 * len(flat),))],
        compiler_params=PARAMS,
        cost_estimate=cost(8 * shape[1] * shape[2]),
        name="unpack_rows",
    )(*flat)


def pick_kernel(first, lists, pool_ref, out_ref, sems):
    copies = []
    for seq in range(out_ref.shape[0]):
        source = pool_ref.at[lists[0, seq, 0], :, :, first : first + out_ref.shape[-1]]
        copies.append(pltpu.make_async_copy(source, out_ref.at[seq], sems.at[seq]))
        copies[-1].start()
    for copy in copies:
        copy.wait()


def pick(first, chunk, send_lists, kv_pool):
    shape = (send_lists.shape[1], 2, NBLEN, chunk)
    return pl.pallas_call(
        functools.partial(pick_kernel, first),
        grid=(1,),
        in_specs=[SCALARS, IN_HBM],
        out_specs=pl.BlockSpec(shape, lambda i: (0, 0, 0, 0)),
        out_shape=in_hbm(shape),
        scratch_shapes=[pltpu.SemaphoreType.DMA((shape[0],))],
        compiler_params=PARAMS,
        cost_estimate=cost(8 * shape[0] * NBLEN * chunk),
        name="pick_entries",
    )(send_lists, kv_pool)


def dot(left, right, left_dim, right_dim):
    return lax.dot_general(
        left, right, (((left_dim,), (right_dim,)), ((), ())), preferred_element_type=F32
    )


def attend_kernel(seqs, parts, uses, *rest):
    half = seqs // 2
    rows_in, held, rest = rest[:parts], rest[parts], rest[parts + 1 :]
    rows_out, near_out, rest = rest[:parts], rest[parts], rest[parts + 1 :]
    far_out, (rows, made, sums) = rest[:half], rest[half:]
    scale = DH ** (-0.5)
    me, mine = lax.axis_index("enc"), lax.axis_index("seq")

    for step in range(parts):
        for n in range(2):
            piece = rows_in[step][n].astype(F32)
            rows[partner(mine, step, parts), n] = pltpu.roll(piece, 1, 0)
    rows[parts] = jnp.zeros(rows.shape[1:], F32)
    made[0, :, :BLOCK] = jnp.zeros((2, BLOCK, DH), F32)
    sums[...] = jnp.zeros_like(sums)
    first_row = lax.broadcasted_iota(jnp.int32, (BLOCK, DH), 0) == 0

    def one_block(block, q, g):
        first, second = uses[0, block, 0], uses[0, block, 1]
        keys = jnp.concatenate([held[first, 0], held[second, 0]], axis=0)
        values = jnp.concatenate([held[first, 1], held[second, 1]], axis=0)
        scores = dot(q, keys, 1, 1) * scale
        weights = jnp.exp(scores - jnp.max(scores, axis=1, keepdims=True))
        probs = weights / jnp.sum(weights, axis=1, keepdims=True)
        probs_low = probs.astype(BF16)
        out = dot(probs_low, values, 1, 0)
        grad_probs = dot(g, values, 1, 1)
        inner = jnp.sum(probs * grad_probs, axis=1, keepdims=True)
        grad_scores = (probs * (grad_probs - inner) * scale).astype(BF16)
        grad_q = dot(grad_scores, keys, 1, 0)
        grad_keys = dot(grad_scores, q, 0, 0)
        grad_values = dot(probs_low, g, 0, 0)
        sums[first, 0] += grad_keys[:NBLEN]
        sums[second, 0] += grad_keys[NBLEN:]
        sums[first, 1] += grad_values[:NBLEN]
        sums[second, 1] += grad_values[NBLEN:]
        return out, grad_q

    def one_part(part, carry):
        q, g = (rows[part, n, BLOCK:].astype(BF16) for n in range(2))
        for n, result in enumerate(one_block(2 * part, q, g)):
            made[part, n, BLOCK:] = result
        q, g = (
            jnp.where(first_row, rows[part, n, :BLOCK], rows[part + 1, n, :BLOCK]).astype(BF16)
            for n in range(2)
        )
        for n, result in enumerate(one_block(2 * part + 1, q, g)):
            made[part + 1, n, :BLOCK] = result
            made[part, n, :1] = result[:1]
        return carry

    if parts <= 4:
        for part in range(parts):
            one_part(part, 0)
    else:
        lax.fori_loop(0, parts, one_part, 0)

    for step in range(parts):
        for n in range(2):
            piece = made[partner(mine, step, parts), n]
            rows_out[step][n] = pltpu.roll(piece, 2 * BLOCK - 1, 0).astype(BF16)
    base = me - me % half
    for step in range(half):
        near_out[step] = sums[base + step].astype(BF16)
        far_out[step][...] = sums[across(me, step, seqs)].astype(BF16)


def attend(uses, rows_in, arrived):
    parts, part_rows = len(rows_in), rows_in[0].shape[1]
    seqs, _, _, chunk = arrived.shape
    half, heads = seqs // 2, chunk // DH
    rows_spec = pl.BlockSpec((2, part_rows, DH), lambda i: (0, 0, i))
    far_spec = pl.BlockSpec((2, NBLEN, DH), lambda i: (0, 0, i))
    pairs = heads * parts * part_rows * 2 * NBLEN
    outs = pl.pallas_call(
        functools.partial(attend_kernel, seqs, parts),
        grid=(heads,),
        in_specs=[SCALARS]
        + [rows_spec] * parts
        + [pl.BlockSpec((seqs, 2, NBLEN, DH), lambda i: (0, 0, 0, i))],
        out_specs=[rows_spec] * parts
        + [pl.BlockSpec((half, 2, NBLEN, DH), lambda i: (0, 0, 0, i))]
        + [far_spec] * half,
        scratch_shapes=[
            pltpu.VMEM((parts + 1, 2, part_rows, DH), F32),
            pltpu.VMEM((parts + 1, 2, part_rows, DH), F32),
            pltpu.VMEM((seqs, 2, NBLEN, DH), F32),
        ],
        out_shape=[in_hbm((2, part_rows, chunk))] * parts
        + [in_hbm((half, 2, NBLEN, chunk))]
        + [in_hbm((2, NBLEN, chunk))] * half,
        compiler_params=PARAMS,
        cost_estimate=cost(
            8 * (seqs + parts) * NBLEN * chunk, ATTEND_WEIGHT * 12 * DH * pairs, pairs
        ),
        name="attend_blocks",
    )(uses, *rows_in, arrived)
    return outs[:parts], outs[parts], outs[parts + 1 :]


def owner_kernel(seqs, lists, near_ref, *rest):
    half = seqs // 2
    far_refs, out_ref, acc = rest[:half], rest[-2], rest[-1]
    me = lax.axis_index("enc")
    base = me - me % half
    acc[...] = jnp.zeros_like(acc)
    for step in range(half):
        acc[lists[0, base + step, 0]] += near_ref[step].astype(F32)
        acc[lists[0, across(me, step, seqs), 0]] += far_refs[step][...].astype(F32)
    out_ref[...] = acc[...].astype(BF16)


def owner_sum(h, send_lists, near, far, shape, so_far):
    half = len(far)
    chunk = near.shape[-1]
    wide = min(chunk, 256)
    steps = chunk // wide
    extra = [] if so_far is None else [so_far]
    return pl.pallas_call(
        functools.partial(owner_kernel, 2 * half),
        grid=(steps,),
        in_specs=[SCALARS, pl.BlockSpec((half, 2, NBLEN, wide), lambda i: (0, 0, 0, i))]
        + [pl.BlockSpec((2, NBLEN, wide), lambda i: (0, 0, i))] * half
        + [ANYWHERE] * len(extra),
        out_specs=pl.BlockSpec(
            (shape[0], 2, NBLEN, wide), lambda i: (0, 0, 0, h * steps + i)
        ),
        scratch_shapes=[pltpu.VMEM((shape[0], 2, NBLEN, wide), F32)],
        out_shape=in_hbm(shape),
        input_output_aliases={half + 2: 0} if extra else {},
        compiler_params=PARAMS,
        cost_estimate=cost(4 * (2 * half + shape[0]) * NBLEN * chunk, 4 * half * NBLEN * chunk),
        name="owner_sum",
    )(send_lists, near, *far, *extra)


def swap_far(pieces, done):
    half = len(pieces)
    there = [[half + (i + step) % half for i in range(half)] for step in range(half)]
    got = []
    for step, piece in enumerate(pieces):
        if len(done) >= DEPTH:
            piece = after(piece, done[-DEPTH])
        pairs = list(enumerate(there[step])) + [(peer, i) for i, peer in enumerate(there[step])]
        got.append(lax.ppermute(piece, "enc", pairs))
        done.append(got[-1])
    return got


def local(seqs, parts, queries, kv_pool, send_lists, block_slots, grad_context):
    width = kv_pool.shape[-1]
    chunks = min(CHUNKS, width // DH)
    chunk = width // chunks
    firsts = [h * chunk for h in range(chunks)]

    arrived, rows = [], []
    for first in firsts:
        picked = pick(first, chunk, send_lists, kv_pool)
        send_lists, queries = after((send_lists, queries), picked)
        if rows:
            picked = after(picked, rows)
        arrived.append(swap_pool(picked))
        if not rows:
            for start in firsts:
                packed = pack(start, chunk, queries, grad_context, width, parts)
                rows.append(swap_rows(packed))
    done, returns, token_parts = [], [], []
    for h in range(chunks):
        rows_out, near, far = attend(block_slots, rows[h], arrived[h])
        far = swap_far(far, done)
        if h > 0:
            near = after(near, done[:DEPTH])
        returns.append((swap_near(near, seqs), far))
        token_parts.append(swap_rows(rows_out))
        block_slots = after(block_slots, token_parts[-1])
    context, grad_queries = unpack(token_parts, firsts, width, queries.shape)
    pool_grads = None
    for h in range(chunks):
        pool_grads = owner_sum(h, send_lists, *returns[h], kv_pool.shape, pool_grads)
    return (context, grad_queries, pool_grads)


def solution(mesh):
    in_specs = (
        P("enc", "seq", None),
        P("enc", None, None, "seq"),
        P("enc", None, None),
        P("enc", None, None),
        P("enc", "seq", None),
    )
    out_specs = (P("enc", "seq", None), P("enc", "seq", None), P("enc", None, None, "seq"))
    body = functools.partial(local, mesh.shape["enc"], mesh.shape["seq"])
    return jax.shard_map(body, mesh=mesh, in_specs=in_specs, out_specs=out_specs, check_vma=False)
```

```python
import functools

import jax
import jax.numpy as jnp
from jax import lax
from jax.experimental import pallas as pl
from jax.experimental.pallas import tpu as pltpu
from jax.sharding import PartitionSpec as P

DH = 128
BLOCK = 64
NBLEN = 128
CHUNKS = 2
DEPTH = 2
ATTEND_WEIGHT = 24
F32 = jnp.float32
BF16 = jnp.bfloat16
VMEM_BYTES = 40 * 1024 * 1024


def partner(index, step, count):
    if count & (count - 1) == 0:
        return index ^ step
    return (step - index) % count


def exchange(array, axis, step, count):
    pairs = [(i, partner(i, step, count)) for i in range(count)]
    return lax.ppermute(array, axis, pairs)


def across(index, step, count):
    half = count // 2
    there = half + (index + step) % half
    return jnp.where(index < half, there, (index - step) % half)


def swap_near(array, count):
    half = count // 2
    groups = [list(range(half)), list(range(half, count))]
    return lax.all_to_all(
        array, "enc", split_axis=0, concat_axis=0, axis_index_groups=groups, tiled=True
    )


def swap_rows(pieces):
    count = len(pieces)
    return [pieces[0]] + [exchange(pieces[step], "seq", step, count) for step in range(1, count)]


def swap_pool(array):
    return lax.all_to_all(array, "enc", split_axis=0, concat_axis=0, tiled=True)


def after(array, earlier):
    return lax.optimization_barrier((array, earlier))[0]


def in_hbm(shape):
    return pltpu.HBM(shape, BF16)


def cost(moved, flops=0, exps=0):
    return pl.CostEstimate(flops=flops, bytes_accessed=moved, transcendentals=exps)


PARAMS = pltpu.CompilerParams(vmem_limit_bytes=VMEM_BYTES)
SCALARS = pl.BlockSpec(memory_space=pltpu.SMEM)
ANYWHERE = pl.BlockSpec(memory_space=pl.ANY)
IN_HBM = pl.BlockSpec(memory_space=pltpu.HBM)


def pack_kernel(first, width, q_ref, g_ref, *rest):
    outs, sems = rest[:-1], rest[-1]
    parts, chunk = len(outs), outs[0].shape[-1]
    me = lax.axis_index("seq")
    copies = []
    for step, out in enumerate(outs):
        start = pl.multiple_of(partner(me, step, parts) * width + first, DH)
        for n, ref in enumerate((q_ref, g_ref)):
            source = ref.at[0, :, pl.ds(start, chunk)]
            copies.append(pltpu.make_async_copy(source, out.at[n], sems.at[2 * step + n]))
            copies[-1].start()
    for copy in copies:
        copy.wait()


def pack(first, chunk, queries, grads, width, parts):
    shape = (2, queries.shape[1], chunk)
    return pl.pallas_call(
        functools.partial(pack_kernel, first, width),
        grid=(1,),
        in_specs=[IN_HBM, IN_HBM],
        out_specs=[pl.BlockSpec(shape, lambda i: (0, 0, 0))] * parts,
        out_shape=[in_hbm(shape)] * parts,
        scratch_shapes=[pltpu.SemaphoreType.DMA((2 * parts,))],
        compiler_params=PARAMS,
        cost_estimate=cost(8 * parts * queries.shape[1] * chunk),
        name="pack_rows",
    )(queries, grads)


def unpack_kernel(firsts, width, *refs):
    ins, (ctx_ref, gq_ref, sems) = refs[:-3], refs[-3:]
    parts = len(ins) // len(firsts)
    me = lax.axis_index("seq")
    copies = []
    for n, src in enumerate(ins):
        first, step = firsts[n // parts], n % parts
        start = pl.multiple_of(partner(me, step, parts) * width + first, DH)
        for k, ref in enumerate((ctx_ref, gq_ref)):
            target = ref.at[0, :, pl.ds(start, src.shape[-1])]
            copies.append(pltpu.make_async_copy(src.at[k], target, sems.at[2 * n + k]))
            copies[-1].start()
    for copy in copies:
        copy.wait()


def unpack(pieces, firsts, width, shape):
    flat = [array for piece in pieces for array in piece]
    return pl.pallas_call(
        functools.partial(unpack_kernel, firsts, width),
        grid=(1,),
        in_specs=[pl.BlockSpec(array.shape, lambda i: (0, 0, 0)) for array in flat],
        out_specs=[IN_HBM, IN_HBM],
        out_shape=[in_hbm(shape)] * 2,
        scratch_shapes=[pltpu.SemaphoreType.DMA((2 * len(flat),))],
        compiler_params=PARAMS,
        cost_estimate=cost(8 * shape[1] * shape[2]),
        name="unpack_rows",
    )(*flat)


def pick_kernel(first, lists, pool_ref, out_ref, sems):
    copies = []
    for seq in range(out_ref.shape[0]):
        source = pool_ref.at[lists[0, seq, 0], :, :, first : first + out_ref.shape[-1]]
        copies.append(pltpu.make_async_copy(source, out_ref.at[seq], sems.at[seq]))
        copies[-1].start()
    for copy in copies:
        copy.wait()


def pick(first, chunk, send_lists, kv_pool):
    shape = (send_lists.shape[1], 2, NBLEN, chunk)
    return pl.pallas_call(
        functools.partial(pick_kernel, first),
        grid=(1,),
        in_specs=[SCALARS, IN_HBM],
        out_specs=pl.BlockSpec(shape, lambda i: (0, 0, 0, 0)),
        out_shape=in_hbm(shape),
        scratch_shapes=[pltpu.SemaphoreType.DMA((shape[0],))],
        compiler_params=PARAMS,
        cost_estimate=cost(8 * shape[0] * NBLEN * chunk),
        name="pick_entries",
    )(send_lists, kv_pool)


def dot(left, right, left_dim, right_dim):
    return lax.dot_general(
        left, right, (((left_dim,), (right_dim,)), ((), ())), preferred_element_type=F32
    )


def attend_kernel(seqs, parts, uses, *rest):
    half = seqs // 2
    rows_in, held, rest = rest[:parts], rest[parts], rest[parts + 1 :]
    rows_out, near_out, rest = rest[:parts], rest[parts], rest[parts + 1 :]
    far_out, (rows, made, sums) = rest[:half], rest[half:]
    scale = DH ** (-0.5)
    me, mine = lax.axis_index("enc"), lax.axis_index("seq")

    for step in range(parts):
        for n in range(2):
            piece = rows_in[step][n].astype(F32)
            rows[partner(mine, step, parts), n] = pltpu.roll(piece, 1, 0)
    rows[parts] = jnp.zeros(rows.shape[1:], F32)
    made[0, :, :BLOCK] = jnp.zeros((2, BLOCK, DH), F32)
    sums[...] = jnp.zeros_like(sums)
    first_row = lax.broadcasted_iota(jnp.int32, (BLOCK, DH), 0) == 0

    def one_block(block, q, g):
        first, second = uses[0, block, 0], uses[0, block, 1]
        keys = jnp.concatenate([held[first, 0], held[second, 0]], axis=0)
        values = jnp.concatenate([held[first, 1], held[second, 1]], axis=0)
        scores = dot(q, keys, 1, 1) * scale
        weights = jnp.exp(scores - jnp.max(scores, axis=1, keepdims=True))
        probs = weights / jnp.sum(weights, axis=1, keepdims=True)
        probs_low = probs.astype(BF16)
        out = dot(probs_low, values, 1, 0)
        grad_probs = dot(g, values, 1, 1)
        inner = jnp.sum(probs * grad_probs, axis=1, keepdims=True)
        grad_scores = (probs * (grad_probs - inner) * scale).astype(BF16)
        grad_q = dot(grad_scores, keys, 1, 0)
        grad_keys = dot(grad_scores, q, 0, 0)
        grad_values = dot(probs_low, g, 0, 0)
        sums[first, 0] += grad_keys[:NBLEN]
        sums[second, 0] += grad_keys[NBLEN:]
        sums[first, 1] += grad_values[:NBLEN]
        sums[second, 1] += grad_values[NBLEN:]
        return out, grad_q

    def one_part(part, carry):
        q, g = (rows[part, n, BLOCK:].astype(BF16) for n in range(2))
        for n, result in enumerate(one_block(2 * part, q, g)):
            made[part, n, BLOCK:] = result
        q, g = (
            jnp.where(first_row, rows[part, n, :BLOCK], rows[part + 1, n, :BLOCK]).astype(BF16)
            for n in range(2)
        )
        for n, result in enumerate(one_block(2 * part + 1, q, g)):
            made[part + 1, n, :BLOCK] = result
            made[part, n, :1] = result[:1]
        return carry

    if parts <= 4:
        for part in range(parts):
            one_part(part, 0)
    else:
        lax.fori_loop(0, parts, one_part, 0)

    for step in range(parts):
        for n in range(2):
            piece = made[partner(mine, step, parts), n]
            rows_out[step][n] = pltpu.roll(piece, 2 * BLOCK - 1, 0).astype(BF16)
    base = me - me % half
    for step in range(half):
        near_out[step] = sums[base + step].astype(BF16)
        far_out[step][...] = sums[across(me, step, seqs)].astype(BF16)


def attend(uses, rows_in, arrived):
    parts, part_rows = len(rows_in), rows_in[0].shape[1]
    seqs, _, _, chunk = arrived.shape
    half, heads = seqs // 2, chunk // DH
    rows_spec = pl.BlockSpec((2, part_rows, DH), lambda i: (0, 0, i))
    far_spec = pl.BlockSpec((2, NBLEN, DH), lambda i: (0, 0, i))
    pairs = heads * parts * part_rows * 2 * NBLEN
    outs = pl.pallas_call(
        functools.partial(attend_kernel, seqs, parts),
        grid=(heads,),
        in_specs=[SCALARS]
        + [rows_spec] * parts
        + [pl.BlockSpec((seqs, 2, NBLEN, DH), lambda i: (0, 0, 0, i))],
        out_specs=[rows_spec] * parts
        + [pl.BlockSpec((half, 2, NBLEN, DH), lambda i: (0, 0, 0, i))]
        + [far_spec] * half,
        scratch_shapes=[
            pltpu.VMEM((parts + 1, 2, part_rows, DH), F32),
            pltpu.VMEM((parts + 1, 2, part_rows, DH), F32),
            pltpu.VMEM((seqs, 2, NBLEN, DH), F32),
        ],
        out_shape=[in_hbm((2, part_rows, chunk))] * parts
        + [in_hbm((half, 2, NBLEN, chunk))]
        + [in_hbm((2, NBLEN, chunk))] * half,
        compiler_params=PARAMS,
        cost_estimate=cost(
            8 * (seqs + parts) * NBLEN * chunk, ATTEND_WEIGHT * 12 * DH * pairs, pairs
        ),
        name="attend_blocks",
    )(uses, *rows_in, arrived)
    return outs[:parts], outs[parts], outs[parts + 1 :]


def owner_kernel(seqs, lists, near_ref, *rest):
    half = seqs // 2
    far_refs, out_ref, acc = rest[:half], rest[-2], rest[-1]
    me = lax.axis_index("enc")
    base = me - me % half
    acc[...] = jnp.zeros_like(acc)
    for step in range(half):
        acc[lists[0, base + step, 0]] += near_ref[step].astype(F32)
        acc[lists[0, across(me, step, seqs), 0]] += far_refs[step][...].astype(F32)
    out_ref[...] = acc[...].astype(BF16)


def owner_sum(h, send_lists, near, far, shape, so_far):
    half = len(far)
    chunk = near.shape[-1]
    wide = min(chunk, 256)
    steps = chunk // wide
    extra = [] if so_far is None else [so_far]
    return pl.pallas_call(
        functools.partial(owner_kernel, 2 * half),
        grid=(steps,),
        in_specs=[SCALARS, pl.BlockSpec((half, 2, NBLEN, wide), lambda i: (0, 0, 0, i))]
        + [pl.BlockSpec((2, NBLEN, wide), lambda i: (0, 0, i))] * half
        + [ANYWHERE] * len(extra),
        out_specs=pl.BlockSpec(
            (shape[0], 2, NBLEN, wide), lambda i: (0, 0, 0, h * steps + i)
        ),
        scratch_shapes=[pltpu.VMEM((shape[0], 2, NBLEN, wide), F32)],
        out_shape=in_hbm(shape),
        input_output_aliases={half + 2: 0} if extra else {},
        compiler_params=PARAMS,
        cost_estimate=cost(4 * (2 * half + shape[0]) * NBLEN * chunk, 4 * half * NBLEN * chunk),
        name="owner_sum",
    )(send_lists, near, *far, *extra)


def swap_far(pieces, done):
    half = len(pieces)
    there = [[half + (i + step) % half for i in range(half)] for step in range(half)]
    got = []
    for step, piece in enumerate(pieces):
        if len(done) >= DEPTH:
            piece = after(piece, done[-DEPTH])
        pairs = list(enumerate(there[step])) + [(peer, i) for i, peer in enumerate(there[step])]
        got.append(lax.ppermute(piece, "enc", pairs))
        done.append(got[-1])
    return got


def local(seqs, parts, queries, kv_pool, send_lists, block_slots, grad_context):
    width = kv_pool.shape[-1]
    chunks = min(CHUNKS, width // DH)
    chunk = width // chunks
    firsts = [h * chunk for h in range(chunks)]

    arrived, rows = [], []
    for first in firsts:
        picked = pick(first, chunk, send_lists, kv_pool)
        send_lists, queries = after((send_lists, queries), picked)
        if rows:
            picked = after(picked, rows)
        arrived.append(swap_pool(picked))
        if not rows:
            for start in firsts:
                packed = pack(start, chunk, queries, grad_context, width, parts)
                rows.append(swap_rows(packed))
    done, returns, token_parts = [], [], []
    for h in range(chunks):
        rows_out, near, far = attend(block_slots, rows[h], arrived[h])
        far = swap_far(far, done)
        returns.append((swap_near(near, seqs), far))
        token_parts.append(swap_rows(rows_out))
        block_slots = after(block_slots, (token_parts[-1], far[:DEPTH]))
    context, grad_queries = unpack(token_parts, firsts, width, queries.shape)
    pool_grads = None
    for h in range(chunks):
        pool_grads = owner_sum(h, send_lists, *returns[h], kv_pool.shape, pool_grads)
    return (context, grad_queries, pool_grads)


def solution(mesh):
    in_specs = (
        P("enc", "seq", None),
        P("enc", None, None, "seq"),
        P("enc", None, None),
        P("enc", None, None),
        P("enc", "seq", None),
    )
    out_specs = (P("enc", "seq", None), P("enc", "seq", None), P("enc", None, None, "seq"))
    body = functools.partial(local, mesh.shape["enc"], mesh.shape["seq"])
    return jax.shard_map(body, mesh=mesh, in_specs=in_specs, out_specs=out_specs, check_vma=False)
```

```python
import functools

import jax
import jax.numpy as jnp
from jax import lax
from jax.experimental import pallas as pl
from jax.experimental.pallas import tpu as pltpu
from jax.sharding import PartitionSpec as P

DH = 128
BLOCK = 64
NBLEN = 128
CHUNKS = 2
DEPTH = 2
ATTEND_WEIGHT = 24
F32 = jnp.float32
BF16 = jnp.bfloat16
VMEM_BYTES = 40 * 1024 * 1024


def partner(index, step, count):
    if count & (count - 1) == 0:
        return index ^ step
    return (step - index) % count


def exchange(array, axis, step, count):
    pairs = [(i, partner(i, step, count)) for i in range(count)]
    return lax.ppermute(array, axis, pairs)


def across(index, step, count):
    half = count // 2
    there = half + (index + step) % half
    return jnp.where(index < half, there, (index - step) % half)


def swap_near(array, count):
    half = count // 2
    groups = [list(range(half)), list(range(half, count))]
    return lax.all_to_all(
        array, "enc", split_axis=0, concat_axis=0, axis_index_groups=groups, tiled=True
    )


def swap_rows(pieces):
    count = len(pieces)
    return [pieces[0]] + [exchange(pieces[step], "seq", step, count) for step in range(1, count)]


def swap_pool(array):
    return lax.all_to_all(array, "enc", split_axis=0, concat_axis=0, tiled=True)


def after(array, earlier):
    return lax.optimization_barrier((array, earlier))[0]


def in_hbm(shape):
    return pltpu.HBM(shape, BF16)


def cost(moved, flops=0, exps=0):
    return pl.CostEstimate(flops=flops, bytes_accessed=moved, transcendentals=exps)


PARAMS = pltpu.CompilerParams(vmem_limit_bytes=VMEM_BYTES)
SCALARS = pl.BlockSpec(memory_space=pltpu.SMEM)
ANYWHERE = pl.BlockSpec(memory_space=pl.ANY)
IN_HBM = pl.BlockSpec(memory_space=pltpu.HBM)


def pack_kernel(first, width, q_ref, g_ref, *rest):
    outs, sems = rest[:-1], rest[-1]
    parts, chunk = len(outs), outs[0].shape[-1]
    me = lax.axis_index("seq")
    copies = []
    for step, out in enumerate(outs):
        start = pl.multiple_of(partner(me, step, parts) * width + first, DH)
        for n, ref in enumerate((q_ref, g_ref)):
            source = ref.at[0, :, pl.ds(start, chunk)]
            copies.append(pltpu.make_async_copy(source, out.at[n], sems.at[2 * step + n]))
            copies[-1].start()
    for copy in copies:
        copy.wait()


def pack(first, chunk, queries, grads, width, parts):
    shape = (2, queries.shape[1], chunk)
    return pl.pallas_call(
        functools.partial(pack_kernel, first, width),
        grid=(1,),
        in_specs=[IN_HBM, IN_HBM],
        out_specs=[pl.BlockSpec(shape, lambda i: (0, 0, 0))] * parts,
        out_shape=[in_hbm(shape)] * parts,
        scratch_shapes=[pltpu.SemaphoreType.DMA((2 * parts,))],
        compiler_params=PARAMS,
        cost_estimate=cost(8 * parts * queries.shape[1] * chunk),
        name="pack_rows",
    )(queries, grads)


def unpack_kernel(firsts, width, *refs):
    ins, (ctx_ref, gq_ref, sems) = refs[:-3], refs[-3:]
    parts = len(ins) // len(firsts)
    me = lax.axis_index("seq")
    copies = []
    for n, src in enumerate(ins):
        first, step = firsts[n // parts], n % parts
        start = pl.multiple_of(partner(me, step, parts) * width + first, DH)
        for k, ref in enumerate((ctx_ref, gq_ref)):
            target = ref.at[0, :, pl.ds(start, src.shape[-1])]
            copies.append(pltpu.make_async_copy(src.at[k], target, sems.at[2 * n + k]))
            copies[-1].start()
    for copy in copies:
        copy.wait()


def unpack(pieces, firsts, width, shape):
    flat = [array for piece in pieces for array in piece]
    return pl.pallas_call(
        functools.partial(unpack_kernel, firsts, width),
        grid=(1,),
        in_specs=[pl.BlockSpec(array.shape, lambda i: (0, 0, 0)) for array in flat],
        out_specs=[IN_HBM, IN_HBM],
        out_shape=[in_hbm(shape)] * 2,
        scratch_shapes=[pltpu.SemaphoreType.DMA((2 * len(flat),))],
        compiler_params=PARAMS,
        cost_estimate=cost(8 * shape[1] * shape[2]),
        name="unpack_rows",
    )(*flat)


def pick_kernel(first, lists, pool_ref, out_ref, sems):
    copies = []
    for seq in range(out_ref.shape[0]):
        source = pool_ref.at[lists[0, seq, 0], :, :, first : first + out_ref.shape[-1]]
        copies.append(pltpu.make_async_copy(source, out_ref.at[seq], sems.at[seq]))
        copies[-1].start()
    for copy in copies:
        copy.wait()


def pick(first, chunk, send_lists, kv_pool):
    shape = (send_lists.shape[1], 2, NBLEN, chunk)
    return pl.pallas_call(
        functools.partial(pick_kernel, first),
        grid=(1,),
        in_specs=[SCALARS, IN_HBM],
        out_specs=pl.BlockSpec(shape, lambda i: (0, 0, 0, 0)),
        out_shape=in_hbm(shape),
        scratch_shapes=[pltpu.SemaphoreType.DMA((shape[0],))],
        compiler_params=PARAMS,
        cost_estimate=cost(8 * shape[0] * NBLEN * chunk),
        name="pick_entries",
    )(send_lists, kv_pool)


def dot(left, right, left_dim, right_dim):
    return lax.dot_general(
        left, right, (((left_dim,), (right_dim,)), ((), ())), preferred_element_type=F32
    )


def attend_kernel(seqs, parts, uses, *rest):
    half = seqs // 2
    rows_in, held, rest = rest[:parts], rest[parts], rest[parts + 1 :]
    rows_out, near_out, rest = rest[:parts], rest[parts], rest[parts + 1 :]
    far_out, (rows, made, sums) = rest[:half], rest[half:]
    scale = DH ** (-0.5)
    me, mine = lax.axis_index("enc"), lax.axis_index("seq")

    for step in range(parts):
        for n in range(2):
            piece = rows_in[step][n].astype(F32)
            rows[partner(mine, step, parts), n] = pltpu.roll(piece, 1, 0)
    rows[parts] = jnp.zeros(rows.shape[1:], F32)
    made[0, :, :BLOCK] = jnp.zeros((2, BLOCK, DH), F32)
    sums[...] = jnp.zeros_like(sums)
    first_row = lax.broadcasted_iota(jnp.int32, (BLOCK, DH), 0) == 0

    def one_block(block, q, g):
        first, second = uses[0, block, 0], uses[0, block, 1]
        keys = jnp.concatenate([held[first, 0], held[second, 0]], axis=0)
        values = jnp.concatenate([held[first, 1], held[second, 1]], axis=0)
        scores = dot(q, keys, 1, 1) * scale
        weights = jnp.exp(scores - jnp.max(scores, axis=1, keepdims=True))
        probs = weights / jnp.sum(weights, axis=1, keepdims=True)
        probs_low = probs.astype(BF16)
        out = dot(probs_low, values, 1, 0)
        grad_probs = dot(g, values, 1, 1)
        inner = jnp.sum(probs * grad_probs, axis=1, keepdims=True)
        grad_scores = (probs * (grad_probs - inner) * scale).astype(BF16)
        grad_q = dot(grad_scores, keys, 1, 0)
        grad_keys = dot(grad_scores, q, 0, 0)
        grad_values = dot(probs_low, g, 0, 0)
        sums[first, 0] += grad_keys[:NBLEN]
        sums[second, 0] += grad_keys[NBLEN:]
        sums[first, 1] += grad_values[:NBLEN]
        sums[second, 1] += grad_values[NBLEN:]
        return out, grad_q

    def one_part(part, carry):
        q, g = (rows[part, n, BLOCK:].astype(BF16) for n in range(2))
        for n, result in enumerate(one_block(2 * part, q, g)):
            made[part, n, BLOCK:] = result
        q, g = (
            jnp.where(first_row, rows[part, n, :BLOCK], rows[part + 1, n, :BLOCK]).astype(BF16)
            for n in range(2)
        )
        for n, result in enumerate(one_block(2 * part + 1, q, g)):
            made[part + 1, n, :BLOCK] = result
            made[part, n, :1] = result[:1]
        return carry

    if parts <= 4:
        for part in range(parts):
            one_part(part, 0)
    else:
        lax.fori_loop(0, parts, one_part, 0)

    for step in range(parts):
        for n in range(2):
            piece = made[partner(mine, step, parts), n]
            rows_out[step][n] = pltpu.roll(piece, 2 * BLOCK - 1, 0).astype(BF16)
    base = me - me % half
    for step in range(half):
        near_out[step] = sums[base + step].astype(BF16)
        far_out[step][...] = sums[across(me, step, seqs)].astype(BF16)


def attend(uses, rows_in, arrived):
    parts, part_rows = len(rows_in), rows_in[0].shape[1]
    seqs, _, _, chunk = arrived.shape
    half, heads = seqs // 2, chunk // DH
    rows_spec = pl.BlockSpec((2, part_rows, DH), lambda i: (0, 0, i))
    far_spec = pl.BlockSpec((2, NBLEN, DH), lambda i: (0, 0, i))
    pairs = heads * parts * part_rows * 2 * NBLEN
    outs = pl.pallas_call(
        functools.partial(attend_kernel, seqs, parts),
        grid=(heads,),
        in_specs=[SCALARS]
        + [rows_spec] * parts
        + [pl.BlockSpec((seqs, 2, NBLEN, DH), lambda i: (0, 0, 0, i))],
        out_specs=[rows_spec] * parts
        + [pl.BlockSpec((half, 2, NBLEN, DH), lambda i: (0, 0, 0, i))]
        + [far_spec] * half,
        scratch_shapes=[
            pltpu.VMEM((parts + 1, 2, part_rows, DH), F32),
            pltpu.VMEM((parts + 1, 2, part_rows, DH), F32),
            pltpu.VMEM((seqs, 2, NBLEN, DH), F32),
        ],
        out_shape=[in_hbm((2, part_rows, chunk))] * parts
        + [in_hbm((half, 2, NBLEN, chunk))]
        + [in_hbm((2, NBLEN, chunk))] * half,
        compiler_params=PARAMS,
        cost_estimate=cost(
            8 * (seqs + parts) * NBLEN * chunk, ATTEND_WEIGHT * 12 * DH * pairs, pairs
        ),
        name="attend_blocks",
    )(uses, *rows_in, arrived)
    return outs[:parts], outs[parts], outs[parts + 1 :]


def owner_kernel(seqs, lists, near_ref, *rest):
    half = seqs // 2
    far_refs, out_ref, acc = rest[:half], rest[-2], rest[-1]
    me = lax.axis_index("enc")
    base = me - me % half
    acc[...] = jnp.zeros_like(acc)
    for step in range(half):
        acc[lists[0, base + step, 0]] += near_ref[step].astype(F32)
        acc[lists[0, across(me, step, seqs), 0]] += far_refs[step][...].astype(F32)
    out_ref[...] = acc[...].astype(BF16)


def owner_sum(h, send_lists, near, far, shape, so_far):
    half = len(far)
    chunk = near.shape[-1]
    wide = min(chunk, 256)
    steps = chunk // wide
    extra = [] if so_far is None else [so_far]
    return pl.pallas_call(
        functools.partial(owner_kernel, 2 * half),
        grid=(steps,),
        in_specs=[SCALARS, pl.BlockSpec((half, 2, NBLEN, wide), lambda i: (0, 0, 0, i))]
        + [pl.BlockSpec((2, NBLEN, wide), lambda i: (0, 0, i))] * half
        + [ANYWHERE] * len(extra),
        out_specs=pl.BlockSpec(
            (shape[0], 2, NBLEN, wide), lambda i: (0, 0, 0, h * steps + i)
        ),
        scratch_shapes=[pltpu.VMEM((shape[0], 2, NBLEN, wide), F32)],
        out_shape=in_hbm(shape),
        input_output_aliases={half + 2: 0} if extra else {},
        compiler_params=PARAMS,
        cost_estimate=cost(4 * (2 * half + shape[0]) * NBLEN * chunk, 4 * half * NBLEN * chunk),
        name="owner_sum",
    )(send_lists, near, *far, *extra)


def swap_far(pieces, done):
    half = len(pieces)
    there = [[half + (i + step) % half for i in range(half)] for step in range(half)]
    got = []
    for step, piece in enumerate(pieces):
        if len(done) >= DEPTH:
            piece = after(piece, done[-DEPTH])
        pairs = list(enumerate(there[step])) + [(peer, i) for i, peer in enumerate(there[step])]
        got.append(lax.ppermute(piece, "enc", pairs))
        done.append(got[-1])
    return got


def local(seqs, parts, queries, kv_pool, send_lists, block_slots, grad_context):
    width = kv_pool.shape[-1]
    chunks = min(CHUNKS, width // DH)
    chunk = width // chunks
    firsts = [h * chunk for h in range(chunks)]

    arrived, rows = [], []
    for first in firsts:
        picked = pick(first, chunk, send_lists, kv_pool)
        send_lists, queries = after((send_lists, queries), picked)
        if rows:
            picked = after(picked, rows)
        arrived.append(swap_pool(picked))
        if not rows:
            for start in firsts:
                packed = pack(start, chunk, queries, grad_context, width, parts)
                rows.append(swap_rows(packed))
    done, returns, token_parts = [], [], []
    for h in range(chunks):
        rows_out, near, far = attend(block_slots, rows[h], arrived[h])
        far = swap_far(far, done)
        if h > 0:
            near = after(near, done[: seqs // 2])
        returns.append((swap_near(near, seqs), far))
        token_parts.append(swap_rows(rows_out))
        block_slots = after(block_slots, (token_parts[-1], far[:DEPTH]))
    context, grad_queries = unpack(token_parts, firsts, width, queries.shape)
    pool_grads = None
    for h in range(chunks):
        pool_grads = owner_sum(h, send_lists, *returns[h], kv_pool.shape, pool_grads)
    return (context, grad_queries, pool_grads)


def solution(mesh):
    in_specs = (
        P("enc", "seq", None),
        P("enc", None, None, "seq"),
        P("enc", None, None),
        P("enc", None, None),
        P("enc", "seq", None),
    )
    out_specs = (P("enc", "seq", None), P("enc", "seq", None), P("enc", None, None, "seq"))
    body = functools.partial(local, mesh.shape["enc"], mesh.shape["seq"])
    return jax.shard_map(body, mesh=mesh, in_specs=in_specs, out_specs=out_specs, check_vma=False)
```

```python
import functools
import math

import jax
import jax.numpy as jnp
from jax import lax
from jax.experimental import pallas as pl
from jax.experimental.pallas import tpu as pltpu
from jax.sharding import PartitionSpec as P

DH = 128
BLOCK = 64
NBLEN = 128
DEPTH = 2
ATTEND_WEIGHT = 24
F32 = jnp.float32
BF16 = jnp.bfloat16
VMEM_BYTES = 40 * 1024 * 1024


def partner(index, step, count):
    if count & (count - 1) == 0:
        return index ^ step
    return (step - index) % count


def exchange(array, axis, step, count):
    pairs = [(i, partner(i, step, count)) for i in range(count)]
    return lax.ppermute(array, axis, pairs)


def across(index, step, count):
    half = count // 2
    there = half + (index + step) % half
    return jnp.where(index < half, there, (index - step) % half)


def swap_near(array, count):
    half = count // 2
    groups = [list(range(half)), list(range(half, count))]
    return lax.all_to_all(
        array, "enc", split_axis=0, concat_axis=0, axis_index_groups=groups, tiled=True
    )


def swap_rows(pieces):
    count = len(pieces)
    return [pieces[0]] + [exchange(pieces[step], "seq", step, count) for step in range(1, count)]


def swap_pool(array):
    return lax.all_to_all(array, "enc", split_axis=0, concat_axis=0, tiled=True)


def after(array, earlier):
    return lax.optimization_barrier((array, earlier))[0]


def in_hbm(shape):
    return pltpu.HBM(shape, BF16)


def cost(moved, flops=0, exps=0):
    return pl.CostEstimate(flops=flops, bytes_accessed=moved, transcendentals=exps)


PARAMS = pltpu.CompilerParams(vmem_limit_bytes=VMEM_BYTES)
SCALARS = pl.BlockSpec(memory_space=pltpu.SMEM)
ANYWHERE = pl.BlockSpec(memory_space=pl.ANY)
IN_HBM = pl.BlockSpec(memory_space=pltpu.HBM)


def pack_kernel(first, width, q_ref, g_ref, *rest):
    outs, sems = rest[:-1], rest[-1]
    parts, chunk = len(outs), outs[0].shape[-1]
    me = lax.axis_index("seq")
    copies = []
    for step, out in enumerate(outs):
        start = pl.multiple_of(partner(me, step, parts) * width + first, DH)
        for n, ref in enumerate((q_ref, g_ref)):
            source = ref.at[0, :, pl.ds(start, chunk)]
            copies.append(pltpu.make_async_copy(source, out.at[n], sems.at[2 * step + n]))
            copies[-1].start()
    for copy in copies:
        copy.wait()


def pack(first, chunk, queries, grads, width, parts):
    shape = (2, queries.shape[1], chunk)
    return pl.pallas_call(
        functools.partial(pack_kernel, first, width),
        grid=(1,),
        in_specs=[IN_HBM, IN_HBM],
        out_specs=[pl.BlockSpec(shape, lambda i: (0, 0, 0))] * parts,
        out_shape=[in_hbm(shape)] * parts,
        scratch_shapes=[pltpu.SemaphoreType.DMA((2 * parts,))],
        compiler_params=PARAMS,
        cost_estimate=cost(8 * parts * queries.shape[1] * chunk),
        name="pack_rows",
    )(queries, grads)


def unpack_kernel(firsts, width, *refs):
    ins, (ctx_ref, gq_ref, sems) = refs[:-3], refs[-3:]
    parts = len(ins) // len(firsts)
    me = lax.axis_index("seq")
    copies = []
    for n, src in enumerate(ins):
        first, step = firsts[n // parts], n % parts
        start = pl.multiple_of(partner(me, step, parts) * width + first, DH)
        for k, ref in enumerate((ctx_ref, gq_ref)):
            target = ref.at[0, :, pl.ds(start, src.shape[-1])]
            copies.append(pltpu.make_async_copy(src.at[k], target, sems.at[2 * n + k]))
            copies[-1].start()
    for copy in copies:
        copy.wait()


def unpack(pieces, firsts, width, shape):
    flat = [array for piece in pieces for array in piece]
    return pl.pallas_call(
        functools.partial(unpack_kernel, firsts, width),
        grid=(1,),
        in_specs=[pl.BlockSpec(array.shape, lambda i: (0, 0, 0)) for array in flat],
        out_specs=[IN_HBM, IN_HBM],
        out_shape=[in_hbm(shape)] * 2,
        scratch_shapes=[pltpu.SemaphoreType.DMA((2 * len(flat),))],
        compiler_params=PARAMS,
        cost_estimate=cost(8 * shape[1] * shape[2]),
        name="unpack_rows",
    )(*flat)


def pick_kernel(first, lists, pool_ref, out_ref, sems):
    copies = []
    for seq in range(out_ref.shape[0]):
        source = pool_ref.at[lists[0, seq, 0], :, :, first : first + out_ref.shape[-1]]
        copies.append(pltpu.make_async_copy(source, out_ref.at[seq], sems.at[seq]))
        copies[-1].start()
    for copy in copies:
        copy.wait()


def pick(first, chunk, send_lists, kv_pool):
    shape = (send_lists.shape[1], 2, NBLEN, chunk)
    return pl.pallas_call(
        functools.partial(pick_kernel, first),
        grid=(1,),
        in_specs=[SCALARS, IN_HBM],
        out_specs=pl.BlockSpec(shape, lambda i: (0, 0, 0, 0)),
        out_shape=in_hbm(shape),
        scratch_shapes=[pltpu.SemaphoreType.DMA((shape[0],))],
        compiler_params=PARAMS,
        cost_estimate=cost(8 * shape[0] * NBLEN * chunk),
        name="pick_entries",
    )(send_lists, kv_pool)


def dot(left, right, left_dim, right_dim):
    return lax.dot_general(
        left, right, (((left_dim,), (right_dim,)), ((), ())), preferred_element_type=F32
    )


def attend_kernel(seqs, parts, uses, *rest):
    half = seqs // 2
    rows_in, held, rest = rest[:parts], rest[parts], rest[parts + 1 :]
    rows_out, near_out, rest = rest[:parts], rest[parts], rest[parts + 1 :]
    far_out, (rows, made, sums) = rest[:half], rest[half:]
    scale = DH ** (-0.5)
    me, mine = lax.axis_index("enc"), lax.axis_index("seq")

    for step in range(parts):
        for n in range(2):
            piece = rows_in[step][n].astype(F32)
            rows[partner(mine, step, parts), n] = pltpu.roll(piece, 1, 0)
    rows[parts] = jnp.zeros(rows.shape[1:], F32)
    made[0, :, :BLOCK] = jnp.zeros((2, BLOCK, DH), F32)
    sums[...] = jnp.zeros_like(sums)
    first_row = lax.broadcasted_iota(jnp.int32, (BLOCK, DH), 0) == 0

    def one_block(block, q, g):
        first, second = uses[0, block, 0], uses[0, block, 1]
        keys = jnp.concatenate([held[first, 0], held[second, 0]], axis=0)
        values = jnp.concatenate([held[first, 1], held[second, 1]], axis=0)
        scores = dot(q, keys, 1, 1) * scale
        weights = jnp.exp(scores - jnp.max(scores, axis=1, keepdims=True))
        probs = weights / jnp.sum(weights, axis=1, keepdims=True)
        probs_low = probs.astype(BF16)
        out = dot(probs_low, values, 1, 0)
        grad_probs = dot(g, values, 1, 1)
        inner = jnp.sum(probs * grad_probs, axis=1, keepdims=True)
        grad_scores = (probs * (grad_probs - inner) * scale).astype(BF16)
        grad_q = dot(grad_scores, keys, 1, 0)
        grad_keys = dot(grad_scores, q, 0, 0)
        grad_values = dot(probs_low, g, 0, 0)
        sums[first, 0] += grad_keys[:NBLEN]
        sums[second, 0] += grad_keys[NBLEN:]
        sums[first, 1] += grad_values[:NBLEN]
        sums[second, 1] += grad_values[NBLEN:]
        return out, grad_q

    def one_part(part, carry):
        q, g = (rows[part, n, BLOCK:].astype(BF16) for n in range(2))
        for n, result in enumerate(one_block(2 * part, q, g)):
            made[part, n, BLOCK:] = result
        q, g = (
            jnp.where(first_row, rows[part, n, :BLOCK], rows[part + 1, n, :BLOCK]).astype(BF16)
            for n in range(2)
        )
        for n, result in enumerate(one_block(2 * part + 1, q, g)):
            made[part + 1, n, :BLOCK] = result
            made[part, n, :1] = result[:1]
        return carry

    if parts <= 4:
        for part in range(parts):
            one_part(part, 0)
    else:
        lax.fori_loop(0, parts, one_part, 0)

    for step in range(parts):
        for n in range(2):
            piece = made[partner(mine, step, parts), n]
            rows_out[step][n] = pltpu.roll(piece, 2 * BLOCK - 1, 0).astype(BF16)
    base = me - me % half
    for step in range(half):
        near_out[step] = sums[base + step].astype(BF16)
        far_out[step][...] = sums[across(me, step, seqs)].astype(BF16)


def attend(uses, rows_in, arrived):
    parts, part_rows = len(rows_in), rows_in[0].shape[1]
    seqs, _, _, chunk = arrived.shape
    half, heads = seqs // 2, chunk // DH
    rows_spec = pl.BlockSpec((2, part_rows, DH), lambda i: (0, 0, i))
    far_spec = pl.BlockSpec((2, NBLEN, DH), lambda i: (0, 0, i))
    pairs = heads * parts * part_rows * 2 * NBLEN
    outs = pl.pallas_call(
        functools.partial(attend_kernel, seqs, parts),
        grid=(heads,),
        in_specs=[SCALARS]
        + [rows_spec] * parts
        + [pl.BlockSpec((seqs, 2, NBLEN, DH), lambda i: (0, 0, 0, i))],
        out_specs=[rows_spec] * parts
        + [pl.BlockSpec((half, 2, NBLEN, DH), lambda i: (0, 0, 0, i))]
        + [far_spec] * half,
        scratch_shapes=[
            pltpu.VMEM((parts + 1, 2, part_rows, DH), F32),
            pltpu.VMEM((parts + 1, 2, part_rows, DH), F32),
            pltpu.VMEM((seqs, 2, NBLEN, DH), F32),
        ],
        out_shape=[in_hbm((2, part_rows, chunk))] * parts
        + [in_hbm((half, 2, NBLEN, chunk))]
        + [in_hbm((2, NBLEN, chunk))] * half,
        compiler_params=PARAMS,
        cost_estimate=cost(
            8 * (seqs + parts) * NBLEN * chunk, ATTEND_WEIGHT * 12 * DH * pairs, pairs
        ),
        name="attend_blocks",
    )(uses, *rows_in, arrived)
    return outs[:parts], outs[parts], outs[parts + 1 :]


def owner_kernel(seqs, lists, near_ref, *rest):
    half = seqs // 2
    far_refs, out_ref, acc = rest[:half], rest[-2], rest[-1]
    me = lax.axis_index("enc")
    base = me - me % half
    acc[...] = jnp.zeros_like(acc)
    for step in range(half):
        acc[lists[0, base + step, 0]] += near_ref[step].astype(F32)
        acc[lists[0, across(me, step, seqs), 0]] += far_refs[step][...].astype(F32)
    out_ref[...] = acc[...].astype(BF16)


def owner_sum(first, send_lists, near, far, shape, so_far):
    half = len(far)
    chunk = near.shape[-1]
    wide = math.gcd(math.gcd(first, chunk), 256)
    skip, steps = first // wide, chunk // wide
    extra = [] if so_far is None else [so_far]
    return pl.pallas_call(
        functools.partial(owner_kernel, 2 * half),
        grid=(steps,),
        in_specs=[SCALARS, pl.BlockSpec((half, 2, NBLEN, wide), lambda i: (0, 0, 0, i))]
        + [pl.BlockSpec((2, NBLEN, wide), lambda i: (0, 0, i))] * half
        + [ANYWHERE] * len(extra),
        out_specs=pl.BlockSpec(
            (shape[0], 2, NBLEN, wide), lambda i: (0, 0, 0, skip + i)
        ),
        scratch_shapes=[pltpu.VMEM((shape[0], 2, NBLEN, wide), F32)],
        out_shape=in_hbm(shape),
        input_output_aliases={half + 2: 0} if extra else {},
        compiler_params=PARAMS,
        cost_estimate=cost(4 * (2 * half + shape[0]) * NBLEN * chunk, 4 * half * NBLEN * chunk),
        name="owner_sum",
    )(send_lists, near, *far, *extra)


def swap_far(pieces, done):
    half = len(pieces)
    there = [[half + (i + step) % half for i in range(half)] for step in range(half)]
    got = []
    for step, piece in enumerate(pieces):
        if len(done) >= DEPTH:
            piece = after(piece, done[-DEPTH])
        pairs = list(enumerate(there[step])) + [(peer, i) for i, peer in enumerate(there[step])]
        got.append(lax.ppermute(piece, "enc", pairs))
        done.append(got[-1])
    return got


def local(seqs, parts, queries, kv_pool, send_lists, block_slots, grad_context):
    width = kv_pool.shape[-1]
    heads = width // DH
    cut = (5 * heads // 8) * DH
    bounds = [(0, cut), (cut, width - cut)]
    firsts = [first for first, _ in bounds]

    arrived, rows = [], []
    for first, chunk in bounds:
        picked = pick(first, chunk, send_lists, kv_pool)
        send_lists, queries = after((send_lists, queries), picked)
        if rows:
            picked = after(picked, rows)
        arrived.append(swap_pool(picked))
        if not rows:
            for start, size in bounds:
                packed = pack(start, size, queries, grad_context, width, parts)
                rows.append(swap_rows(packed))
    done, returns, token_parts = [], [], []
    for h in range(2):
        rows_out, near, far = attend(block_slots, rows[h], arrived[h])
        far = swap_far(far, done)
        if h > 0:
            near = after(near, done[: seqs // 2])
        returns.append((swap_near(near, seqs), far))
        token_parts.append(swap_rows(rows_out))
        block_slots = after(block_slots, (token_parts[-1], far[:DEPTH]))
    context, grad_queries = unpack(token_parts, firsts, width, queries.shape)
    pool_grads = None
    for h, first in enumerate(firsts):
        pool_grads = owner_sum(first, send_lists, *returns[h], kv_pool.shape, pool_grads)
    return (context, grad_queries, pool_grads)


def solution(mesh):
    in_specs = (
        P("enc", "seq", None),
        P("enc", None, None, "seq"),
        P("enc", None, None),
        P("enc", None, None),
        P("enc", "seq", None),
    )
    out_specs = (P("enc", "seq", None), P("enc", "seq", None), P("enc", None, None, "seq"))
    body = functools.partial(local, mesh.shape["enc"], mesh.shape["seq"])
    return jax.shard_map(body, mesh=mesh, in_specs=in_specs, out_specs=out_specs, check_vma=False)
```

```python
import functools

import jax
import jax.numpy as jnp
from jax import lax
from jax.experimental import pallas as pl
from jax.experimental.pallas import tpu as pltpu
from jax.sharding import PartitionSpec as P

DH = 128
BLOCK = 64
NBLEN = 128
CHUNKS = 2
DEPTH = 2
ATTEND_WEIGHT = 24
F32 = jnp.float32
BF16 = jnp.bfloat16
LOG2E = 1.4426950408889634
VMEM_BYTES = 40 * 1024 * 1024


def partner(index, step, count):
    if count & (count - 1) == 0:
        return index ^ step
    return (step - index) % count


def exchange(array, axis, step, count):
    pairs = [(i, partner(i, step, count)) for i in range(count)]
    return lax.ppermute(array, axis, pairs)


def across(index, step, count):
    half = count // 2
    there = half + (index + step) % half
    return jnp.where(index < half, there, (index - step) % half)


def swap_near(array, count):
    half = count // 2
    groups = [list(range(half)), list(range(half, count))]
    return lax.all_to_all(
        array, "enc", split_axis=0, concat_axis=0, axis_index_groups=groups, tiled=True
    )


def swap_rows(pieces):
    count = len(pieces)
    return [pieces[0]] + [exchange(pieces[step], "seq", step, count) for step in range(1, count)]


def swap_pool(array):
    return lax.all_to_all(array, "enc", split_axis=0, concat_axis=0, tiled=True)


def after(array, earlier):
    return lax.optimization_barrier((array, earlier))[0]


def in_hbm(shape):
    return pltpu.HBM(shape, BF16)


def cost(moved, flops=0, exps=0):
    return pl.CostEstimate(flops=flops, bytes_accessed=moved, transcendentals=exps)


PARAMS = pltpu.CompilerParams(vmem_limit_bytes=VMEM_BYTES)
SCALARS = pl.BlockSpec(memory_space=pltpu.SMEM)
ANYWHERE = pl.BlockSpec(memory_space=pl.ANY)
IN_HBM = pl.BlockSpec(memory_space=pltpu.HBM)


def pack_kernel(first, width, q_ref, g_ref, *rest):
    outs, sems = rest[:-1], rest[-1]
    parts, chunk = len(outs), outs[0].shape[-1]
    me = lax.axis_index("seq")
    copies = []
    for step, out in enumerate(outs):
        start = pl.multiple_of(partner(me, step, parts) * width + first, DH)
        for n, ref in enumerate((q_ref, g_ref)):
            source = ref.at[0, :, pl.ds(start, chunk)]
            copies.append(pltpu.make_async_copy(source, out.at[n], sems.at[2 * step + n]))
            copies[-1].start()
    for copy in copies:
        copy.wait()


def pack(first, chunk, queries, grads, width, parts):
    shape = (2, queries.shape[1], chunk)
    return pl.pallas_call(
        functools.partial(pack_kernel, first, width),
        grid=(1,),
        in_specs=[IN_HBM, IN_HBM],
        out_specs=[pl.BlockSpec(shape, lambda i: (0, 0, 0))] * parts,
        out_shape=[in_hbm(shape)] * parts,
        scratch_shapes=[pltpu.SemaphoreType.DMA((2 * parts,))],
        compiler_params=PARAMS,
        cost_estimate=cost(8 * parts * queries.shape[1] * chunk),
        name="pack_rows",
    )(queries, grads)


def unpack_kernel(firsts, width, *refs):
    ins, (ctx_ref, gq_ref, sems) = refs[:-3], refs[-3:]
    parts = len(ins) // len(firsts)
    me = lax.axis_index("seq")
    copies = []
    for n, src in enumerate(ins):
        first, step = firsts[n // parts], n % parts
        start = pl.multiple_of(partner(me, step, parts) * width + first, DH)
        for k, ref in enumerate((ctx_ref, gq_ref)):
            target = ref.at[0, :, pl.ds(start, src.shape[-1])]
            copies.append(pltpu.make_async_copy(src.at[k], target, sems.at[2 * n + k]))
            copies[-1].start()
    for copy in copies:
        copy.wait()


def unpack(pieces, firsts, width, shape):
    flat = [array for piece in pieces for array in piece]
    return pl.pallas_call(
        functools.partial(unpack_kernel, firsts, width),
        grid=(1,),
        in_specs=[pl.BlockSpec(array.shape, lambda i: (0, 0, 0)) for array in flat],
        out_specs=[IN_HBM, IN_HBM],
        out_shape=[in_hbm(shape)] * 2,
        scratch_shapes=[pltpu.SemaphoreType.DMA((2 * len(flat),))],
        compiler_params=PARAMS,
        cost_estimate=cost(8 * shape[1] * shape[2]),
        name="unpack_rows",
    )(*flat)


def pick_kernel(first, lists, pool_ref, out_ref, sems):
    copies = []
    for seq in range(out_ref.shape[0]):
        source = pool_ref.at[lists[0, seq, 0], :, :, first : first + out_ref.shape[-1]]
        copies.append(pltpu.make_async_copy(source, out_ref.at[seq], sems.at[seq]))
        copies[-1].start()
    for copy in copies:
        copy.wait()


def pick(first, chunk, send_lists, kv_pool):
    shape = (send_lists.shape[1], 2, NBLEN, chunk)
    return pl.pallas_call(
        functools.partial(pick_kernel, first),
        grid=(1,),
        in_specs=[SCALARS, IN_HBM],
        out_specs=pl.BlockSpec(shape, lambda i: (0, 0, 0, 0)),
        out_shape=in_hbm(shape),
        scratch_shapes=[pltpu.SemaphoreType.DMA((shape[0],))],
        compiler_params=PARAMS,
        cost_estimate=cost(8 * shape[0] * NBLEN * chunk),
        name="pick_entries",
    )(send_lists, pltpu.with_memory_space_constraint(kv_pool, pltpu.HBM))


def dot(left, right, left_dim, right_dim):
    return lax.dot_general(
        left, right, (((left_dim,), (right_dim,)), ((), ())), preferred_element_type=F32
    )


def attend_kernel(seqs, parts, uses, *rest):
    half = seqs // 2
    rows_in, held, rest = rest[:parts], rest[parts], rest[parts + 1 :]
    rows_out, near_out, rest = rest[:parts], rest[parts], rest[parts + 1 :]
    far_out, (rows, made, sums) = rest[:half], rest[half:]
    scale = DH ** (-0.5)
    me, mine = lax.axis_index("enc"), lax.axis_index("seq")

    for step in range(parts):
        for n in range(2):
            piece = rows_in[step][n].astype(F32)
            rows[partner(mine, step, parts), n] = pltpu.roll(piece, 1, 0)
    rows[parts] = jnp.zeros(rows.shape[1:], F32)
    made[0, :, :BLOCK] = jnp.zeros((2, BLOCK, DH), F32)
    sums[...] = jnp.zeros_like(sums)
    first_row = lax.broadcasted_iota(jnp.int32, (BLOCK, DH), 0) == 0

    def blocks_of(first, qs, gs):
        several = range(len(qs))
        slots = [(uses[0, first + n, 0], uses[0, first + n, 1]) for n in several]
        keys = [jnp.concatenate([held[a, 0], held[b, 0]], axis=0) for a, b in slots]
        values = [jnp.concatenate([held[a, 1], held[b, 1]], axis=0) for a, b in slots]
        scores = [dot(qs[n], keys[n], 1, 1) for n in several]
        grad_probs = [dot(gs[n], values[n], 1, 1) for n in several]
        peaks = [jnp.max(scores[n], axis=1, keepdims=True) for n in several]
        weights = [jnp.exp2((scores[n] - peaks[n]) * (scale * LOG2E)) for n in several]
        shares = [1.0 / jnp.sum(weights[n], axis=1, keepdims=True) for n in several]
        probs = [weights[n] * shares[n] for n in several]
        probs_low = [probs[n].astype(BF16) for n in several]
        inner = [jnp.sum(probs[n] * grad_probs[n], axis=1, keepdims=True) for n in several]
        out = [dot(probs_low[n], values[n], 1, 0) for n in several]
        grad_values = [dot(probs_low[n], gs[n], 0, 0) for n in several]
        grad_scores = [
            (probs[n] * ((grad_probs[n] - inner[n]) * scale)).astype(BF16) for n in several
        ]
        grad_q = [dot(grad_scores[n], keys[n], 1, 0) for n in several]
        grad_keys = [dot(grad_scores[n], qs[n], 0, 0) for n in several]
        for n, (a, b) in enumerate(slots):
            sums[a, 0] += grad_keys[n][:NBLEN]
            sums[b, 0] += grad_keys[n][NBLEN:]
            sums[a, 1] += grad_values[n][:NBLEN]
            sums[b, 1] += grad_values[n][NBLEN:]
        return out, grad_q

    def one_part(part, carry):
        inputs = []
        for n in range(2):
            later = jnp.where(first_row, rows[part, n, :BLOCK], rows[part + 1, n, :BLOCK])
            inputs.append([rows[part, n, BLOCK:].astype(BF16), later.astype(BF16)])
        for n, (even, odd) in enumerate(blocks_of(2 * part, *inputs)):
            made[part, n, BLOCK:] = even
            made[part + 1, n, :BLOCK] = odd
            made[part, n, :1] = odd[:1]
        return carry

    if parts <= 4:
        for part in range(parts):
            one_part(part, 0)
    else:
        lax.fori_loop(0, parts, one_part, 0)

    for step in range(parts):
        for n in range(2):
            piece = made[partner(mine, step, parts), n]
            rows_out[step][n] = pltpu.roll(piece, 2 * BLOCK - 1, 0).astype(BF16)
    base = me - me % half
    for step in range(half):
        near_out[step] = sums[base + step].astype(BF16)
        far_out[step][...] = sums[across(me, step, seqs)].astype(BF16)


def attend(uses, rows_in, arrived):
    parts, part_rows = len(rows_in), rows_in[0].shape[1]
    seqs, _, _, chunk = arrived.shape
    half, heads = seqs // 2, chunk // DH
    rows_spec = pl.BlockSpec((2, part_rows, DH), lambda i: (0, 0, i))
    far_spec = pl.BlockSpec((2, NBLEN, DH), lambda i: (0, 0, i))
    pairs = heads * parts * part_rows * 2 * NBLEN
    outs = pl.pallas_call(
        functools.partial(attend_kernel, seqs, parts),
        grid=(heads,),
        in_specs=[SCALARS]
        + [rows_spec] * parts
        + [pl.BlockSpec((seqs, 2, NBLEN, DH), lambda i: (0, 0, 0, i))],
        out_specs=[rows_spec] * parts
        + [pl.BlockSpec((half, 2, NBLEN, DH), lambda i: (0, 0, 0, i))]
        + [far_spec] * half,
        scratch_shapes=[
            pltpu.VMEM((parts + 1, 2, part_rows, DH), F32),
            pltpu.VMEM((parts + 1, 2, part_rows, DH), F32),
            pltpu.VMEM((seqs, 2, NBLEN, DH), F32),
        ],
        out_shape=[in_hbm((2, part_rows, chunk))] * parts
        + [in_hbm((half, 2, NBLEN, chunk))]
        + [in_hbm((2, NBLEN, chunk))] * half,
        compiler_params=PARAMS,
        cost_estimate=cost(
            8 * (seqs + parts) * NBLEN * chunk, ATTEND_WEIGHT * 12 * DH * pairs, pairs
        ),
        name="attend_blocks",
    )(uses, *rows_in, arrived)
    return outs[:parts], outs[parts], outs[parts + 1 :]


def owner_kernel(seqs, lists, near_ref, *rest):
    half = seqs // 2
    far_refs, out_ref, acc = rest[:half], rest[-2], rest[-1]
    me = lax.axis_index("enc")
    base = me - me % half
    acc[...] = jnp.zeros_like(acc)
    for step in range(half):
        acc[lists[0, base + step, 0]] += near_ref[step].astype(F32)
        acc[lists[0, across(me, step, seqs), 0]] += far_refs[step][...].astype(F32)
    out_ref[...] = acc[...].astype(BF16)


def owner_sum(h, send_lists, near, far, shape, so_far):
    half = len(far)
    chunk = near.shape[-1]
    wide = min(chunk, 256)
    steps = chunk // wide
    extra = [] if so_far is None else [so_far]
    return pl.pallas_call(
        functools.partial(owner_kernel, 2 * half),
        grid=(steps,),
        in_specs=[SCALARS, pl.BlockSpec((half, 2, NBLEN, wide), lambda i: (0, 0, 0, i))]
        + [pl.BlockSpec((2, NBLEN, wide), lambda i: (0, 0, i))] * half
        + [ANYWHERE] * len(extra),
        out_specs=pl.BlockSpec(
            (shape[0], 2, NBLEN, wide), lambda i: (0, 0, 0, h * steps + i)
        ),
        scratch_shapes=[pltpu.VMEM((shape[0], 2, NBLEN, wide), F32)],
        out_shape=in_hbm(shape),
        input_output_aliases={half + 2: 0} if extra else {},
        compiler_params=PARAMS,
        cost_estimate=cost(4 * (2 * half + shape[0]) * NBLEN * chunk, 4 * half * NBLEN * chunk),
        name="owner_sum",
    )(send_lists, near, *far, *extra)


def swap_far(pieces, done):
    half = len(pieces)
    there = [[half + (i + step) % half for i in range(half)] for step in range(half)]
    got = []
    for step, piece in enumerate(pieces):
        if len(done) >= DEPTH:
            piece = after(piece, done[-DEPTH])
        pairs = list(enumerate(there[step])) + [(peer, i) for i, peer in enumerate(there[step])]
        got.append(lax.ppermute(piece, "enc", pairs))
        done.append(got[-1])
    return got


def local(seqs, parts, queries, kv_pool, send_lists, block_slots, grad_context):
    width = kv_pool.shape[-1]
    chunks = min(CHUNKS, width // DH)
    chunk = width // chunks
    firsts = [h * chunk for h in range(chunks)]

    arrived, rows = [], []
    for first in firsts:
        picked = pick(first, chunk, send_lists, kv_pool)
        send_lists, queries = after((send_lists, queries), picked)
        if rows:
            picked = after(picked, rows)
        arrived.append(swap_pool(picked))
        if not rows:
            for start in firsts:
                packed = pack(start, chunk, queries, grad_context, width, parts)
                rows.append(swap_rows(packed))
    done, returns, token_parts = [], [], []
    for h in range(chunks):
        rows_out, near, far = attend(block_slots, rows[h], arrived[h])
        far = swap_far(far, done)
        if h > 0:
            near = after(near, done[: seqs // 2])
        returns.append((swap_near(near, seqs), far))
        token_parts.append(swap_rows(rows_out))
        block_slots = after(block_slots, (token_parts[-1], far[:DEPTH]))
    context, grad_queries = unpack(token_parts, firsts, width, queries.shape)
    pool_grads = None
    for h in range(chunks):
        pool_grads = owner_sum(h, send_lists, *returns[h], kv_pool.shape, pool_grads)
    return (context, grad_queries, pool_grads)


def solution(mesh):
    in_specs = (
        P("enc", "seq", None),
        P("enc", None, None, "seq"),
        P("enc", None, None),
        P("enc", None, None),
        P("enc", "seq", None),
    )
    out_specs = (P("enc", "seq", None), P("enc", "seq", None), P("enc", None, None, "seq"))
    body = functools.partial(local, mesh.shape["enc"], mesh.shape["seq"])
    return jax.shard_map(body, mesh=mesh, in_specs=in_specs, out_specs=out_specs, check_vma=False)
```

```python
import functools

import jax
import jax.numpy as jnp
from jax import lax
from jax.experimental import pallas as pl
from jax.experimental.pallas import tpu as pltpu
from jax.sharding import PartitionSpec as P

DH = 128
BLOCK = 64
NBLEN = 128
CHUNKS = 2
DEPTH = 2
ATTEND_WEIGHT = 24
F32 = jnp.float32
BF16 = jnp.bfloat16
LOG2E = 1.4426950408889634
VMEM_BYTES = 40 * 1024 * 1024


def partner(index, step, count):
    if count & (count - 1) == 0:
        return index ^ step
    return (step - index) % count


def exchange(array, axis, step, count):
    pairs = [(i, partner(i, step, count)) for i in range(count)]
    return lax.ppermute(array, axis, pairs)


def across(index, step, count):
    half = count // 2
    there = half + (index + step) % half
    return jnp.where(index < half, there, (index - step) % half)


def swap_near(array, count):
    half = count // 2
    groups = [list(range(half)), list(range(half, count))]
    return lax.all_to_all(
        array, "enc", split_axis=0, concat_axis=0, axis_index_groups=groups, tiled=True
    )


def swap_rows(pieces):
    count = len(pieces)
    return [pieces[0]] + [exchange(pieces[step], "seq", step, count) for step in range(1, count)]


def swap_pool(array):
    return lax.all_to_all(array, "enc", split_axis=0, concat_axis=0, tiled=True)


def after(array, earlier):
    return lax.optimization_barrier((array, earlier))[0]


def in_hbm(shape):
    return pltpu.HBM(shape, BF16)


def cost(moved, flops=0, exps=0):
    return pl.CostEstimate(flops=flops, bytes_accessed=moved, transcendentals=exps)


PARAMS = pltpu.CompilerParams(vmem_limit_bytes=VMEM_BYTES)
SCALARS = pl.BlockSpec(memory_space=pltpu.SMEM)
ANYWHERE = pl.BlockSpec(memory_space=pl.ANY)
IN_HBM = pl.BlockSpec(memory_space=pltpu.HBM)


def pack_kernel(first, width, q_ref, g_ref, *rest):
    outs, sems = rest[:-1], rest[-1]
    parts, chunk = len(outs), outs[0].shape[-1]
    me = lax.axis_index("seq")
    copies = []
    for step, out in enumerate(outs):
        start = pl.multiple_of(partner(me, step, parts) * width + first, DH)
        for n, ref in enumerate((q_ref, g_ref)):
            source = ref.at[0, :, pl.ds(start, chunk)]
            copies.append(pltpu.make_async_copy(source, out.at[n], sems.at[2 * step + n]))
            copies[-1].start()
    for copy in copies:
        copy.wait()


def pack(first, chunk, queries, grads, width, parts):
    shape = (2, queries.shape[1], chunk)
    return pl.pallas_call(
        functools.partial(pack_kernel, first, width),
        grid=(1,),
        in_specs=[IN_HBM, IN_HBM],
        out_specs=[pl.BlockSpec(shape, lambda i: (0, 0, 0))] * parts,
        out_shape=[in_hbm(shape)] * parts,
        scratch_shapes=[pltpu.SemaphoreType.DMA((2 * parts,))],
        compiler_params=PARAMS,
        cost_estimate=cost(8 * parts * queries.shape[1] * chunk),
        name="pack_rows",
    )(queries, grads)


def unpack_kernel(firsts, width, *refs):
    ins, (ctx_ref, gq_ref, sems) = refs[:-3], refs[-3:]
    parts = len(ins) // len(firsts)
    me = lax.axis_index("seq")
    copies = []
    for n, src in enumerate(ins):
        first, step = firsts[n // parts], n % parts
        start = pl.multiple_of(partner(me, step, parts) * width + first, DH)
        for k, ref in enumerate((ctx_ref, gq_ref)):
            target = ref.at[0, :, pl.ds(start, src.shape[-1])]
            copies.append(pltpu.make_async_copy(src.at[k], target, sems.at[2 * n + k]))
            copies[-1].start()
    for copy in copies:
        copy.wait()


def unpack(pieces, firsts, width, shape):
    flat = [array for piece in pieces for array in piece]
    return pl.pallas_call(
        functools.partial(unpack_kernel, firsts, width),
        grid=(1,),
        in_specs=[pl.BlockSpec(array.shape, lambda i: (0, 0, 0)) for array in flat],
        out_specs=[IN_HBM, IN_HBM],
        out_shape=[in_hbm(shape)] * 2,
        scratch_shapes=[pltpu.SemaphoreType.DMA((2 * len(flat),))],
        compiler_params=PARAMS,
        cost_estimate=cost(8 * shape[1] * shape[2]),
        name="unpack_rows",
    )(*flat)


def pick_kernel(first, lists, pool_ref, out_ref, held, sems):
    seqs, chunk = held.shape[0], held.shape[-1]
    arriving, leaving = [], []
    for seq in range(seqs):
        source = pool_ref.at[lists[0, seq, 0], :, :, first : first + chunk]
        arriving.append(pltpu.make_async_copy(source, held.at[seq], sems.at[0, seq]))
        leaving.append(pltpu.make_async_copy(held.at[seq], out_ref.at[seq], sems.at[1, seq]))
        arriving[seq].start()
    for seq in range(seqs):
        arriving[seq].wait()
        leaving[seq].start()
    for seq in range(seqs):
        leaving[seq].wait()


def pick(first, chunk, send_lists, kv_pool):
    shape = (send_lists.shape[1], 2, NBLEN, chunk)
    return pl.pallas_call(
        functools.partial(pick_kernel, first),
        grid=(1,),
        in_specs=[SCALARS, IN_HBM],
        out_specs=IN_HBM,
        out_shape=in_hbm(shape),
        scratch_shapes=[pltpu.VMEM(shape, BF16), pltpu.SemaphoreType.DMA((2, shape[0]))],
        compiler_params=PARAMS,
        cost_estimate=cost(8 * shape[0] * NBLEN * chunk),
        name="pick_entries",
    )(send_lists, pltpu.with_memory_space_constraint(kv_pool, pltpu.HBM))


def dot(left, right, left_dim, right_dim):
    return lax.dot_general(
        left, right, (((left_dim,), (right_dim,)), ((), ())), preferred_element_type=F32
    )


def attend_kernel(seqs, parts, uses, *rest):
    half = seqs // 2
    rows_in, held, rest = rest[:parts], rest[parts], rest[parts + 1 :]
    rows_out, near_out, rest = rest[:parts], rest[parts], rest[parts + 1 :]
    far_out, (rows, made, sums) = rest[:half], rest[half:]
    scale = DH ** (-0.5)
    me, mine = lax.axis_index("enc"), lax.axis_index("seq")

    for step in range(parts):
        for n in range(2):
            piece = rows_in[step][n].astype(F32)
            rows[partner(mine, step, parts), n] = pltpu.roll(piece, 1, 0)
    rows[parts] = jnp.zeros(rows.shape[1:], F32)
    made[0, :, :BLOCK] = jnp.zeros((2, BLOCK, DH), F32)
    sums[...] = jnp.zeros_like(sums)
    first_row = lax.broadcasted_iota(jnp.int32, (BLOCK, DH), 0) == 0

    def blocks_of(first, qs, gs):
        several = range(len(qs))
        slots = [(uses[0, first + n, 0], uses[0, first + n, 1]) for n in several]
        keys = [jnp.concatenate([held[a, 0], held[b, 0]], axis=0) for a, b in slots]
        values = [jnp.concatenate([held[a, 1], held[b, 1]], axis=0) for a, b in slots]
        scores = [dot(qs[n], keys[n], 1, 1) for n in several]
        grad_probs = [dot(gs[n], values[n], 1, 1) for n in several]
        peaks = [jnp.max(scores[n], axis=1, keepdims=True) for n in several]
        weights = [jnp.exp2((scores[n] - peaks[n]) * (scale * LOG2E)) for n in several]
        shares = [1.0 / jnp.sum(weights[n], axis=1, keepdims=True) for n in several]
        probs = [weights[n] * shares[n] for n in several]
        probs_low = [probs[n].astype(BF16) for n in several]
        inner = [jnp.sum(probs[n] * grad_probs[n], axis=1, keepdims=True) for n in several]
        out = [dot(probs_low[n], values[n], 1, 0) for n in several]
        grad_values = [dot(probs_low[n], gs[n], 0, 0) for n in several]
        grad_scores = [
            (probs[n] * ((grad_probs[n] - inner[n]) * scale)).astype(BF16) for n in several
        ]
        grad_q = [dot(grad_scores[n], keys[n], 1, 0) for n in several]
        grad_keys = [dot(grad_scores[n], qs[n], 0, 0) for n in several]
        for n, (a, b) in enumerate(slots):
            sums[a, 0] += grad_keys[n][:NBLEN]
            sums[b, 0] += grad_keys[n][NBLEN:]
            sums[a, 1] += grad_values[n][:NBLEN]
            sums[b, 1] += grad_values[n][NBLEN:]
        return out, grad_q

    def one_part(part, carry):
        inputs = []
        for n in range(2):
            later = jnp.where(first_row, rows[part, n, :BLOCK], rows[part + 1, n, :BLOCK])
            inputs.append([rows[part, n, BLOCK:].astype(BF16), later.astype(BF16)])
        for n, (even, odd) in enumerate(blocks_of(2 * part, *inputs)):
            made[part, n, BLOCK:] = even
            made[part + 1, n, :BLOCK] = odd
            made[part, n, :1] = odd[:1]
        return carry

    if parts <= 4:
        for part in range(parts):
            one_part(part, 0)
    else:
        lax.fori_loop(0, parts, one_part, 0)

    for step in range(parts):
        for n in range(2):
            piece = made[partner(mine, step, parts), n]
            rows_out[step][n] = pltpu.roll(piece, 2 * BLOCK - 1, 0).astype(BF16)
    base = me - me % half
    for step in range(half):
        near_out[step] = sums[base + step].astype(BF16)
        far_out[step][...] = sums[across(me, step, seqs)].astype(BF16)


def attend(uses, rows_in, arrived):
    parts, part_rows = len(rows_in), rows_in[0].shape[1]
    seqs, _, _, chunk = arrived.shape
    half, heads = seqs // 2, chunk // DH
    rows_spec = pl.BlockSpec((2, part_rows, DH), lambda i: (0, 0, i))
    far_spec = pl.BlockSpec((2, NBLEN, DH), lambda i: (0, 0, i))
    pairs = heads * parts * part_rows * 2 * NBLEN
    outs = pl.pallas_call(
        functools.partial(attend_kernel, seqs, parts),
        grid=(heads,),
        in_specs=[SCALARS]
        + [rows_spec] * parts
        + [pl.BlockSpec((seqs, 2, NBLEN, DH), lambda i: (0, 0, 0, i))],
        out_specs=[rows_spec] * parts
        + [pl.BlockSpec((half, 2, NBLEN, DH), lambda i: (0, 0, 0, i))]
        + [far_spec] * half,
        scratch_shapes=[
            pltpu.VMEM((parts + 1, 2, part_rows, DH), F32),
            pltpu.VMEM((parts + 1, 2, part_rows, DH), F32),
            pltpu.VMEM((seqs, 2, NBLEN, DH), F32),
        ],
        out_shape=[in_hbm((2, part_rows, chunk))] * parts
        + [in_hbm((half, 2, NBLEN, chunk))]
        + [in_hbm((2, NBLEN, chunk))] * half,
        compiler_params=PARAMS,
        cost_estimate=cost(
            8 * (seqs + parts) * NBLEN * chunk, ATTEND_WEIGHT * 12 * DH * pairs, pairs
        ),
        name="attend_blocks",
    )(uses, *rows_in, arrived)
    return outs[:parts], outs[parts], outs[parts + 1 :]


def owner_kernel(seqs, lists, near_ref, *rest):
    half = seqs // 2
    far_refs, out_ref, acc = rest[:half], rest[-2], rest[-1]
    me = lax.axis_index("enc")
    base = me - me % half
    acc[...] = jnp.zeros_like(acc)
    for step in range(half):
        acc[lists[0, base + step, 0]] += near_ref[step].astype(F32)
        acc[lists[0, across(me, step, seqs), 0]] += far_refs[step][...].astype(F32)
    out_ref[...] = acc[...].astype(BF16)


def owner_sum(h, send_lists, near, far, shape, so_far):
    half = len(far)
    chunk = near.shape[-1]
    wide = min(chunk, 256)
    steps = chunk // wide
    extra = [] if so_far is None else [so_far]
    return pl.pallas_call(
        functools.partial(owner_kernel, 2 * half),
        grid=(steps,),
        in_specs=[SCALARS, pl.BlockSpec((half, 2, NBLEN, wide), lambda i: (0, 0, 0, i))]
        + [pl.BlockSpec((2, NBLEN, wide), lambda i: (0, 0, i))] * half
        + [ANYWHERE] * len(extra),
        out_specs=pl.BlockSpec(
            (shape[0], 2, NBLEN, wide), lambda i: (0, 0, 0, h * steps + i)
        ),
        scratch_shapes=[pltpu.VMEM((shape[0], 2, NBLEN, wide), F32)],
        out_shape=in_hbm(shape),
        input_output_aliases={half + 2: 0} if extra else {},
        compiler_params=PARAMS,
        cost_estimate=cost(4 * (2 * half + shape[0]) * NBLEN * chunk, 4 * half * NBLEN * chunk),
        name="owner_sum",
    )(send_lists, near, *far, *extra)


def swap_far(pieces, done):
    half = len(pieces)
    there = [[half + (i + step) % half for i in range(half)] for step in range(half)]
    got = []
    for step, piece in enumerate(pieces):
        if len(done) >= DEPTH:
            piece = after(piece, done[-DEPTH])
        pairs = list(enumerate(there[step])) + [(peer, i) for i, peer in enumerate(there[step])]
        got.append(lax.ppermute(piece, "enc", pairs))
        done.append(got[-1])
    return got


def local(seqs, parts, queries, kv_pool, send_lists, block_slots, grad_context):
    width = kv_pool.shape[-1]
    chunks = min(CHUNKS, width // DH)
    chunk = width // chunks
    firsts = [h * chunk for h in range(chunks)]

    arrived, rows = [], []
    for first in firsts:
        picked = pick(first, chunk, send_lists, kv_pool)
        send_lists, queries = after((send_lists, queries), picked)
        if rows:
            picked = after(picked, rows)
        arrived.append(swap_pool(picked))
        if not rows:
            for start in firsts:
                packed = pack(start, chunk, queries, grad_context, width, parts)
                rows.append(swap_rows(packed))
    done, returns, token_parts = [], [], []
    for h in range(chunks):
        rows_out, near, far = attend(block_slots, rows[h], arrived[h])
        far = swap_far(far, done)
        if h > 0:
            near = after(near, done[seqs // 2])
        returns.append((swap_near(near, seqs), far))
        token_parts.append(swap_rows(rows_out))
        block_slots = after(block_slots, (token_parts[-1], far[:DEPTH]))
    context, grad_queries = unpack(token_parts, firsts, width, queries.shape)
    pool_grads = None
    for h in range(chunks):
        pool_grads = owner_sum(h, send_lists, *returns[h], kv_pool.shape, pool_grads)
    return (context, grad_queries, pool_grads)


def solution(mesh):
    in_specs = (
        P("enc", "seq", None),
        P("enc", None, None, "seq"),
        P("enc", None, None),
        P("enc", None, None),
        P("enc", "seq", None),
    )
    out_specs = (P("enc", "seq", None), P("enc", "seq", None), P("enc", None, None, "seq"))
    body = functools.partial(local, mesh.shape["enc"], mesh.shape["seq"])
    return jax.shard_map(body, mesh=mesh, in_specs=in_specs, out_specs=out_specs, check_vma=False)
```

```python
import functools
import math

import jax
import jax.numpy as jnp
from jax import lax
from jax.experimental import pallas as pl
from jax.experimental.pallas import tpu as pltpu
from jax.sharding import PartitionSpec as P

DH = 128
BLOCK = 64
NBLEN = 128
ATTEND_WEIGHT = 24
SHARE = 8
F32 = jnp.float32
BF16 = jnp.bfloat16
LOG2E = 1.4426950408889634
VMEM_BYTES = 40 * 1024 * 1024


def partner(index, step, count):
    if count & (count - 1) == 0:
        return index ^ step
    return (step - index) % count


def exchange(array, axis, step, count):
    pairs = [(i, partner(i, step, count)) for i in range(count)]
    return lax.ppermute(array, axis, pairs)


def across(index, step, count):
    half = count // 2
    there = half + (index + step) % half
    return jnp.where(index < half, there, (index - step) % half)


def swap_near(array, count):
    half = count // 2
    groups = [list(range(half)), list(range(half, count))]
    return lax.all_to_all(
        array, "enc", split_axis=0, concat_axis=0, axis_index_groups=groups, tiled=True
    )


def swap_rows(pieces):
    count = len(pieces)
    return [pieces[0]] + [exchange(pieces[step], "seq", step, count) for step in range(1, count)]


def swap_pool(array):
    return lax.all_to_all(array, "enc", split_axis=0, concat_axis=0, tiled=True)


def after(array, earlier):
    return lax.optimization_barrier((array, earlier))[0]


def in_hbm(shape):
    return pltpu.HBM(shape, BF16)


def cost(moved, flops=0, exps=0):
    return pl.CostEstimate(flops=flops, bytes_accessed=moved, transcendentals=exps)


PARAMS = pltpu.CompilerParams(vmem_limit_bytes=VMEM_BYTES)
SCALARS = pl.BlockSpec(memory_space=pltpu.SMEM)
ANYWHERE = pl.BlockSpec(memory_space=pl.ANY)
IN_HBM = pl.BlockSpec(memory_space=pltpu.HBM)


def pack_kernel(first, width, q_ref, g_ref, *rest):
    outs, sems = rest[:-1], rest[-1]
    parts, chunk = len(outs), outs[0].shape[-1]
    me = lax.axis_index("seq")
    copies = []
    for step, out in enumerate(outs):
        start = pl.multiple_of(partner(me, step, parts) * width + first, DH)
        for n, ref in enumerate((q_ref, g_ref)):
            source = ref.at[0, :, pl.ds(start, chunk)]
            copies.append(pltpu.make_async_copy(source, out.at[n], sems.at[2 * step + n]))
            copies[-1].start()
    for copy in copies:
        copy.wait()


def pack(first, chunk, queries, grads, width, parts):
    shape = (2, queries.shape[1], chunk)
    return pl.pallas_call(
        functools.partial(pack_kernel, first, width),
        grid=(1,),
        in_specs=[IN_HBM, IN_HBM],
        out_specs=[pl.BlockSpec(shape, lambda i: (0, 0, 0))] * parts,
        out_shape=[in_hbm(shape)] * parts,
        scratch_shapes=[pltpu.SemaphoreType.DMA((2 * parts,))],
        compiler_params=PARAMS,
        cost_estimate=cost(8 * parts * queries.shape[1] * chunk),
        name="pack_rows",
    )(queries, grads)


def unpack_kernel(firsts, width, *refs):
    ins, (ctx_ref, gq_ref, sems) = refs[:-3], refs[-3:]
    parts = len(ins) // len(firsts)
    me = lax.axis_index("seq")
    copies = []
    for n, src in enumerate(ins):
        first, step = firsts[n // parts], n % parts
        start = pl.multiple_of(partner(me, step, parts) * width + first, DH)
        for k, ref in enumerate((ctx_ref, gq_ref)):
            target = ref.at[0, :, pl.ds(start, src.shape[-1])]
            copies.append(pltpu.make_async_copy(src.at[k], target, sems.at[2 * n + k]))
            copies[-1].start()
    for copy in copies:
        copy.wait()


def unpack(pieces, firsts, width, shape):
    flat = [array for piece in pieces for array in piece]
    return pl.pallas_call(
        functools.partial(unpack_kernel, firsts, width),
        grid=(1,),
        in_specs=[pl.BlockSpec(array.shape, lambda i: (0, 0, 0)) for array in flat],
        out_specs=[IN_HBM, IN_HBM],
        out_shape=[in_hbm(shape)] * 2,
        scratch_shapes=[pltpu.SemaphoreType.DMA((2 * len(flat),))],
        compiler_params=PARAMS,
        cost_estimate=cost(8 * shape[1] * shape[2]),
        name="unpack_rows",
    )(*flat)


def pick_kernel(first, lists, pool_ref, out_ref, held, sems):
    seqs, chunk = held.shape[0], held.shape[-1]
    arriving, leaving = [], []
    for seq in range(seqs):
        source = pool_ref.at[lists[0, seq, 0], :, :, first : first + chunk]
        arriving.append(pltpu.make_async_copy(source, held.at[seq], sems.at[0, seq]))
        leaving.append(pltpu.make_async_copy(held.at[seq], out_ref.at[seq], sems.at[1, seq]))
        arriving[seq].start()
    for seq in range(seqs):
        arriving[seq].wait()
        leaving[seq].start()
    for seq in range(seqs):
        leaving[seq].wait()


def pick(first, chunk, send_lists, kv_pool):
    shape = (send_lists.shape[1], 2, NBLEN, chunk)
    return pl.pallas_call(
        functools.partial(pick_kernel, first),
        grid=(1,),
        in_specs=[SCALARS, IN_HBM],
        out_specs=IN_HBM,
        out_shape=in_hbm(shape),
        scratch_shapes=[pltpu.VMEM(shape, BF16), pltpu.SemaphoreType.DMA((2, shape[0]))],
        compiler_params=PARAMS,
        cost_estimate=cost(8 * shape[0] * NBLEN * chunk),
        name="pick_entries",
    )(send_lists, pltpu.with_memory_space_constraint(kv_pool, pltpu.HBM))


def dot(left, right, left_dim, right_dim):
    return lax.dot_general(
        left, right, (((left_dim,), (right_dim,)), ((), ())), preferred_element_type=F32
    )


def attend_kernel(seqs, parts, split, uses, *rest):
    half = seqs // 2
    rows_in, held, rest = rest[:parts], rest[parts], rest[parts + 1 :]
    rows_out, kv_out, (rows, made, sums) = rest[:parts], rest[parts:-3], rest[-3:]
    scale = DH ** (-0.5)
    me, mine = lax.axis_index("enc"), lax.axis_index("seq")

    for step in range(parts):
        for n in range(2):
            piece = rows_in[step][n].astype(F32)
            rows[partner(mine, step, parts), n] = pltpu.roll(piece, 1, 0)
    rows[parts] = jnp.zeros(rows.shape[1:], F32)
    made[0, :, :BLOCK] = jnp.zeros((2, BLOCK, DH), F32)
    sums[...] = jnp.zeros_like(sums)
    first_row = lax.broadcasted_iota(jnp.int32, (BLOCK, DH), 0) == 0

    def blocks_of(first, qs, gs):
        several = range(len(qs))
        slots = [(uses[0, first + n, 0], uses[0, first + n, 1]) for n in several]
        keys = [jnp.concatenate([held[a, 0], held[b, 0]], axis=0) for a, b in slots]
        values = [jnp.concatenate([held[a, 1], held[b, 1]], axis=0) for a, b in slots]
        scores = [dot(qs[n], keys[n], 1, 1) for n in several]
        grad_probs = [dot(gs[n], values[n], 1, 1) for n in several]
        peaks = [jnp.max(scores[n], axis=1, keepdims=True) for n in several]
        weights = [jnp.exp2((scores[n] - peaks[n]) * (scale * LOG2E)) for n in several]
        shares = [1.0 / jnp.sum(weights[n], axis=1, keepdims=True) for n in several]
        probs = [weights[n] * shares[n] for n in several]
        probs_low = [probs[n].astype(BF16) for n in several]
        inner = [jnp.sum(probs[n] * grad_probs[n], axis=1, keepdims=True) for n in several]
        out = [dot(probs_low[n], values[n], 1, 0) for n in several]
        grad_values = [dot(probs_low[n], gs[n], 0, 0) for n in several]
        grad_scores = [
            (probs[n] * ((grad_probs[n] - inner[n]) * scale)).astype(BF16) for n in several
        ]
        grad_q = [dot(grad_scores[n], keys[n], 1, 0) for n in several]
        grad_keys = [dot(grad_scores[n], qs[n], 0, 0) for n in several]
        for n, (a, b) in enumerate(slots):
            sums[a, 0] += grad_keys[n][:NBLEN]
            sums[b, 0] += grad_keys[n][NBLEN:]
            sums[a, 1] += grad_values[n][:NBLEN]
            sums[b, 1] += grad_values[n][NBLEN:]
        return out, grad_q

    def one_part(part, carry):
        inputs = []
        for n in range(2):
            later = jnp.where(first_row, rows[part, n, :BLOCK], rows[part + 1, n, :BLOCK])
            inputs.append([rows[part, n, BLOCK:].astype(BF16), later.astype(BF16)])
        for n, (even, odd) in enumerate(blocks_of(2 * part, *inputs)):
            made[part, n, BLOCK:] = even
            made[part + 1, n, :BLOCK] = odd
            made[part, n, :1] = odd[:1]
        return carry

    if parts <= 4:
        for part in range(parts):
            one_part(part, 0)
    else:
        lax.fori_loop(0, parts, one_part, 0)

    for step in range(parts):
        for n in range(2):
            piece = made[partner(mine, step, parts), n]
            rows_out[step][n] = pltpu.roll(piece, 2 * BLOCK - 1, 0).astype(BF16)
    if split:
        base = me - me % half
        for step in range(half):
            kv_out[0][step] = sums[base + step].astype(BF16)
            kv_out[1 + step][...] = sums[across(me, step, seqs)].astype(BF16)
    else:
        kv_out[0][...] = sums[...].astype(BF16)


def attend(uses, rows_in, arrived, split):
    parts, part_rows = len(rows_in), rows_in[0].shape[1]
    seqs, _, _, chunk = arrived.shape
    half, heads = seqs // 2, chunk // DH
    rows_spec = pl.BlockSpec((2, part_rows, DH), lambda i: (0, 0, i))
    shapes = [(seqs, 2, NBLEN)]
    if split:
        shapes = [(half, 2, NBLEN)] + [(2, NBLEN)] * half
    kv_specs = [
        pl.BlockSpec((*shape, DH), lambda i, n=len(shape): (0,) * n + (i,)) for shape in shapes
    ]
    pairs = heads * parts * part_rows * 2 * NBLEN
    outs = pl.pallas_call(
        functools.partial(attend_kernel, seqs, parts, split),
        grid=(heads,),
        in_specs=[SCALARS]
        + [rows_spec] * parts
        + [pl.BlockSpec((seqs, 2, NBLEN, DH), lambda i: (0, 0, 0, i))],
        out_specs=[rows_spec] * parts + kv_specs,
        scratch_shapes=[
            pltpu.VMEM((parts + 1, 2, part_rows, DH), F32),
            pltpu.VMEM((parts + 1, 2, part_rows, DH), F32),
            pltpu.VMEM((seqs, 2, NBLEN, DH), F32),
        ],
        out_shape=[in_hbm((2, part_rows, chunk))] * parts
        + [in_hbm((*shape, chunk)) for shape in shapes],
        compiler_params=PARAMS,
        cost_estimate=cost(
            8 * (seqs + parts) * NBLEN * chunk, ATTEND_WEIGHT * 12 * DH * pairs, pairs
        ),
        name="attend_blocks",
    )(uses, *rows_in, arrived)
    return outs[:parts], outs[parts:]


def owner_kernel(seqs, lists, *rest):
    half = seqs // 2
    first_ref, out_ref, acc = rest[0], rest[-2], rest[-1]
    me = lax.axis_index("enc")
    base = me - me % half
    acc[...] = jnp.zeros_like(acc)
    if first_ref.shape[0] == seqs:
        for seq in range(seqs):
            acc[lists[0, seq, 0]] += first_ref[seq].astype(F32)
    else:
        for step in range(half):
            acc[lists[0, base + step, 0]] += first_ref[step].astype(F32)
            acc[lists[0, across(me, step, seqs), 0]] += rest[1 + step][...].astype(F32)
    out_ref[...] = acc[...].astype(BF16)


def owner_sum(first, send_lists, back, shape, so_far):
    seqs = send_lists.shape[1]
    chunk = back[0].shape[-1]
    wide = math.gcd(math.gcd(first, chunk), 256)
    skip, steps = first // wide, chunk // wide
    extra = [] if so_far is None else [so_far]
    specs = [
        pl.BlockSpec((*array.shape[:-1], wide), lambda i, n=array.ndim - 1: (0,) * n + (i,))
        for array in back
    ]
    return pl.pallas_call(
        functools.partial(owner_kernel, seqs),
        grid=(steps,),
        in_specs=[SCALARS] + specs + [ANYWHERE] * len(extra),
        out_specs=pl.BlockSpec(
            (shape[0], 2, NBLEN, wide), lambda i: (0, 0, 0, skip + i)
        ),
        scratch_shapes=[pltpu.VMEM((shape[0], 2, NBLEN, wide), F32)],
        out_shape=in_hbm(shape),
        input_output_aliases={len(back) + 1: 0} if extra else {},
        compiler_params=PARAMS,
        cost_estimate=cost(4 * (seqs + shape[0]) * NBLEN * chunk, 2 * seqs * NBLEN * chunk),
        name="owner_sum",
    )(send_lists, *back, *extra)


def swap_far(pieces):
    half = len(pieces)
    got = []
    for step, piece in enumerate(pieces):
        there = [half + (i + step) % half for i in range(half)]
        pairs = list(enumerate(there)) + [(peer, i) for i, peer in enumerate(there)]
        got.append(lax.ppermute(piece, "enc", pairs))
    return got


def local(seqs, parts, queries, kv_pool, send_lists, block_slots, grad_context):
    width = kv_pool.shape[-1]
    cut = (SHARE * width // DH // 16) * DH
    bounds = [(0, cut), (cut, width - cut)]
    firsts = [first for first, _ in bounds]

    arrived, rows = [], []
    for first, chunk in bounds:
        picked = pick(first, chunk, send_lists, kv_pool)
        send_lists, queries = after((send_lists, queries), picked)
        if rows:
            picked = after(picked, rows)
        arrived.append(swap_pool(picked))
        if not rows:
            for start, size in bounds:
                packed = pack(start, size, queries, grad_context, width, parts)
                rows.append(swap_rows(packed))

    rows_out, (near, *far) = attend(block_slots, rows[0], arrived[0], True)
    far = swap_far(far)
    returns = [[swap_near(near, seqs), *far]]
    token_parts = [swap_rows(rows_out)]
    block_slots = after(block_slots, token_parts[0])
    rows_out, (whole,) = attend(block_slots, rows[1], arrived[1], False)
    token_parts.append(swap_rows(rows_out))
    returns.append([swap_pool(after(whole, far))])

    context, grad_queries = unpack(token_parts, firsts, width, queries.shape)
    pool_grads = None
    for first, back in zip(firsts, returns):
        pool_grads = owner_sum(first, send_lists, back, kv_pool.shape, pool_grads)
    return (context, grad_queries, pool_grads)


def solution(mesh):
    in_specs = (
        P("enc", "seq", None),
        P("enc", None, None, "seq"),
        P("enc", None, None),
        P("enc", None, None),
        P("enc", "seq", None),
    )
    out_specs = (P("enc", "seq", None), P("enc", "seq", None), P("enc", None, None, "seq"))
    body = functools.partial(local, mesh.shape["enc"], mesh.shape["seq"])
    return jax.shard_map(body, mesh=mesh, in_specs=in_specs, out_specs=out_specs, check_vma=False)
```

```python
import functools
import math

import jax
import jax.numpy as jnp
from jax import lax
from jax.experimental import pallas as pl
from jax.experimental.pallas import tpu as pltpu
from jax.sharding import PartitionSpec as P

DH = 128
BLOCK = 64
NBLEN = 128
ATTEND_WEIGHT = 24
SHARE = 8
F32 = jnp.float32
BF16 = jnp.bfloat16
LOG2E = 1.4426950408889634
VMEM_BYTES = 40 * 1024 * 1024


def partner(index, step, count):
    if count & (count - 1) == 0:
        return index ^ step
    return (step - index) % count


def exchange(array, axis, step, count):
    pairs = [(i, partner(i, step, count)) for i in range(count)]
    return lax.ppermute(array, axis, pairs)


def across(index, step, count):
    half = count // 2
    there = half + (index + step) % half
    return jnp.where(index < half, there, (index - step) % half)


def swap_near(array, count):
    half = count // 2
    groups = [list(range(half)), list(range(half, count))]
    return lax.all_to_all(
        array, "enc", split_axis=0, concat_axis=0, axis_index_groups=groups, tiled=True
    )


def swap_rows(pieces):
    count = len(pieces)
    return [pieces[0]] + [exchange(pieces[step], "seq", step, count) for step in range(1, count)]


def swap_pool(array):
    return lax.all_to_all(array, "enc", split_axis=0, concat_axis=0, tiled=True)


def after(array, earlier):
    return lax.optimization_barrier((array, earlier))[0]


def in_hbm(shape):
    return pltpu.HBM(shape, BF16)


def cost(moved, flops=0, exps=0):
    return pl.CostEstimate(flops=flops, bytes_accessed=moved, transcendentals=exps)


PARAMS = pltpu.CompilerParams(vmem_limit_bytes=VMEM_BYTES)
SCALARS = pl.BlockSpec(memory_space=pltpu.SMEM)
ANYWHERE = pl.BlockSpec(memory_space=pl.ANY)
IN_HBM = pl.BlockSpec(memory_space=pltpu.HBM)


def pack_kernel(first, width, q_ref, g_ref, *rest):
    outs, sems = rest[:-1], rest[-1]
    parts, chunk = len(outs), outs[0].shape[-1]
    me = lax.axis_index("seq")
    copies = []
    for step, out in enumerate(outs):
        start = pl.multiple_of(partner(me, step, parts) * width + first, DH)
        for n, ref in enumerate((q_ref, g_ref)):
            source = ref.at[0, :, pl.ds(start, chunk)]
            copies.append(pltpu.make_async_copy(source, out.at[n], sems.at[2 * step + n]))
            copies[-1].start()
    for copy in copies:
        copy.wait()


def pack(first, chunk, queries, grads, width, parts):
    shape = (2, queries.shape[1], chunk)
    return pl.pallas_call(
        functools.partial(pack_kernel, first, width),
        grid=(1,),
        in_specs=[IN_HBM, IN_HBM],
        out_specs=[pl.BlockSpec(shape, lambda i: (0, 0, 0))] * parts,
        out_shape=[in_hbm(shape)] * parts,
        scratch_shapes=[pltpu.SemaphoreType.DMA((2 * parts,))],
        compiler_params=PARAMS,
        cost_estimate=cost(8 * parts * queries.shape[1] * chunk),
        name="pack_rows",
    )(queries, grads)


def unpack_kernel(firsts, width, *refs):
    ins, (ctx_ref, gq_ref, sems) = refs[:-3], refs[-3:]
    parts = len(ins) // len(firsts)
    me = lax.axis_index("seq")
    copies = []
    for n, src in enumerate(ins):
        first, step = firsts[n // parts], n % parts
        start = pl.multiple_of(partner(me, step, parts) * width + first, DH)
        for k, ref in enumerate((ctx_ref, gq_ref)):
            target = ref.at[0, :, pl.ds(start, src.shape[-1])]
            copies.append(pltpu.make_async_copy(src.at[k], target, sems.at[2 * n + k]))
            copies[-1].start()
    for copy in copies:
        copy.wait()


def unpack(pieces, firsts, width, shape):
    flat = [array for piece in pieces for array in piece]
    return pl.pallas_call(
        functools.partial(unpack_kernel, firsts, width),
        grid=(1,),
        in_specs=[pl.BlockSpec(array.shape, lambda i: (0, 0, 0)) for array in flat],
        out_specs=[IN_HBM, IN_HBM],
        out_shape=[in_hbm(shape)] * 2,
        scratch_shapes=[pltpu.SemaphoreType.DMA((2 * len(flat),))],
        compiler_params=PARAMS,
        cost_estimate=cost(8 * shape[1] * shape[2]),
        name="unpack_rows",
    )(*flat)


def kv_shapes(seqs, chunk, split):
    half = seqs // 2
    if split:
        return [(half, 2, NBLEN, chunk)] + [(2, NBLEN, chunk)] * half
    return [(seqs, 2, NBLEN, chunk)]


def kv_views(refs, seqs, split):
    if not split:
        return [(seq, refs[0].at[seq]) for seq in range(seqs)]
    half = seqs // 2
    me = lax.axis_index("enc")
    near = [(me - me % half + step, refs[0].at[step]) for step in range(half)]
    return near + [(across(me, step, seqs), refs[1 + step]) for step in range(half)]


def pick_kernel(first, split, seqs, lists, pool_ref, *rest):
    outs, held, sems = rest[:-2], rest[-2], rest[-1]
    chunk = held.shape[-1]
    arriving, leaving = [], []
    for n, (seq, out) in enumerate(kv_views(outs, seqs, split)):
        source = pool_ref.at[lists[0, seq, 0], :, :, first : first + chunk]
        arriving.append(pltpu.make_async_copy(source, held.at[n], sems.at[0, n]))
        leaving.append(pltpu.make_async_copy(held.at[n], out, sems.at[1, n]))
        arriving[n].start()
    for n in range(seqs):
        arriving[n].wait()
        leaving[n].start()
    for n in range(seqs):
        leaving[n].wait()


def pick(first, chunk, split, send_lists, kv_pool):
    seqs = send_lists.shape[1]
    shapes = kv_shapes(seqs, chunk, split)
    return pl.pallas_call(
        functools.partial(pick_kernel, first, split, seqs),
        grid=(1,),
        in_specs=[SCALARS, IN_HBM],
        out_specs=[IN_HBM] * len(shapes),
        out_shape=[in_hbm(shape) for shape in shapes],
        scratch_shapes=[
            pltpu.VMEM((seqs, 2, NBLEN, chunk), BF16),
            pltpu.SemaphoreType.DMA((2, seqs)),
        ],
        compiler_params=PARAMS,
        cost_estimate=cost(8 * seqs * NBLEN * chunk),
        name="pick_entries",
    )(send_lists, pltpu.with_memory_space_constraint(kv_pool, pltpu.HBM))


def dot(left, right, left_dim, right_dim):
    return lax.dot_general(
        left, right, (((left_dim,), (right_dim,)), ((), ())), preferred_element_type=F32
    )


def attend_kernel(seqs, parts, split, uses, *rest):
    pieces = 1 + seqs // 2 if split else 1
    rows_in, rest = rest[:parts], rest[parts:]
    kv_in, rest = rest[:pieces], rest[pieces:]
    rows_out, rest = rest[:parts], rest[parts:]
    kv_out, rest = rest[:pieces], rest[pieces:]
    held, rows, made, sums = rest if split else (kv_in[0], *rest)
    scale = DH ** (-0.5)
    mine = lax.axis_index("seq")

    if split:
        for slot, piece in kv_views(kv_in, seqs, split):
            held[slot] = piece[...]
    for step in range(parts):
        for n in range(2):
            piece = rows_in[step][n].astype(F32)
            rows[partner(mine, step, parts), n] = pltpu.roll(piece, 1, 0)
    rows[parts] = jnp.zeros(rows.shape[1:], F32)
    made[0, :, :BLOCK] = jnp.zeros((2, BLOCK, DH), F32)
    sums[...] = jnp.zeros_like(sums)
    first_row = lax.broadcasted_iota(jnp.int32, (BLOCK, DH), 0) == 0

    def blocks_of(first, qs, gs):
        several = range(len(qs))
        slots = [(uses[0, first + n, 0], uses[0, first + n, 1]) for n in several]
        keys = [jnp.concatenate([held[a, 0], held[b, 0]], axis=0) for a, b in slots]
        values = [jnp.concatenate([held[a, 1], held[b, 1]], axis=0) for a, b in slots]
        scores = [dot(qs[n], keys[n], 1, 1) for n in several]
        grad_probs = [dot(gs[n], values[n], 1, 1) for n in several]
        peaks = [jnp.max(scores[n], axis=1, keepdims=True) for n in several]
        weights = [jnp.exp2((scores[n] - peaks[n]) * (scale * LOG2E)) for n in several]
        shares = [1.0 / jnp.sum(weights[n], axis=1, keepdims=True) for n in several]
        probs = [weights[n] * shares[n] for n in several]
        probs_low = [probs[n].astype(BF16) for n in several]
        inner = [jnp.sum(probs[n] * grad_probs[n], axis=1, keepdims=True) for n in several]
        out = [dot(probs_low[n], values[n], 1, 0) for n in several]
        grad_values = [dot(probs_low[n], gs[n], 0, 0) for n in several]
        grad_scores = [
            (probs[n] * ((grad_probs[n] - inner[n]) * scale)).astype(BF16) for n in several
        ]
        grad_q = [dot(grad_scores[n], keys[n], 1, 0) for n in several]
        grad_keys = [dot(grad_scores[n], qs[n], 0, 0) for n in several]
        for n, (a, b) in enumerate(slots):
            sums[a, 0] += grad_keys[n][:NBLEN]
            sums[b, 0] += grad_keys[n][NBLEN:]
            sums[a, 1] += grad_values[n][:NBLEN]
            sums[b, 1] += grad_values[n][NBLEN:]
        return out, grad_q

    def one_part(part, carry):
        inputs = []
        for n in range(2):
            later = jnp.where(first_row, rows[part, n, :BLOCK], rows[part + 1, n, :BLOCK])
            inputs.append([rows[part, n, BLOCK:].astype(BF16), later.astype(BF16)])
        for n, (even, odd) in enumerate(blocks_of(2 * part, *inputs)):
            made[part, n, BLOCK:] = even
            made[part + 1, n, :BLOCK] = odd
            made[part, n, :1] = odd[:1]
        return carry

    if parts <= 4:
        for part in range(parts):
            one_part(part, 0)
    else:
        lax.fori_loop(0, parts, one_part, 0)

    for step in range(parts):
        for n in range(2):
            piece = made[partner(mine, step, parts), n]
            rows_out[step][n] = pltpu.roll(piece, 2 * BLOCK - 1, 0).astype(BF16)
    for slot, piece in kv_views(kv_out, seqs, split):
        piece[...] = sums[slot].astype(BF16)


def heads_spec(shape, wide):
    return pl.BlockSpec((*shape[:-1], wide), lambda i, n=len(shape) - 1: (0,) * n + (i,))


def attend(uses, rows_in, kv_in):
    parts, part_rows = len(rows_in), rows_in[0].shape[1]
    split = len(kv_in) > 1
    seqs = 2 * kv_in[0].shape[0] if split else kv_in[0].shape[0]
    chunk = kv_in[0].shape[-1]
    heads = chunk // DH
    shapes = [array.shape for array in (*rows_in, *kv_in)]
    specs = [heads_spec(shape, DH) for shape in shapes]
    pairs = heads * parts * part_rows * 2 * NBLEN
    held = [pltpu.VMEM((seqs, 2, NBLEN, DH), BF16)] if split else []
    outs = pl.pallas_call(
        functools.partial(attend_kernel, seqs, parts, split),
        grid=(heads,),
        in_specs=[SCALARS] + specs,
        out_specs=specs,
        scratch_shapes=held
        + [
            pltpu.VMEM((parts + 1, 2, part_rows, DH), F32),
            pltpu.VMEM((parts + 1, 2, part_rows, DH), F32),
            pltpu.VMEM((seqs, 2, NBLEN, DH), F32),
        ],
        out_shape=[in_hbm(shape) for shape in shapes],
        compiler_params=PARAMS,
        cost_estimate=cost(
            8 * (seqs + parts) * NBLEN * chunk, ATTEND_WEIGHT * 12 * DH * pairs, pairs
        ),
        name="attend_blocks",
    )(uses, *rows_in, *kv_in)
    return outs[:parts], outs[parts:]


def owner_kernel(seqs, pieces, lists, *rest):
    out_ref, acc = rest[-2], rest[-1]
    acc[...] = jnp.zeros_like(acc)
    for seq, piece in kv_views(rest[:pieces], seqs, pieces > 1):
        acc[lists[0, seq, 0]] += piece[...].astype(F32)
    out_ref[...] = acc[...].astype(BF16)


def owner_sum(first, send_lists, back, shape, so_far):
    seqs = send_lists.shape[1]
    chunk = back[0].shape[-1]
    wide = math.gcd(math.gcd(first, chunk), 256)
    skip, steps = first // wide, chunk // wide
    extra = [] if so_far is None else [so_far]
    specs = [heads_spec(array.shape, wide) for array in back]
    return pl.pallas_call(
        functools.partial(owner_kernel, seqs, len(back)),
        grid=(steps,),
        in_specs=[SCALARS] + specs + [ANYWHERE] * len(extra),
        out_specs=pl.BlockSpec(
            (shape[0], 2, NBLEN, wide), lambda i: (0, 0, 0, skip + i)
        ),
        scratch_shapes=[pltpu.VMEM((shape[0], 2, NBLEN, wide), F32)],
        out_shape=in_hbm(shape),
        input_output_aliases={len(back) + 1: 0} if extra else {},
        compiler_params=PARAMS,
        cost_estimate=cost(4 * (seqs + shape[0]) * NBLEN * chunk, 2 * seqs * NBLEN * chunk),
        name="owner_sum",
    )(send_lists, *back, *extra)


def swap_far(pieces):
    half = len(pieces)
    got = []
    for step, piece in enumerate(pieces):
        there = [half + (i + step) % half for i in range(half)]
        pairs = list(enumerate(there)) + [(peer, i) for i, peer in enumerate(there)]
        if step >= 2:
            piece = after(piece, got[step - 2])
        got.append(lax.ppermute(piece, "enc", pairs))
    return got


def local(seqs, parts, queries, kv_pool, send_lists, block_slots, grad_context):
    width = kv_pool.shape[-1]
    cut = (SHARE * width // DH // 16) * DH
    bounds = [(0, cut), (cut, width - cut)]
    firsts = [first for first, _ in bounds]

    picked = pick(*bounds[0], False, send_lists, kv_pool)
    send_lists, queries = after((send_lists, queries), picked[0])
    early = swap_pool(picked[0])
    near, *far = pick(*bounds[1], True, send_lists, kv_pool)
    queries = after(queries, near)
    rows = [
        swap_rows(pack(first, chunk, queries, grad_context, width, parts))
        for first, chunk in bounds
    ]
    far = swap_far(after(far, rows))
    near = swap_near(near, seqs)

    early = after(early, (far[:2], rows))
    rows_out, whole = attend(block_slots, rows[0], [early])
    token_parts = [swap_rows(rows_out)]
    returns = [[swap_pool(after(whole[0], far))]]
    block_slots = after(block_slots, token_parts[0])
    rows_out, (near, *far) = attend(block_slots, rows[1], [near, *far])
    far = swap_far(far)
    token_parts.append(swap_rows(rows_out))
    returns.append([swap_near(after(near, far[:2]), seqs), *far])

    context, grad_queries = unpack(token_parts, firsts, width, queries.shape)
    pool_grads = None
    for first, back in zip(firsts, returns):
        pool_grads = owner_sum(first, send_lists, back, kv_pool.shape, pool_grads)
    return (context, grad_queries, pool_grads)


def solution(mesh):
    in_specs = (
        P("enc", "seq", None),
        P("enc", None, None, "seq"),
        P("enc", None, None),
        P("enc", None, None),
        P("enc", "seq", None),
    )
    out_specs = (P("enc", "seq", None), P("enc", "seq", None), P("enc", None, None, "seq"))
    body = functools.partial(local, mesh.shape["enc"], mesh.shape["seq"])
    return jax.shard_map(body, mesh=mesh, in_specs=in_specs, out_specs=out_specs, check_vma=False)
```

```python
import functools
import math

import jax
import jax.numpy as jnp
from jax import lax
from jax.experimental import pallas as pl
from jax.experimental.pallas import tpu as pltpu
from jax.sharding import PartitionSpec as P

DH = 128
BLOCK = 64
NBLEN = 128
ATTEND_WEIGHT = 24
SHARE = 8
F32 = jnp.float32
BF16 = jnp.bfloat16
LOG2E = 1.4426950408889634
VMEM_BYTES = 40 * 1024 * 1024


def partner(index, step, count):
    if count & (count - 1) == 0:
        return index ^ step
    return (step - index) % count


def exchange(array, axis, step, count):
    pairs = [(i, partner(i, step, count)) for i in range(count)]
    return lax.ppermute(array, axis, pairs)


def across(index, step, count):
    half = count // 2
    there = half + (index + step) % half
    return jnp.where(index < half, there, (index - step) % half)


def swap_near(array, count):
    half = count // 2
    groups = [list(range(half)), list(range(half, count))]
    return lax.all_to_all(
        array, "enc", split_axis=0, concat_axis=0, axis_index_groups=groups, tiled=True
    )


def swap_half(pieces, count):
    half = count // 2
    got = [pieces[0]]
    for step in range(1, half):
        pairs = [(i, i - i % half + partner(i % half, step, half)) for i in range(count)]
        got.append(lax.ppermute(pieces[step], "enc", pairs))
    return got


def swap_rows(pieces):
    count = len(pieces)
    return [pieces[0]] + [exchange(pieces[step], "seq", step, count) for step in range(1, count)]


def swap_pool(array):
    return lax.all_to_all(array, "enc", split_axis=0, concat_axis=0, tiled=True)


def after(array, earlier):
    return lax.optimization_barrier((array, earlier))[0]


def in_hbm(shape):
    return pltpu.HBM(shape, BF16)


def cost(moved, flops=0, exps=0):
    return pl.CostEstimate(flops=flops, bytes_accessed=moved, transcendentals=exps)


PARAMS = pltpu.CompilerParams(vmem_limit_bytes=VMEM_BYTES)
SCALARS = pl.BlockSpec(memory_space=pltpu.SMEM)
ANYWHERE = pl.BlockSpec(memory_space=pl.ANY)
IN_HBM = pl.BlockSpec(memory_space=pltpu.HBM)


def pack_kernel(first, width, q_ref, g_ref, *rest):
    outs, sems = rest[:-1], rest[-1]
    parts, chunk = len(outs), outs[0].shape[-1]
    me = lax.axis_index("seq")
    copies = []
    for step, out in enumerate(outs):
        start = pl.multiple_of(partner(me, step, parts) * width + first, DH)
        for n, ref in enumerate((q_ref, g_ref)):
            source = ref.at[0, :, pl.ds(start, chunk)]
            copies.append(pltpu.make_async_copy(source, out.at[n], sems.at[2 * step + n]))
            copies[-1].start()
    for copy in copies:
        copy.wait()


def pack(first, chunk, queries, grads, width, parts):
    shape = (2, queries.shape[1], chunk)
    return pl.pallas_call(
        functools.partial(pack_kernel, first, width),
        grid=(1,),
        in_specs=[IN_HBM, IN_HBM],
        out_specs=[pl.BlockSpec(shape, lambda i: (0, 0, 0))] * parts,
        out_shape=[in_hbm(shape)] * parts,
        scratch_shapes=[pltpu.SemaphoreType.DMA((2 * parts,))],
        compiler_params=PARAMS,
        cost_estimate=cost(8 * parts * queries.shape[1] * chunk),
        name="pack_rows",
    )(queries, grads)


def unpack_kernel(firsts, width, *refs):
    ins, (ctx_ref, gq_ref, sems) = refs[:-3], refs[-3:]
    parts = len(ins) // len(firsts)
    me = lax.axis_index("seq")
    copies = []
    for n, src in enumerate(ins):
        first, step = firsts[n // parts], n % parts
        start = pl.multiple_of(partner(me, step, parts) * width + first, DH)
        for k, ref in enumerate((ctx_ref, gq_ref)):
            target = ref.at[0, :, pl.ds(start, src.shape[-1])]
            copies.append(pltpu.make_async_copy(src.at[k], target, sems.at[2 * n + k]))
            copies[-1].start()
    for copy in copies:
        copy.wait()


def unpack(pieces, firsts, width, shape):
    flat = [array for piece in pieces for array in piece]
    return pl.pallas_call(
        functools.partial(unpack_kernel, firsts, width),
        grid=(1,),
        in_specs=[pl.BlockSpec(array.shape, lambda i: (0, 0, 0)) for array in flat],
        out_specs=[IN_HBM, IN_HBM],
        out_shape=[in_hbm(shape)] * 2,
        scratch_shapes=[pltpu.SemaphoreType.DMA((2 * len(flat),))],
        compiler_params=PARAMS,
        cost_estimate=cost(8 * shape[1] * shape[2]),
        name="unpack_rows",
    )(*flat)


def kv_shapes(seqs, chunk, form):
    half = seqs // 2
    one = (2, NBLEN, chunk)
    return [[(seqs, *one)], [(half, *one)] + [one] * half, [one] * seqs][form]


def kv_views(refs, seqs, form):
    if form == 0:
        return [(seq, refs[0].at[seq]) for seq in range(seqs)]
    half = seqs // 2
    me = lax.axis_index("enc")
    base = me - me % half
    if form == 1:
        near = [(base + step, refs[0].at[step]) for step in range(half)]
    else:
        near = [(base + partner(me % half, step, half), refs[step]) for step in range(half)]
    return near + [(across(me, step, seqs), refs[step - half]) for step in range(half)]


def pick_kernel(first, form, seqs, lists, pool_ref, *rest):
    outs, held, sems = rest[:-2], rest[-2], rest[-1]
    chunk = held.shape[-1]
    arriving, leaving = [], []
    for n, (seq, out) in enumerate(kv_views(outs, seqs, form)):
        source = pool_ref.at[lists[0, seq, 0], :, :, first : first + chunk]
        arriving.append(pltpu.make_async_copy(source, held.at[n], sems.at[0, n]))
        leaving.append(pltpu.make_async_copy(held.at[n], out, sems.at[1, n]))
        arriving[n].start()
    for n in range(seqs):
        arriving[n].wait()
        leaving[n].start()
    for n in range(seqs):
        leaving[n].wait()


def pick(first, chunk, form, send_lists, kv_pool):
    seqs = send_lists.shape[1]
    shapes = kv_shapes(seqs, chunk, form)
    return pl.pallas_call(
        functools.partial(pick_kernel, first, form, seqs),
        grid=(1,),
        in_specs=[SCALARS, IN_HBM],
        out_specs=[IN_HBM] * len(shapes),
        out_shape=[in_hbm(shape) for shape in shapes],
        scratch_shapes=[
            pltpu.VMEM((seqs, 2, NBLEN, chunk), BF16),
            pltpu.SemaphoreType.DMA((2, seqs)),
        ],
        compiler_params=PARAMS,
        cost_estimate=cost(8 * seqs * NBLEN * chunk),
        name="pick_entries",
    )(send_lists, pltpu.with_memory_space_constraint(kv_pool, pltpu.HBM))


def dot(left, right, left_dim, right_dim):
    return lax.dot_general(
        left, right, (((left_dim,), (right_dim,)), ((), ())), preferred_element_type=F32
    )


def attend_kernel(seqs, parts, forms, pieces, uses, *rest):
    rows_in, rest = rest[:parts], rest[parts:]
    kv_in, rest = rest[: pieces[0]], rest[pieces[0] :]
    rows_out, rest = rest[:parts], rest[parts:]
    kv_out, rest = rest[: pieces[1]], rest[pieces[1] :]
    held, rows, made, sums = rest if forms[0] else (kv_in[0], *rest)
    scale = DH ** (-0.5)
    mine = lax.axis_index("seq")

    if forms[0]:
        for slot, piece in kv_views(kv_in, seqs, forms[0]):
            held[slot] = piece[...]
    for step in range(parts):
        for n in range(2):
            piece = rows_in[step][n].astype(F32)
            rows[partner(mine, step, parts), n] = pltpu.roll(piece, 1, 0)
    rows[parts] = jnp.zeros(rows.shape[1:], F32)
    made[0, :, :BLOCK] = jnp.zeros((2, BLOCK, DH), F32)
    sums[...] = jnp.zeros_like(sums)
    first_row = lax.broadcasted_iota(jnp.int32, (BLOCK, DH), 0) == 0

    def blocks_of(first, qs, gs):
        several = range(len(qs))
        slots = [(uses[0, first + n, 0], uses[0, first + n, 1]) for n in several]
        keys = [jnp.concatenate([held[a, 0], held[b, 0]], axis=0) for a, b in slots]
        values = [jnp.concatenate([held[a, 1], held[b, 1]], axis=0) for a, b in slots]
        scores = [dot(qs[n], keys[n], 1, 1) for n in several]
        grad_probs = [dot(gs[n], values[n], 1, 1) for n in several]
        peaks = [jnp.max(scores[n], axis=1, keepdims=True) for n in several]
        weights = [jnp.exp2((scores[n] - peaks[n]) * (scale * LOG2E)) for n in several]
        shares = [1.0 / jnp.sum(weights[n], axis=1, keepdims=True) for n in several]
        probs = [weights[n] * shares[n] for n in several]
        probs_low = [probs[n].astype(BF16) for n in several]
        inner = [jnp.sum(probs[n] * grad_probs[n], axis=1, keepdims=True) for n in several]
        out = [dot(probs_low[n], values[n], 1, 0) for n in several]
        grad_values = [dot(probs_low[n], gs[n], 0, 0) for n in several]
        grad_scores = [
            (probs[n] * ((grad_probs[n] - inner[n]) * scale)).astype(BF16) for n in several
        ]
        grad_q = [dot(grad_scores[n], keys[n], 1, 0) for n in several]
        grad_keys = [dot(grad_scores[n], qs[n], 0, 0) for n in several]
        for n, (a, b) in enumerate(slots):
            sums[a, 0] += grad_keys[n][:NBLEN]
            sums[b, 0] += grad_keys[n][NBLEN:]
            sums[a, 1] += grad_values[n][:NBLEN]
            sums[b, 1] += grad_values[n][NBLEN:]
        return out, grad_q

    def one_part(part, carry):
        inputs = []
        for n in range(2):
            later = jnp.where(first_row, rows[part, n, :BLOCK], rows[part + 1, n, :BLOCK])
            inputs.append([rows[part, n, BLOCK:].astype(BF16), later.astype(BF16)])
        for n, (even, odd) in enumerate(blocks_of(2 * part, *inputs)):
            made[part, n, BLOCK:] = even
            made[part + 1, n, :BLOCK] = odd
            made[part, n, :1] = odd[:1]
        return carry

    if parts <= 4:
        for part in range(parts):
            one_part(part, 0)
    else:
        lax.fori_loop(0, parts, one_part, 0)

    for step in range(parts):
        for n in range(2):
            piece = made[partner(mine, step, parts), n]
            rows_out[step][n] = pltpu.roll(piece, 2 * BLOCK - 1, 0).astype(BF16)
    for slot, piece in kv_views(kv_out, seqs, forms[1]):
        piece[...] = sums[slot].astype(BF16)


def heads_spec(shape, wide):
    return pl.BlockSpec((*shape[:-1], wide), lambda i, n=len(shape) - 1: (0,) * n + (i,))


def attend(seqs, forms, uses, rows_in, kv_in):
    parts, part_rows = len(rows_in), rows_in[0].shape[1]
    chunk = kv_in[0].shape[-1]
    heads = chunk // DH
    rows_shapes = [array.shape for array in rows_in]
    in_shapes, out_shapes = (kv_shapes(seqs, chunk, form) for form in forms)
    pairs = heads * parts * part_rows * 2 * NBLEN
    held = [pltpu.VMEM((seqs, 2, NBLEN, DH), BF16)] if forms[0] else []
    pieces = (len(in_shapes), len(out_shapes))
    outs = pl.pallas_call(
        functools.partial(attend_kernel, seqs, parts, forms, pieces),
        grid=(heads,),
        in_specs=[SCALARS] + [heads_spec(shape, DH) for shape in rows_shapes + in_shapes],
        out_specs=[heads_spec(shape, DH) for shape in rows_shapes + out_shapes],
        scratch_shapes=held
        + [
            pltpu.VMEM((parts + 1, 2, part_rows, DH), F32),
            pltpu.VMEM((parts + 1, 2, part_rows, DH), F32),
            pltpu.VMEM((seqs, 2, NBLEN, DH), F32),
        ],
        out_shape=[in_hbm(shape) for shape in rows_shapes + out_shapes],
        compiler_params=PARAMS,
        cost_estimate=cost(
            8 * (seqs + parts) * NBLEN * chunk, ATTEND_WEIGHT * 12 * DH * pairs, pairs
        ),
        name="attend_blocks",
    )(uses, *rows_in, *kv_in)
    return outs[:parts], outs[parts:]


def owner_kernel(seqs, form, pieces, lists, *rest):
    out_ref, acc = rest[-2], rest[-1]
    acc[...] = jnp.zeros_like(acc)
    for seq, piece in kv_views(rest[:pieces], seqs, form):
        acc[lists[0, seq, 0]] += piece[...].astype(F32)
    out_ref[...] = acc[...].astype(BF16)


def owner_sum(first, form, send_lists, back, shape, so_far):
    seqs = send_lists.shape[1]
    chunk = back[0].shape[-1]
    wide = math.gcd(math.gcd(first, chunk), 256)
    skip, steps = first // wide, chunk // wide
    extra = [] if so_far is None else [so_far]
    specs = [heads_spec(array.shape, wide) for array in back]
    return pl.pallas_call(
        functools.partial(owner_kernel, seqs, form, len(back)),
        grid=(steps,),
        in_specs=[SCALARS] + specs + [ANYWHERE] * len(extra),
        out_specs=pl.BlockSpec(
            (shape[0], 2, NBLEN, wide), lambda i: (0, 0, 0, skip + i)
        ),
        scratch_shapes=[pltpu.VMEM((shape[0], 2, NBLEN, wide), F32)],
        out_shape=in_hbm(shape),
        input_output_aliases={len(back) + 1: 0} if extra else {},
        compiler_params=PARAMS,
        cost_estimate=cost(4 * (seqs + shape[0]) * NBLEN * chunk, 2 * seqs * NBLEN * chunk),
        name="owner_sum",
    )(send_lists, *back, *extra)


def swap_far(pieces, depth):
    half = len(pieces)
    got = []
    for step, piece in enumerate(pieces):
        there = [half + (i + step) % half for i in range(half)]
        pairs = list(enumerate(there)) + [(peer, i) for i, peer in enumerate(there)]
        if step >= depth:
            piece = after(piece, got[step - depth])
        got.append(lax.ppermute(piece, "enc", pairs))
    return got


def local(seqs, parts, queries, kv_pool, send_lists, block_slots, grad_context):
    width = kv_pool.shape[-1]
    cut = (SHARE * width // DH // 16) * DH
    bounds = [(0, cut), (cut, width - cut)]
    firsts = [first for first, _ in bounds]

    picked = pick(*bounds[0], 0, send_lists, kv_pool)
    send_lists, queries = after((send_lists, queries), picked[0])
    early = swap_pool(picked[0])
    near, *far = pick(*bounds[1], 1, send_lists, kv_pool)
    queries = after(queries, near)
    rows = [
        swap_rows(pack(first, chunk, queries, grad_context, width, parts))
        for first, chunk in bounds
    ]
    far = swap_far(after(far, rows), seqs)
    near = swap_near(near, seqs)

    early = after(early, far[0])
    rows_out, whole = attend(seqs, (0, 0), block_slots, rows[0], [early])
    token_parts = [swap_rows(rows_out)]
    returns = [[swap_pool(after(whole[0], far))]]
    block_slots = after(block_slots, token_parts[0])
    rows_out, back = attend(seqs, (1, 2), block_slots, rows[1], [near, *far])
    near, far = back[: seqs // 2], back[seqs // 2 :]
    far = swap_far(far, 2)
    token_parts.append(swap_rows(rows_out))
    near = swap_half(after(near, token_parts[1]), seqs)
    returns.append([*near, *far])

    context, grad_queries = unpack(token_parts, firsts, width, queries.shape)
    pool_grads = None
    for first, form, back in zip(firsts, (0, 2), returns):
        pool_grads = owner_sum(first, form, send_lists, back, kv_pool.shape, pool_grads)
    return (context, grad_queries, pool_grads)


def solution(mesh):
    in_specs = (
        P("enc", "seq", None),
        P("enc", None, None, "seq"),
        P("enc", None, None),
        P("enc", None, None),
        P("enc", "seq", None),
    )
    out_specs = (P("enc", "seq", None), P("enc", "seq", None), P("enc", None, None, "seq"))
    body = functools.partial(local, mesh.shape["enc"], mesh.shape["seq"])
    return jax.shard_map(body, mesh=mesh, in_specs=in_specs, out_specs=out_specs, check_vma=False)
```

```python
import functools
import math

import jax
import jax.numpy as jnp
from jax import lax
from jax.experimental import pallas as pl
from jax.experimental.pallas import tpu as pltpu
from jax.sharding import PartitionSpec as P

DH = 128
BLOCK = 64
NBLEN = 128
ATTEND_WEIGHT = 24
SHARE = 8
READS = 3
F32 = jnp.float32
BF16 = jnp.bfloat16
LOG2E = 1.4426950408889634
VMEM_BYTES = 40 * 1024 * 1024


def partner(index, step, count):
    if count & (count - 1) == 0:
        return index ^ step
    return (step - index) % count


def exchange(array, axis, step, count):
    pairs = [(i, partner(i, step, count)) for i in range(count)]
    return lax.ppermute(array, axis, pairs)


def across(index, step, count):
    half = count // 2
    there = half + (index + step) % half
    return jnp.where(index < half, there, (index - step) % half)


def swap_half(pieces, count):
    half = count // 2
    got = [pieces[0]]
    for step in range(1, half):
        pairs = [(i, i - i % half + partner(i % half, step, half)) for i in range(count)]
        got.append(lax.ppermute(pieces[step], "enc", pairs))
    return got


def swap_rows(pieces):
    count = len(pieces)
    return [pieces[0]] + [exchange(pieces[step], "seq", step, count) for step in range(1, count)]


def swap_pool(array):
    return lax.all_to_all(array, "enc", split_axis=0, concat_axis=0, tiled=True)


def after(array, earlier):
    return lax.optimization_barrier((array, earlier))[0]


def in_hbm(shape):
    return pltpu.HBM(shape, BF16)


def cost(moved, flops=0, exps=0):
    return pl.CostEstimate(flops=flops, bytes_accessed=moved, transcendentals=exps)


PARAMS = pltpu.CompilerParams(vmem_limit_bytes=VMEM_BYTES)
SCALARS = pl.BlockSpec(memory_space=pltpu.SMEM)
ANYWHERE = pl.BlockSpec(memory_space=pl.ANY)
IN_HBM = pl.BlockSpec(memory_space=pltpu.HBM)


def pack_kernel(first, width, q_ref, g_ref, *rest):
    outs, sems = rest[:-1], rest[-1]
    parts, chunk = len(outs), outs[0].shape[-1]
    me = lax.axis_index("seq")
    copies = []
    for step, out in enumerate(outs):
        start = pl.multiple_of(partner(me, step, parts) * width + first, DH)
        for n, ref in enumerate((q_ref, g_ref)):
            source = ref.at[0, :, pl.ds(start, chunk)]
            copies.append(pltpu.make_async_copy(source, out.at[n], sems.at[2 * step + n]))
            copies[-1].start()
    for copy in copies:
        copy.wait()


def pack(first, chunk, queries, grads, width, parts):
    shape = (2, queries.shape[1], chunk)
    return pl.pallas_call(
        functools.partial(pack_kernel, first, width),
        grid=(1,),
        in_specs=[IN_HBM, IN_HBM],
        out_specs=[pl.BlockSpec(shape, lambda i: (0, 0, 0))] * parts,
        out_shape=[in_hbm(shape)] * parts,
        scratch_shapes=[pltpu.SemaphoreType.DMA((2 * parts,))],
        compiler_params=PARAMS,
        cost_estimate=cost(8 * parts * queries.shape[1] * chunk),
        name="pack_rows",
    )(queries, grads)


def unpack_kernel(firsts, width, *refs):
    ins, (ctx_ref, gq_ref, sems) = refs[:-3], refs[-3:]
    parts = len(ins) // len(firsts)
    me = lax.axis_index("seq")
    copies = []
    for n, src in enumerate(ins):
        first, step = firsts[n // parts], n % parts
        start = pl.multiple_of(partner(me, step, parts) * width + first, DH)
        for k, ref in enumerate((ctx_ref, gq_ref)):
            target = ref.at[0, :, pl.ds(start, src.shape[-1])]
            copies.append(pltpu.make_async_copy(src.at[k], target, sems.at[2 * n + k]))
            copies[-1].start()
    for copy in copies:
        copy.wait()


def unpack(pieces, firsts, width, shape):
    flat = [array for piece in pieces for array in piece]
    return pl.pallas_call(
        functools.partial(unpack_kernel, firsts, width),
        grid=(1,),
        in_specs=[pl.BlockSpec(array.shape, lambda i: (0, 0, 0)) for array in flat],
        out_specs=[IN_HBM, IN_HBM],
        out_shape=[in_hbm(shape)] * 2,
        scratch_shapes=[pltpu.SemaphoreType.DMA((2 * len(flat),))],
        compiler_params=PARAMS,
        cost_estimate=cost(8 * shape[1] * shape[2]),
        name="unpack_rows",
    )(*flat)


def kv_shapes(seqs, chunk, form):
    one = (2, NBLEN, chunk)
    return [one] * seqs if form else [(seqs, *one)]


def kv_views(refs, seqs, form):
    if form == 0:
        return [(seq, refs[0].at[seq]) for seq in range(seqs)]
    half = seqs // 2
    me = lax.axis_index("enc")
    base = me - me % half
    near = [(base + partner(me % half, step, half), refs[step]) for step in range(half)]
    return near + [(across(me, step, seqs), refs[step - half]) for step in range(half)]


def pick_kernel(first, form, seqs, lists, pool_ref, *rest):
    outs, held, sems = rest[:-2], rest[-2], rest[-1]
    chunk = held.shape[-1]
    arriving, leaving = [], []
    for n, (seq, out) in enumerate(kv_views(outs, seqs, form)):
        source = pool_ref.at[lists[0, seq, 0], :, :, first : first + chunk]
        arriving.append(pltpu.make_async_copy(source, held.at[n], sems.at[0, n]))
        leaving.append(pltpu.make_async_copy(held.at[n], out, sems.at[1, n]))
    for n in range(READS):
        arriving[n].start()
    for n in range(seqs):
        arriving[n].wait()
        leaving[n].start()
        if n + READS < seqs:
            arriving[n + READS].start()
    for n in range(seqs):
        leaving[n].wait()


def pick(first, chunk, form, send_lists, kv_pool):
    seqs = send_lists.shape[1]
    shapes = kv_shapes(seqs, chunk, form)
    return pl.pallas_call(
        functools.partial(pick_kernel, first, form, seqs),
        grid=(1,),
        in_specs=[SCALARS, IN_HBM],
        out_specs=[IN_HBM] * len(shapes),
        out_shape=[in_hbm(shape) for shape in shapes],
        scratch_shapes=[
            pltpu.VMEM((seqs, 2, NBLEN, chunk), BF16),
            pltpu.SemaphoreType.DMA((2, seqs)),
        ],
        compiler_params=PARAMS,
        cost_estimate=cost(8 * seqs * NBLEN * chunk),
        name="pick_entries",
    )(send_lists, pltpu.with_memory_space_constraint(kv_pool, pltpu.HBM))


def dot(left, right, left_dim, right_dim):
    return lax.dot_general(
        left, right, (((left_dim,), (right_dim,)), ((), ())), preferred_element_type=F32
    )


def attend_kernel(seqs, parts, forms, pieces, uses, *rest):
    rows_in, rest = rest[:parts], rest[parts:]
    kv_in, rest = rest[: pieces[0]], rest[pieces[0] :]
    rows_out, rest = rest[:parts], rest[parts:]
    kv_out, rest = rest[: pieces[1]], rest[pieces[1] :]
    held, rows, made, sums = rest if forms[0] else (kv_in[0], *rest)
    scale = DH ** (-0.5)
    mine = lax.axis_index("seq")

    if forms[0]:
        for slot, piece in kv_views(kv_in, seqs, forms[0]):
            held[slot] = piece[...]
    for step in range(parts):
        for n in range(2):
            piece = rows_in[step][n].astype(F32)
            rows[partner(mine, step, parts), n] = pltpu.roll(piece, 1, 0)
    rows[parts] = jnp.zeros(rows.shape[1:], F32)
    made[0, :, :BLOCK] = jnp.zeros((2, BLOCK, DH), F32)
    sums[...] = jnp.zeros_like(sums)
    first_row = lax.broadcasted_iota(jnp.int32, (BLOCK, DH), 0) == 0

    def blocks_of(first, qs, gs):
        several = range(len(qs))
        slots = [(uses[0, first + n, 0], uses[0, first + n, 1]) for n in several]
        keys = [jnp.concatenate([held[a, 0], held[b, 0]], axis=0) for a, b in slots]
        values = [jnp.concatenate([held[a, 1], held[b, 1]], axis=0) for a, b in slots]
        scores = [dot(qs[n], keys[n], 1, 1) for n in several]
        grad_probs = [dot(gs[n], values[n], 1, 1) for n in several]
        peaks = [jnp.max(scores[n], axis=1, keepdims=True) for n in several]
        weights = [jnp.exp2((scores[n] - peaks[n]) * (scale * LOG2E)) for n in several]
        shares = [1.0 / jnp.sum(weights[n], axis=1, keepdims=True) for n in several]
        probs = [weights[n] * shares[n] for n in several]
        probs_low = [probs[n].astype(BF16) for n in several]
        inner = [jnp.sum(probs[n] * grad_probs[n], axis=1, keepdims=True) for n in several]
        out = [dot(probs_low[n], values[n], 1, 0) for n in several]
        grad_values = [dot(probs_low[n], gs[n], 0, 0) for n in several]
        grad_scores = [
            (probs[n] * ((grad_probs[n] - inner[n]) * scale)).astype(BF16) for n in several
        ]
        grad_q = [dot(grad_scores[n], keys[n], 1, 0) for n in several]
        grad_keys = [dot(grad_scores[n], qs[n], 0, 0) for n in several]
        for n, (a, b) in enumerate(slots):
            sums[a, 0] += grad_keys[n][:NBLEN]
            sums[b, 0] += grad_keys[n][NBLEN:]
            sums[a, 1] += grad_values[n][:NBLEN]
            sums[b, 1] += grad_values[n][NBLEN:]
        return out, grad_q

    def one_part(part, carry):
        inputs = []
        for n in range(2):
            later = jnp.where(first_row, rows[part, n, :BLOCK], rows[part + 1, n, :BLOCK])
            inputs.append([rows[part, n, BLOCK:].astype(BF16), later.astype(BF16)])
        for n, (even, odd) in enumerate(blocks_of(2 * part, *inputs)):
            made[part, n, BLOCK:] = even
            made[part + 1, n, :BLOCK] = odd
            made[part, n, :1] = odd[:1]
        return carry

    if parts <= 4:
        for part in range(parts):
            one_part(part, 0)
    else:
        lax.fori_loop(0, parts, one_part, 0)

    for step in range(parts):
        for n in range(2):
            piece = made[partner(mine, step, parts), n]
            rows_out[step][n] = pltpu.roll(piece, 2 * BLOCK - 1, 0).astype(BF16)
    for slot, piece in kv_views(kv_out, seqs, forms[1]):
        piece[...] = sums[slot].astype(BF16)


def heads_spec(shape, wide):
    return pl.BlockSpec((*shape[:-1], wide), lambda i, n=len(shape) - 1: (0,) * n + (i,))


def attend(seqs, forms, uses, rows_in, kv_in):
    parts, part_rows = len(rows_in), rows_in[0].shape[1]
    chunk = kv_in[0].shape[-1]
    heads = chunk // DH
    rows_shapes = [array.shape for array in rows_in]
    in_shapes, out_shapes = (kv_shapes(seqs, chunk, form) for form in forms)
    pairs = heads * parts * part_rows * 2 * NBLEN
    held = [pltpu.VMEM((seqs, 2, NBLEN, DH), BF16)] if forms[0] else []
    pieces = (len(in_shapes), len(out_shapes))
    outs = pl.pallas_call(
        functools.partial(attend_kernel, seqs, parts, forms, pieces),
        grid=(heads,),
        in_specs=[SCALARS] + [heads_spec(shape, DH) for shape in rows_shapes + in_shapes],
        out_specs=[heads_spec(shape, DH) for shape in rows_shapes + out_shapes],
        scratch_shapes=held
        + [
            pltpu.VMEM((parts + 1, 2, part_rows, DH), F32),
            pltpu.VMEM((parts + 1, 2, part_rows, DH), F32),
            pltpu.VMEM((seqs, 2, NBLEN, DH), F32),
        ],
        out_shape=[in_hbm(shape) for shape in rows_shapes + out_shapes],
        compiler_params=PARAMS,
        cost_estimate=cost(
            8 * (seqs + parts) * NBLEN * chunk, ATTEND_WEIGHT * 12 * DH * pairs, pairs
        ),
        name="attend_blocks",
    )(uses, *rows_in, *kv_in)
    return outs[:parts], outs[parts:]


def owner_kernel(seqs, form, pieces, lists, *rest):
    out_ref, acc = rest[-2], rest[-1]
    acc[...] = jnp.zeros_like(acc)
    for seq, piece in kv_views(rest[:pieces], seqs, form):
        acc[lists[0, seq, 0]] += piece[...].astype(F32)
    out_ref[...] = acc[...].astype(BF16)


def owner_sum(first, form, send_lists, back, shape, so_far):
    seqs = send_lists.shape[1]
    chunk = back[0].shape[-1]
    wide = math.gcd(math.gcd(first, chunk), 256)
    skip, steps = first // wide, chunk // wide
    extra = [] if so_far is None else [so_far]
    specs = [heads_spec(array.shape, wide) for array in back]
    return pl.pallas_call(
        functools.partial(owner_kernel, seqs, form, len(back)),
        grid=(steps,),
        in_specs=[SCALARS] + specs + [ANYWHERE] * len(extra),
        out_specs=pl.BlockSpec(
            (shape[0], 2, NBLEN, wide), lambda i: (0, 0, 0, skip + i)
        ),
        scratch_shapes=[pltpu.VMEM((shape[0], 2, NBLEN, wide), F32)],
        out_shape=in_hbm(shape),
        input_output_aliases={len(back) + 1: 0} if extra else {},
        compiler_params=PARAMS,
        cost_estimate=cost(4 * (seqs + shape[0]) * NBLEN * chunk, 2 * seqs * NBLEN * chunk),
        name="owner_sum",
    )(send_lists, *back, *extra)


def swap_far(pieces, depth):
    half = len(pieces)
    got = []
    for step, piece in enumerate(pieces):
        there = [half + (i + step) % half for i in range(half)]
        pairs = list(enumerate(there)) + [(peer, i) for i, peer in enumerate(there)]
        if step >= depth:
            piece = after(piece, got[step - depth])
        got.append(lax.ppermute(piece, "enc", pairs))
    return got


def local(seqs, parts, queries, kv_pool, send_lists, block_slots, grad_context):
    width = kv_pool.shape[-1]
    cut = (SHARE * width // DH // 16) * DH
    bounds = [(0, cut), (cut, width - cut)]
    firsts = [first for first, _ in bounds]

    picked = pick(*bounds[0], 0, send_lists, kv_pool)
    send_lists, queries = after((send_lists, queries), picked[0])
    early = swap_pool(picked[0])
    picked = pick(*bounds[1], 1, send_lists, kv_pool)
    near, far = picked[: seqs // 2], picked[seqs // 2 :]
    queries = after(queries, near[0])
    rows = [
        swap_rows(pack(first, chunk, queries, grad_context, width, parts))
        for first, chunk in bounds
    ]
    near = swap_half(after(near, rows), seqs)
    far = swap_far(after(far, near), seqs)

    early = after(early, far[0])
    rows_out, whole = attend(seqs, (0, 0), block_slots, rows[0], [early])
    token_parts = [swap_rows(rows_out)]
    returns = [[swap_pool(after(whole[0], far))]]
    block_slots = after(block_slots, token_parts[0])
    rows_out, back = attend(seqs, (1, 1), block_slots, rows[1], [*near, *far])
    near, far = back[: seqs // 2], back[seqs // 2 :]
    far = swap_far(far, 2)
    token_parts.append(swap_rows(rows_out))
    near = swap_half(after(near, token_parts[1]), seqs)
    returns.append([*near, *far])

    context, grad_queries = unpack(token_parts, firsts, width, queries.shape)
    pool_grads = None
    for first, form, back in zip(firsts, (0, 1), returns):
        pool_grads = owner_sum(first, form, send_lists, back, kv_pool.shape, pool_grads)
    return (context, grad_queries, pool_grads)


def solution(mesh):
    in_specs = (
        P("enc", "seq", None),
        P("enc", None, None, "seq"),
        P("enc", None, None),
        P("enc", None, None),
        P("enc", "seq", None),
    )
    out_specs = (P("enc", "seq", None), P("enc", "seq", None), P("enc", None, None, "seq"))
    body = functools.partial(local, mesh.shape["enc"], mesh.shape["seq"])
    return jax.shard_map(body, mesh=mesh, in_specs=in_specs, out_specs=out_specs, check_vma=False)
```

```python
import functools
import math

import jax
import jax.numpy as jnp
from jax import lax
from jax.experimental import pallas as pl
from jax.experimental.pallas import tpu as pltpu
from jax.sharding import PartitionSpec as P

DH = 128
BLOCK = 64
NBLEN = 128
ATTEND_WEIGHT = 24
SHARE = 8
F32 = jnp.float32
BF16 = jnp.bfloat16
LOG2E = 1.4426950408889634
VMEM_BYTES = 40 * 1024 * 1024


def partner(index, step, count):
    if count & (count - 1) == 0:
        return index ^ step
    return (step - index) % count


def exchange(array, axis, step, count):
    pairs = [(i, partner(i, step, count)) for i in range(count)]
    return lax.ppermute(array, axis, pairs)


def across(index, step, count):
    half = count // 2
    there = half + (index + step) % half
    return jnp.where(index < half, there, (index - step) % half)


def swap_near(array, count):
    half = count // 2
    groups = [list(range(half)), list(range(half, count))]
    return lax.all_to_all(
        array, "enc", split_axis=0, concat_axis=0, axis_index_groups=groups, tiled=True
    )


def swap_half(pieces, count):
    half = count // 2
    got = [pieces[0]]
    for step in range(1, half):
        pairs = [(i, i - i % half + partner(i % half, step, half)) for i in range(count)]
        got.append(lax.ppermute(pieces[step], "enc", pairs))
    return got


def swap_rows(pieces):
    count = len(pieces)
    return [pieces[0]] + [exchange(pieces[step], "seq", step, count) for step in range(1, count)]


def swap_pool(array):
    return lax.all_to_all(array, "enc", split_axis=0, concat_axis=0, tiled=True)


def after(array, earlier):
    return lax.optimization_barrier((array, earlier))[0]


def in_hbm(shape):
    return pltpu.HBM(shape, BF16)


def cost(moved, flops=0, exps=0):
    return pl.CostEstimate(flops=flops, bytes_accessed=moved, transcendentals=exps)


PARAMS = pltpu.CompilerParams(vmem_limit_bytes=VMEM_BYTES)
SCALARS = pl.BlockSpec(memory_space=pltpu.SMEM)
ANYWHERE = pl.BlockSpec(memory_space=pl.ANY)
IN_HBM = pl.BlockSpec(memory_space=pltpu.HBM)


def pack_kernel(first, width, q_ref, g_ref, *rest):
    outs, sems = rest[:-1], rest[-1]
    parts, chunk = len(outs), outs[0].shape[-1]
    me = lax.axis_index("seq")
    copies = []
    for step, out in enumerate(outs):
        start = pl.multiple_of(partner(me, step, parts) * width + first, DH)
        for n, ref in enumerate((q_ref, g_ref)):
            source = ref.at[0, :, pl.ds(start, chunk)]
            copies.append(pltpu.make_async_copy(source, out.at[n], sems.at[2 * step + n]))
            copies[-1].start()
    for copy in copies:
        copy.wait()


def pack(first, chunk, queries, grads, width, parts):
    shape = (2, queries.shape[1], chunk)
    return pl.pallas_call(
        functools.partial(pack_kernel, first, width),
        grid=(1,),
        in_specs=[IN_HBM, IN_HBM],
        out_specs=[pl.BlockSpec(shape, lambda i: (0, 0, 0))] * parts,
        out_shape=[in_hbm(shape)] * parts,
        scratch_shapes=[pltpu.SemaphoreType.DMA((2 * parts,))],
        compiler_params=PARAMS,
        cost_estimate=cost(8 * parts * queries.shape[1] * chunk),
        name="pack_rows",
    )(queries, grads)


def unpack_kernel(firsts, width, *refs):
    ins, (ctx_ref, gq_ref, sems) = refs[:-3], refs[-3:]
    parts = len(ins) // len(firsts)
    me = lax.axis_index("seq")
    copies = []
    for n, src in enumerate(ins):
        first, step = firsts[n // parts], n % parts
        start = pl.multiple_of(partner(me, step, parts) * width + first, DH)
        for k, ref in enumerate((ctx_ref, gq_ref)):
            target = ref.at[0, :, pl.ds(start, src.shape[-1])]
            copies.append(pltpu.make_async_copy(src.at[k], target, sems.at[2 * n + k]))
            copies[-1].start()
    for copy in copies:
        copy.wait()


def unpack(pieces, firsts, width, shape):
    flat = [array for piece in pieces for array in piece]
    return pl.pallas_call(
        functools.partial(unpack_kernel, firsts, width),
        grid=(1,),
        in_specs=[pl.BlockSpec(array.shape, lambda i: (0, 0, 0)) for array in flat],
        out_specs=[IN_HBM, IN_HBM],
        out_shape=[in_hbm(shape)] * 2,
        scratch_shapes=[pltpu.SemaphoreType.DMA((2 * len(flat),))],
        compiler_params=PARAMS,
        cost_estimate=cost(8 * shape[1] * shape[2]),
        name="unpack_rows",
    )(*flat)


def kv_shapes(seqs, chunk, form):
    half = seqs // 2
    one = (2, NBLEN, chunk)
    return [[(seqs, *one)], [(half, *one)] + [one] * half, [one] * seqs][form]


def kv_views(refs, seqs, form):
    if form == 0:
        return [(seq, refs[0].at[seq]) for seq in range(seqs)]
    half = seqs // 2
    me = lax.axis_index("enc")
    base = me - me % half
    if form == 1:
        near = [(base + step, refs[0].at[step]) for step in range(half)]
    else:
        near = [(base + partner(me % half, step, half), refs[step]) for step in range(half)]
    return near + [(across(me, step, seqs), refs[step - half]) for step in range(half)]


def pick_kernel(first, form, seqs, lists, pool_ref, *rest):
    outs, held, sems = rest[:-2], rest[-2], rest[-1]
    chunk = held.shape[-1]
    arriving, leaving = [], []
    for n, (seq, out) in enumerate(kv_views(outs, seqs, form)):
        entry = lists[0, seq, 0]
        for k in range(2):
            source = pool_ref.at[entry, k, :, first : first + chunk]
            arriving.append(pltpu.make_async_copy(source, held.at[n, k], sems.at[0, n, k]))
            leaving.append(pltpu.make_async_copy(held.at[n, k], out.at[k], sems.at[1, n, k]))
            arriving[-1].start()
    for arrival, departure in zip(arriving, leaving):
        arrival.wait()
        departure.start()
    for departure in leaving:
        departure.wait()


def pick(first, chunk, form, send_lists, kv_pool):
    seqs = send_lists.shape[1]
    shapes = kv_shapes(seqs, chunk, form)
    return pl.pallas_call(
        functools.partial(pick_kernel, first, form, seqs),
        grid=(1,),
        in_specs=[SCALARS, IN_HBM],
        out_specs=[IN_HBM] * len(shapes),
        out_shape=[in_hbm(shape) for shape in shapes],
        scratch_shapes=[
            pltpu.VMEM((seqs, 2, NBLEN, chunk), BF16),
            pltpu.SemaphoreType.DMA((2, seqs, 2)),
        ],
        compiler_params=PARAMS,
        cost_estimate=cost(8 * seqs * NBLEN * chunk),
        name="pick_entries",
    )(send_lists, pltpu.with_memory_space_constraint(kv_pool, pltpu.HBM))


def dot(left, right, left_dim, right_dim):
    return lax.dot_general(
        left, right, (((left_dim,), (right_dim,)), ((), ())), preferred_element_type=F32
    )


def attend_kernel(seqs, parts, forms, pieces, uses, *rest):
    rows_in, rest = rest[:parts], rest[parts:]
    kv_in, rest = rest[: pieces[0]], rest[pieces[0] :]
    rows_out, rest = rest[:parts], rest[parts:]
    kv_out, rest = rest[: pieces[1]], rest[pieces[1] :]
    held, rows, made, sums = rest if forms[0] else (kv_in[0], *rest)
    scale = DH ** (-0.5)
    mine = lax.axis_index("seq")

    if forms[0]:
        for slot, piece in kv_views(kv_in, seqs, forms[0]):
            held[slot] = piece[...]
    for step in range(parts):
        for n in range(2):
            piece = rows_in[step][n].astype(F32)
            rows[partner(mine, step, parts), n] = pltpu.roll(piece, 1, 0)
    rows[parts] = jnp.zeros(rows.shape[1:], F32)
    made[0, :, :BLOCK] = jnp.zeros((2, BLOCK, DH), F32)
    sums[...] = jnp.zeros_like(sums)
    first_row = lax.broadcasted_iota(jnp.int32, (BLOCK, DH), 0) == 0

    def blocks_of(first, qs, gs):
        several = range(len(qs))
        slots = [(uses[0, first + n, 0], uses[0, first + n, 1]) for n in several]
        keys = [jnp.concatenate([held[a, 0], held[b, 0]], axis=0) for a, b in slots]
        values = [jnp.concatenate([held[a, 1], held[b, 1]], axis=0) for a, b in slots]
        scores = [dot(qs[n], keys[n], 1, 1) for n in several]
        grad_probs = [dot(gs[n], values[n], 1, 1) for n in several]
        peaks = [jnp.max(scores[n], axis=1, keepdims=True) for n in several]
        weights = [jnp.exp2((scores[n] - peaks[n]) * (scale * LOG2E)) for n in several]
        shares = [1.0 / jnp.sum(weights[n], axis=1, keepdims=True) for n in several]
        probs = [weights[n] * shares[n] for n in several]
        probs_low = [probs[n].astype(BF16) for n in several]
        inner = [jnp.sum(probs[n] * grad_probs[n], axis=1, keepdims=True) for n in several]
        out = [dot(probs_low[n], values[n], 1, 0) for n in several]
        grad_values = [dot(probs_low[n], gs[n], 0, 0) for n in several]
        grad_scores = [
            (probs[n] * ((grad_probs[n] - inner[n]) * scale)).astype(BF16) for n in several
        ]
        grad_q = [dot(grad_scores[n], keys[n], 1, 0) for n in several]
        grad_keys = [dot(grad_scores[n], qs[n], 0, 0) for n in several]
        for n, (a, b) in enumerate(slots):
            sums[a, 0] += grad_keys[n][:NBLEN]
            sums[b, 0] += grad_keys[n][NBLEN:]
            sums[a, 1] += grad_values[n][:NBLEN]
            sums[b, 1] += grad_values[n][NBLEN:]
        return out, grad_q

    def one_part(part, carry):
        inputs = []
        for n in range(2):
            later = jnp.where(first_row, rows[part, n, :BLOCK], rows[part + 1, n, :BLOCK])
            inputs.append([rows[part, n, BLOCK:].astype(BF16), later.astype(BF16)])
        for n, (even, odd) in enumerate(blocks_of(2 * part, *inputs)):
            made[part, n, BLOCK:] = even
            made[part + 1, n, :BLOCK] = odd
            made[part, n, :1] = odd[:1]
        return carry

    if parts <= 4:
        for part in range(parts):
            one_part(part, 0)
    else:
        lax.fori_loop(0, parts, one_part, 0)

    for step in range(parts):
        for n in range(2):
            piece = made[partner(mine, step, parts), n]
            rows_out[step][n] = pltpu.roll(piece, 2 * BLOCK - 1, 0).astype(BF16)
    for slot, piece in kv_views(kv_out, seqs, forms[1]):
        piece[...] = sums[slot].astype(BF16)


def heads_spec(shape, wide):
    return pl.BlockSpec((*shape[:-1], wide), lambda i, n=len(shape) - 1: (0,) * n + (i,))


def attend(seqs, forms, uses, rows_in, kv_in):
    parts, part_rows = len(rows_in), rows_in[0].shape[1]
    chunk = kv_in[0].shape[-1]
    heads = chunk // DH
    rows_shapes = [array.shape for array in rows_in]
    in_shapes, out_shapes = (kv_shapes(seqs, chunk, form) for form in forms)
    pairs = heads * parts * part_rows * 2 * NBLEN
    held = [pltpu.VMEM((seqs, 2, NBLEN, DH), BF16)] if forms[0] else []
    pieces = (len(in_shapes), len(out_shapes))
    outs = pl.pallas_call(
        functools.partial(attend_kernel, seqs, parts, forms, pieces),
        grid=(heads,),
        in_specs=[SCALARS] + [heads_spec(shape, DH) for shape in rows_shapes + in_shapes],
        out_specs=[heads_spec(shape, DH) for shape in rows_shapes + out_shapes],
        scratch_shapes=held
        + [
            pltpu.VMEM((parts + 1, 2, part_rows, DH), F32),
            pltpu.VMEM((parts + 1, 2, part_rows, DH), F32),
            pltpu.VMEM((seqs, 2, NBLEN, DH), F32),
        ],
        out_shape=[in_hbm(shape) for shape in rows_shapes + out_shapes],
        compiler_params=PARAMS,
        cost_estimate=cost(
            8 * (seqs + parts) * NBLEN * chunk, ATTEND_WEIGHT * 12 * DH * pairs, pairs
        ),
        name="attend_blocks",
    )(uses, *rows_in, *kv_in)
    return outs[:parts], outs[parts:]


def owner_kernel(seqs, form, pieces, lists, *rest):
    out_ref, acc = rest[-2], rest[-1]
    acc[...] = jnp.zeros_like(acc)
    for seq, piece in kv_views(rest[:pieces], seqs, form):
        acc[lists[0, seq, 0]] += piece[...].astype(F32)
    out_ref[...] = acc[...].astype(BF16)


def owner_sum(first, form, send_lists, back, shape, so_far):
    seqs = send_lists.shape[1]
    chunk = back[0].shape[-1]
    wide = math.gcd(math.gcd(first, chunk), 256)
    skip, steps = first // wide, chunk // wide
    extra = [] if so_far is None else [so_far]
    specs = [heads_spec(array.shape, wide) for array in back]
    return pl.pallas_call(
        functools.partial(owner_kernel, seqs, form, len(back)),
        grid=(steps,),
        in_specs=[SCALARS] + specs + [ANYWHERE] * len(extra),
        out_specs=pl.BlockSpec(
            (shape[0], 2, NBLEN, wide), lambda i: (0, 0, 0, skip + i)
        ),
        scratch_shapes=[pltpu.VMEM((shape[0], 2, NBLEN, wide), F32)],
        out_shape=in_hbm(shape),
        input_output_aliases={len(back) + 1: 0} if extra else {},
        compiler_params=PARAMS,
        cost_estimate=cost(4 * (seqs + shape[0]) * NBLEN * chunk, 2 * seqs * NBLEN * chunk),
        name="owner_sum",
    )(send_lists, *back, *extra)


def swap_far(pieces, depth):
    half = len(pieces)
    got = []
    for step, piece in enumerate(pieces):
        there = [half + (i + step) % half for i in range(half)]
        pairs = list(enumerate(there)) + [(peer, i) for i, peer in enumerate(there)]
        if step >= depth:
            piece = after(piece, got[step - depth])
        got.append(lax.ppermute(piece, "enc", pairs))
    return got


def local(seqs, parts, queries, kv_pool, send_lists, block_slots, grad_context):
    width = kv_pool.shape[-1]
    cut = (SHARE * width // DH // 16) * DH
    bounds = [(0, cut), (cut, width - cut)]
    firsts = [first for first, _ in bounds]

    picked = pick(*bounds[0], 0, send_lists, kv_pool)
    send_lists, queries = after((send_lists, queries), picked[0])
    early = swap_pool(picked[0])
    near, *far = pick(*bounds[1], 1, send_lists, kv_pool)
    queries = after(queries, near)
    rows = [
        swap_rows(pack(first, chunk, queries, grad_context, width, parts))
        for first, chunk in bounds
    ]
    far = after(far, rows)
    far = swap_far(far[:1] + after(far[1:], early), seqs)
    near = swap_near(near, seqs)

    early = after(early, far[0])
    rows_out, whole = attend(seqs, (0, 0), block_slots, rows[0], [early])
    token_parts = [swap_rows(rows_out)]
    returns = [[swap_pool(after(whole[0], far))]]
    block_slots = after(block_slots, token_parts[0])
    rows_out, back = attend(seqs, (1, 2), block_slots, rows[1], [near, *far])
    near, far = back[: seqs // 2], back[seqs // 2 :]
    far = swap_far(far, 2)
    token_parts.append(swap_rows(rows_out))
    near = swap_half(after(near, token_parts[1]), seqs)
    returns.append([*near, *far])

    context, grad_queries = unpack(token_parts, firsts, width, queries.shape)
    pool_grads = None
    for first, form, back in zip(firsts, (0, 2), returns):
        pool_grads = owner_sum(first, form, send_lists, back, kv_pool.shape, pool_grads)
    return (context, grad_queries, pool_grads)


def solution(mesh):
    in_specs = (
        P("enc", "seq", None),
        P("enc", None, None, "seq"),
        P("enc", None, None),
        P("enc", None, None),
        P("enc", "seq", None),
    )
    out_specs = (P("enc", "seq", None), P("enc", "seq", None), P("enc", None, None, "seq"))
    body = functools.partial(local, mesh.shape["enc"], mesh.shape["seq"])
    return jax.shard_map(body, mesh=mesh, in_specs=in_specs, out_specs=out_specs, check_vma=False)
```

```python
import functools
import math

import jax
import jax.numpy as jnp
from jax import lax
from jax.experimental import pallas as pl
from jax.experimental.pallas import tpu as pltpu
from jax.sharding import PartitionSpec as P

DH = 128
BLOCK = 64
NBLEN = 128
ATTEND_WEIGHT = 24
SHARE = 8
F32 = jnp.float32
BF16 = jnp.bfloat16
LOG2E = 1.4426950408889634
VMEM_BYTES = 40 * 1024 * 1024


def partner(index, step, count):
    if count & (count - 1) == 0:
        return index ^ step
    return (step - index) % count


def exchange(array, axis, step, count):
    pairs = [(i, partner(i, step, count)) for i in range(count)]
    return lax.ppermute(array, axis, pairs)


def across(index, step, count):
    half = count // 2
    there = half + (index + step) % half
    return jnp.where(index < half, there, (index - step) % half)


def swap_near(array, count):
    half = count // 2
    groups = [list(range(half)), list(range(half, count))]
    return lax.all_to_all(
        array, "enc", split_axis=0, concat_axis=0, axis_index_groups=groups, tiled=True
    )


def swap_half(pieces, count):
    half = count // 2
    got = [pieces[0]]
    for step in range(1, half):
        pairs = [(i, i - i % half + partner(i % half, step, half)) for i in range(count)]
        got.append(lax.ppermute(pieces[step], "enc", pairs))
    return got


def swap_rows(pieces):
    count = len(pieces)
    return [pieces[0]] + [exchange(pieces[step], "seq", step, count) for step in range(1, count)]


def swap_pool(array):
    return lax.all_to_all(array, "enc", split_axis=0, concat_axis=0, tiled=True)


def after(array, earlier):
    return lax.optimization_barrier((array, earlier))[0]


def in_hbm(shape):
    return pltpu.HBM(shape, BF16)


def cost(moved, flops=0, exps=0):
    return pl.CostEstimate(flops=flops, bytes_accessed=moved, transcendentals=exps)


PARAMS = pltpu.CompilerParams(vmem_limit_bytes=VMEM_BYTES)
SCALARS = pl.BlockSpec(memory_space=pltpu.SMEM)
ANYWHERE = pl.BlockSpec(memory_space=pl.ANY)
IN_HBM = pl.BlockSpec(memory_space=pltpu.HBM)


def pack_kernel(first, width, q_ref, g_ref, *rest):
    outs, sems = rest[:-1], rest[-1]
    parts, chunk = len(outs), outs[0].shape[-1]
    me = lax.axis_index("seq")
    copies = []
    for step, out in enumerate(outs):
        start = pl.multiple_of(partner(me, step, parts) * width + first, DH)
        for n, ref in enumerate((q_ref, g_ref)):
            source = ref.at[0, :, pl.ds(start, chunk)]
            copies.append(pltpu.make_async_copy(source, out.at[n], sems.at[2 * step + n]))
            copies[-1].start()
    for copy in copies:
        copy.wait()


def pack(first, chunk, queries, grads, width, parts):
    shape = (2, queries.shape[1], chunk)
    return pl.pallas_call(
        functools.partial(pack_kernel, first, width),
        grid=(1,),
        in_specs=[IN_HBM, IN_HBM],
        out_specs=[pl.BlockSpec(shape, lambda i: (0, 0, 0))] * parts,
        out_shape=[in_hbm(shape)] * parts,
        scratch_shapes=[pltpu.SemaphoreType.DMA((2 * parts,))],
        compiler_params=PARAMS,
        cost_estimate=cost(8 * parts * queries.shape[1] * chunk),
        name="pack_rows",
    )(queries, grads)


def unpack_kernel(firsts, width, *refs):
    ins, (ctx_ref, gq_ref, sems) = refs[:-3], refs[-3:]
    parts = len(ins) // len(firsts)
    me = lax.axis_index("seq")
    copies = []
    for n, src in enumerate(ins):
        first, step = firsts[n // parts], n % parts
        start = pl.multiple_of(partner(me, step, parts) * width + first, DH)
        for k, ref in enumerate((ctx_ref, gq_ref)):
            target = ref.at[0, :, pl.ds(start, src.shape[-1])]
            copies.append(pltpu.make_async_copy(src.at[k], target, sems.at[2 * n + k]))
            copies[-1].start()
    for copy in copies:
        copy.wait()


def unpack(pieces, firsts, width, shape):
    flat = [array for piece in pieces for array in piece]
    return pl.pallas_call(
        functools.partial(unpack_kernel, firsts, width),
        grid=(1,),
        in_specs=[pl.BlockSpec(array.shape, lambda i: (0, 0, 0)) for array in flat],
        out_specs=[IN_HBM, IN_HBM],
        out_shape=[in_hbm(shape)] * 2,
        scratch_shapes=[pltpu.SemaphoreType.DMA((2 * len(flat),))],
        compiler_params=PARAMS,
        cost_estimate=cost(8 * shape[1] * shape[2]),
        name="unpack_rows",
    )(*flat)


def kv_shapes(seqs, chunk, form):
    half = seqs // 2
    one = (2, NBLEN, chunk)
    return [[(seqs, *one)], [(half, *one)] + [one] * half, [one] * seqs][form]


def kv_views(refs, seqs, form):
    if form == 0:
        return [(seq, refs[0].at[seq]) for seq in range(seqs)]
    half = seqs // 2
    me = lax.axis_index("enc")
    base = me - me % half
    if form == 1:
        near = [(base + step, refs[0].at[step]) for step in range(half)]
    else:
        near = [(base + partner(me % half, step, half), refs[step]) for step in range(half)]
    return near + [(across(me, step, seqs), refs[step - half]) for step in range(half)]


def pick_kernel(first, form, seqs, lists, pool_ref, *rest):
    outs, held, sems = rest[:-2], rest[-2], rest[-1]
    chunk = held.shape[-1]
    arriving, leaving = [], []
    for n, (seq, out) in enumerate(kv_views(outs, seqs, form)):
        source = pool_ref.at[lists[0, seq], :, :, first : first + chunk]
        arriving.append(pltpu.make_async_copy(source, held.at[n], sems.at[0, n]))
        leaving.append(pltpu.make_async_copy(held.at[n], out, sems.at[1, n]))
        arriving[n].start()
    for n in range(seqs):
        arriving[n].wait()
        leaving[n].start()
    for n in range(seqs):
        leaving[n].wait()


def pick(first, chunk, form, send_lists, kv_pool):
    seqs = send_lists.shape[1]
    shapes = kv_shapes(seqs, chunk, form)
    return pl.pallas_call(
        functools.partial(pick_kernel, first, form, seqs),
        grid=(1,),
        in_specs=[SCALARS, IN_HBM],
        out_specs=[IN_HBM] * len(shapes),
        out_shape=[in_hbm(shape) for shape in shapes],
        scratch_shapes=[
            pltpu.VMEM((seqs, 2, NBLEN, chunk), BF16),
            pltpu.SemaphoreType.DMA((2, seqs)),
        ],
        compiler_params=PARAMS,
        cost_estimate=cost(8 * seqs * NBLEN * chunk),
        name="pick_entries",
    )(send_lists, pltpu.with_memory_space_constraint(kv_pool, pltpu.HBM))


def dot(left, right, left_dim, right_dim):
    return lax.dot_general(
        left, right, (((left_dim,), (right_dim,)), ((), ())), preferred_element_type=F32
    )


def attend_kernel(seqs, parts, forms, pieces, uses, *rest):
    rows_in, rest = rest[:parts], rest[parts:]
    kv_in, rest = rest[: pieces[0]], rest[pieces[0] :]
    rows_out, rest = rest[:parts], rest[parts:]
    kv_out, rest = rest[: pieces[1]], rest[pieces[1] :]
    held, rows, made, sums = rest if forms[0] else (kv_in[0], *rest)
    scale = DH ** (-0.5)
    mine = lax.axis_index("seq")

    if forms[0]:
        for slot, piece in kv_views(kv_in, seqs, forms[0]):
            held[slot] = piece[...]
    for step in range(parts):
        for n in range(2):
            piece = rows_in[step][n].astype(F32)
            rows[partner(mine, step, parts), n] = pltpu.roll(piece, 1, 0)
    rows[parts] = jnp.zeros(rows.shape[1:], F32)
    made[0, :, :BLOCK] = jnp.zeros((2, BLOCK, DH), F32)
    sums[...] = jnp.zeros_like(sums)
    first_row = lax.broadcasted_iota(jnp.int32, (BLOCK, DH), 0) == 0

    def blocks_of(first, qs, gs):
        several = range(len(qs))
        slots = [(uses[0, first + n, 0], uses[0, first + n, 1]) for n in several]
        keys = [jnp.concatenate([held[a, 0], held[b, 0]], axis=0) for a, b in slots]
        values = [jnp.concatenate([held[a, 1], held[b, 1]], axis=0) for a, b in slots]
        scores = [dot(qs[n], keys[n], 1, 1) for n in several]
        grad_probs = [dot(gs[n], values[n], 1, 1) for n in several]
        peaks = [jnp.max(scores[n], axis=1, keepdims=True) for n in several]
        weights = [jnp.exp2((scores[n] - peaks[n]) * (scale * LOG2E)) for n in several]
        shares = [1.0 / jnp.sum(weights[n], axis=1, keepdims=True) for n in several]
        probs = [weights[n] * shares[n] for n in several]
        probs_low = [probs[n].astype(BF16) for n in several]
        inner = [jnp.sum(probs[n] * grad_probs[n], axis=1, keepdims=True) for n in several]
        out = [dot(probs_low[n], values[n], 1, 0) for n in several]
        grad_values = [dot(probs_low[n], gs[n], 0, 0) for n in several]
        grad_scores = [
            (probs[n] * ((grad_probs[n] - inner[n]) * scale)).astype(BF16) for n in several
        ]
        grad_q = [dot(grad_scores[n], keys[n], 1, 0) for n in several]
        grad_keys = [dot(grad_scores[n], qs[n], 0, 0) for n in several]
        for n, (a, b) in enumerate(slots):
            sums[a, 0] += grad_keys[n][:NBLEN]
            sums[b, 0] += grad_keys[n][NBLEN:]
            sums[a, 1] += grad_values[n][:NBLEN]
            sums[b, 1] += grad_values[n][NBLEN:]
        return out, grad_q

    def one_part(part, carry):
        inputs = []
        for n in range(2):
            later = jnp.where(first_row, rows[part, n, :BLOCK], rows[part + 1, n, :BLOCK])
            inputs.append([rows[part, n, BLOCK:].astype(BF16), later.astype(BF16)])
        for n, (even, odd) in enumerate(blocks_of(2 * part, *inputs)):
            made[part, n, BLOCK:] = even
            made[part + 1, n, :BLOCK] = odd
            made[part, n, :1] = odd[:1]
        return carry

    if parts <= 4:
        for part in range(parts):
            one_part(part, 0)
    else:
        lax.fori_loop(0, parts, one_part, 0)

    for step in range(parts):
        for n in range(2):
            piece = made[partner(mine, step, parts), n]
            rows_out[step][n] = pltpu.roll(piece, 2 * BLOCK - 1, 0).astype(BF16)
    for slot, piece in kv_views(kv_out, seqs, forms[1]):
        piece[...] = sums[slot].astype(BF16)


def heads_spec(shape, wide):
    return pl.BlockSpec((*shape[:-1], wide), lambda i, n=len(shape) - 1: (0,) * n + (i,))


def attend(seqs, forms, uses, rows_in, kv_in):
    parts, part_rows = len(rows_in), rows_in[0].shape[1]
    chunk = kv_in[0].shape[-1]
    heads = chunk // DH
    rows_shapes = [array.shape for array in rows_in]
    in_shapes, out_shapes = (kv_shapes(seqs, chunk, form) for form in forms)
    pairs = heads * parts * part_rows * 2 * NBLEN
    held = [pltpu.VMEM((seqs, 2, NBLEN, DH), BF16)] if forms[0] else []
    pieces = (len(in_shapes), len(out_shapes))
    outs = pl.pallas_call(
        functools.partial(attend_kernel, seqs, parts, forms, pieces),
        grid=(heads,),
        in_specs=[SCALARS] + [heads_spec(shape, DH) for shape in rows_shapes + in_shapes],
        out_specs=[heads_spec(shape, DH) for shape in rows_shapes + out_shapes],
        scratch_shapes=held
        + [
            pltpu.VMEM((parts + 1, 2, part_rows, DH), F32),
            pltpu.VMEM((parts + 1, 2, part_rows, DH), F32),
            pltpu.VMEM((seqs, 2, NBLEN, DH), F32),
        ],
        out_shape=[in_hbm(shape) for shape in rows_shapes + out_shapes],
        compiler_params=PARAMS,
        cost_estimate=cost(
            8 * (seqs + parts) * NBLEN * chunk, ATTEND_WEIGHT * 12 * DH * pairs, pairs
        ),
        name="attend_blocks",
    )(uses, *rows_in, *kv_in)
    return outs[:parts], outs[parts:]


def owner_kernel(seqs, form, pieces, lists, *rest):
    out_ref, acc = rest[-2], rest[-1]
    acc[...] = jnp.zeros_like(acc)
    for seq, piece in kv_views(rest[:pieces], seqs, form):
        acc[lists[0, seq]] += piece[...].astype(F32)
    out_ref[...] = acc[...].astype(BF16)


def owner_sum(first, form, send_lists, back, shape, so_far):
    seqs = send_lists.shape[1]
    chunk = back[0].shape[-1]
    wide = math.gcd(math.gcd(first, chunk), 256)
    skip, steps = first // wide, chunk // wide
    extra = [] if so_far is None else [so_far]
    specs = [heads_spec(array.shape, wide) for array in back]
    return pl.pallas_call(
        functools.partial(owner_kernel, seqs, form, len(back)),
        grid=(steps,),
        in_specs=[SCALARS] + specs + [ANYWHERE] * len(extra),
        out_specs=pl.BlockSpec(
            (shape[0], 2, NBLEN, wide), lambda i: (0, 0, 0, skip + i)
        ),
        scratch_shapes=[pltpu.VMEM((shape[0], 2, NBLEN, wide), F32)],
        out_shape=in_hbm(shape),
        input_output_aliases={len(back) + 1: 0} if extra else {},
        compiler_params=PARAMS,
        cost_estimate=cost(4 * (seqs + shape[0]) * NBLEN * chunk, 2 * seqs * NBLEN * chunk),
        name="owner_sum",
    )(send_lists, *back, *extra)


def swap_far(pieces, depth):
    half = len(pieces)
    got = []
    for step, piece in enumerate(pieces):
        there = [half + (i + step) % half for i in range(half)]
        pairs = list(enumerate(there)) + [(peer, i) for i, peer in enumerate(there)]
        if step >= depth:
            piece = after(piece, got[step - depth])
        got.append(lax.ppermute(piece, "enc", pairs))
    return got


def local(seqs, parts, queries, kv_pool, send_lists, block_slots, grad_context):
    width = kv_pool.shape[-1]
    send_lists = send_lists[:, :, 0]
    cut = (SHARE * width // DH // 16) * DH
    bounds = [(0, cut), (cut, width - cut)]
    firsts = [first for first, _ in bounds]

    picked = pick(*bounds[0], 0, send_lists, kv_pool)
    send_lists, queries = after((send_lists, queries), picked[0])
    early = swap_pool(picked[0])
    near, *far = pick(*bounds[1], 1, send_lists, kv_pool)
    queries = after(queries, near)
    rows = [
        swap_rows(pack(first, chunk, queries, grad_context, width, parts))
        for first, chunk in bounds
    ]
    far = after(far, rows)
    far = swap_far(far[:2] + after(far[2:], early), seqs)
    near = swap_near(near, seqs)

    early = after(early, far[0])
    rows_out, whole = attend(seqs, (0, 0), block_slots, rows[0], [early])
    token_parts = [swap_rows(rows_out)]
    returns = [[swap_pool(after(whole[0], far))]]
    block_slots = after(block_slots, token_parts[0])
    rows_out, back = attend(seqs, (1, 2), block_slots, rows[1], [near, *far])
    near, far = back[: seqs // 2], back[seqs // 2 :]
    far = swap_far(far, 2)
    token_parts.append(swap_rows(rows_out))
    near = swap_half(after(near, token_parts[1]), seqs)
    returns.append([*near, *far])

    context, grad_queries = unpack(token_parts, firsts, width, queries.shape)
    pool_grads = None
    for first, form, back in zip(firsts, (0, 2), returns):
        pool_grads = owner_sum(first, form, send_lists, back, kv_pool.shape, pool_grads)
    return (context, grad_queries, pool_grads)


def solution(mesh):
    in_specs = (
        P("enc", "seq", None),
        P("enc", None, None, "seq"),
        P("enc", None, None),
        P("enc", None, None),
        P("enc", "seq", None),
    )
    out_specs = (P("enc", "seq", None), P("enc", "seq", None), P("enc", None, None, "seq"))
    body = functools.partial(local, mesh.shape["enc"], mesh.shape["seq"])
    return jax.shard_map(body, mesh=mesh, in_specs=in_specs, out_specs=out_specs, check_vma=False)
```

```python
import functools
import math

import jax
import jax.numpy as jnp
from jax import lax
from jax.experimental import pallas as pl
from jax.experimental.pallas import tpu as pltpu
from jax.sharding import PartitionSpec as P

DH = 128
BLOCK = 64
NBLEN = 128
ATTEND_WEIGHT = 24
SHARE = 8
F32 = jnp.float32
BF16 = jnp.bfloat16
LOG2E = 1.4426950408889634
VMEM_BYTES = 40 * 1024 * 1024


def partner(index, step, count):
    if count & (count - 1) == 0:
        return index ^ step
    return (step - index) % count


def exchange(array, axis, step, count):
    pairs = [(i, partner(i, step, count)) for i in range(count)]
    return lax.ppermute(array, axis, pairs)


def across(index, step, count):
    half = count // 2
    there = half + (index + step) % half
    return jnp.where(index < half, there, (index - step) % half)


def swap_near(array, count):
    half = count // 2
    groups = [list(range(half)), list(range(half, count))]
    return lax.all_to_all(
        array, "enc", split_axis=0, concat_axis=0, axis_index_groups=groups, tiled=True
    )


def swap_half(pieces, count):
    half = count // 2
    got = [pieces[0]]
    for step in range(1, half):
        pairs = [(i, i - i % half + partner(i % half, step, half)) for i in range(count)]
        got.append(lax.ppermute(pieces[step], "enc", pairs))
    return got


def swap_rows(pieces):
    count = len(pieces)
    return [pieces[0]] + [exchange(pieces[step], "seq", step, count) for step in range(1, count)]


def swap_pool(array):
    return lax.all_to_all(array, "enc", split_axis=0, concat_axis=0, tiled=True)


def after(array, earlier):
    return lax.optimization_barrier((array, earlier))[0]


def in_hbm(shape):
    return pltpu.HBM(shape, BF16)


def cost(moved, flops=0, exps=0):
    return pl.CostEstimate(flops=flops, bytes_accessed=moved, transcendentals=exps)


PARAMS = pltpu.CompilerParams(vmem_limit_bytes=VMEM_BYTES)
SCALARS = pl.BlockSpec(memory_space=pltpu.SMEM)
ANYWHERE = pl.BlockSpec(memory_space=pl.ANY)
IN_HBM = pl.BlockSpec(memory_space=pltpu.HBM)


def pack_kernel(first, width, q_ref, g_ref, *rest):
    outs, sems = rest[:-1], rest[-1]
    parts, chunk = len(outs), outs[0].shape[-1]
    me = lax.axis_index("seq")
    copies = []
    for step, out in enumerate(outs):
        start = pl.multiple_of(partner(me, step, parts) * width + first, DH)
        for n, ref in enumerate((q_ref, g_ref)):
            source = ref.at[0, :, pl.ds(start, chunk)]
            copies.append(pltpu.make_async_copy(source, out.at[n], sems.at[2 * step + n]))
            copies[-1].start()
    for copy in copies:
        copy.wait()


def pack(first, chunk, queries, grads, width, parts):
    shape = (2, queries.shape[1], chunk)
    return pl.pallas_call(
        functools.partial(pack_kernel, first, width),
        grid=(1,),
        in_specs=[IN_HBM, IN_HBM],
        out_specs=[pl.BlockSpec(shape, lambda i: (0, 0, 0))] * parts,
        out_shape=[in_hbm(shape)] * parts,
        scratch_shapes=[pltpu.SemaphoreType.DMA((2 * parts,))],
        compiler_params=PARAMS,
        cost_estimate=cost(8 * parts * queries.shape[1] * chunk),
        name="pack_rows",
    )(queries, grads)


def unpack_kernel(firsts, width, *refs):
    ins, (ctx_ref, gq_ref, sems) = refs[:-3], refs[-3:]
    parts = len(ins) // len(firsts)
    me = lax.axis_index("seq")
    copies = []
    for n, src in enumerate(ins):
        first, step = firsts[n // parts], n % parts
        start = pl.multiple_of(partner(me, step, parts) * width + first, DH)
        for k, ref in enumerate((ctx_ref, gq_ref)):
            target = ref.at[0, :, pl.ds(start, src.shape[-1])]
            copies.append(pltpu.make_async_copy(src.at[k], target, sems.at[2 * n + k]))
            copies[-1].start()
    for copy in copies:
        copy.wait()


def unpack(pieces, firsts, width, shape):
    flat = [array for piece in pieces for array in piece]
    return pl.pallas_call(
        functools.partial(unpack_kernel, firsts, width),
        grid=(1,),
        in_specs=[pl.BlockSpec(array.shape, lambda i: (0, 0, 0)) for array in flat],
        out_specs=[IN_HBM, IN_HBM],
        out_shape=[in_hbm(shape)] * 2,
        scratch_shapes=[pltpu.SemaphoreType.DMA((2 * len(flat),))],
        compiler_params=PARAMS,
        cost_estimate=cost(8 * shape[1] * shape[2]),
        name="unpack_rows",
    )(*flat)


def kv_shapes(seqs, chunk, form):
    half = seqs // 2
    one = (2, NBLEN, chunk)
    return [[(seqs, *one)], [(half, *one)] + [one] * half, [one] * seqs][form]


def kv_views(refs, seqs, form):
    if form == 0:
        return [(seq, refs[0].at[seq]) for seq in range(seqs)]
    half = seqs // 2
    me = lax.axis_index("enc")
    base = me - me % half
    if form == 1:
        near = [(base + step, refs[0].at[step]) for step in range(half)]
    else:
        near = [(base + partner(me % half, step, half), refs[step]) for step in range(half)]
    return near + [(across(me, step, seqs), refs[step - half]) for step in range(half)]


def pick_kernel(first, form, seqs, lists, pool_ref, *rest):
    outs, held, sems = rest[:-2], rest[-2], rest[-1]
    chunk = held.shape[-1]
    arriving, leaving = [], []
    for n, (seq, out) in enumerate(kv_views(outs, seqs, form)):
        source = pool_ref.at[lists[0, seq], :, :, first : first + chunk]
        arriving.append(pltpu.make_async_copy(source, held.at[n], sems.at[0, n]))
        leaving.append(pltpu.make_async_copy(held.at[n], out, sems.at[1, n]))
        arriving[n].start()
    for n in range(seqs):
        arriving[n].wait()
        leaving[n].start()
    for n in range(seqs):
        leaving[n].wait()


def pick(first, chunk, form, send_lists, kv_pool):
    seqs = send_lists.shape[1]
    shapes = kv_shapes(seqs, chunk, form)
    return pl.pallas_call(
        functools.partial(pick_kernel, first, form, seqs),
        grid=(1,),
        in_specs=[SCALARS, IN_HBM],
        out_specs=[IN_HBM] * len(shapes),
        out_shape=[in_hbm(shape) for shape in shapes],
        scratch_shapes=[
            pltpu.VMEM((seqs, 2, NBLEN, chunk), BF16),
            pltpu.SemaphoreType.DMA((2, seqs)),
        ],
        compiler_params=PARAMS,
        cost_estimate=cost(8 * seqs * NBLEN * chunk),
        name="pick_entries",
    )(send_lists, pltpu.with_memory_space_constraint(kv_pool, pltpu.HBM))


def dot(left, right, left_dim, right_dim):
    return lax.dot_general(
        left, right, (((left_dim,), (right_dim,)), ((), ())), preferred_element_type=F32
    )


def attend_kernel(seqs, parts, forms, pieces, uses, *rest):
    rows_in, rest = rest[:parts], rest[parts:]
    kv_in, rest = rest[: pieces[0]], rest[pieces[0] :]
    rows_out, rest = rest[:parts], rest[parts:]
    kv_out, rest = rest[: pieces[1]], rest[pieces[1] :]
    held, rows, made, sums = rest if forms[0] else (kv_in[0], *rest)
    scale = DH ** (-0.5)
    mine = lax.axis_index("seq")

    if forms[0]:
        for slot, piece in kv_views(kv_in, seqs, forms[0]):
            held[slot] = piece[...]
    for step in range(parts):
        for n in range(2):
            piece = rows_in[step][n].astype(F32)
            rows[partner(mine, step, parts), n] = pltpu.roll(piece, 1, 0)
    rows[parts] = jnp.zeros(rows.shape[1:], F32)
    made[0, :, :BLOCK] = jnp.zeros((2, BLOCK, DH), F32)
    sums[...] = jnp.zeros_like(sums)
    first_row = lax.broadcasted_iota(jnp.int32, (BLOCK, DH), 0) == 0

    def blocks_of(first, qs, gs):
        several = range(len(qs))
        slots = [(uses[0, first + n, 0], uses[0, first + n, 1]) for n in several]
        keys = [jnp.concatenate([held[a, 0], held[b, 0]], axis=0) for a, b in slots]
        values = [jnp.concatenate([held[a, 1], held[b, 1]], axis=0) for a, b in slots]
        scores = [dot(qs[n], keys[n], 1, 1) for n in several]
        grad_probs = [dot(gs[n], values[n], 1, 1) for n in several]
        peaks = [jnp.max(scores[n], axis=1, keepdims=True) for n in several]
        weights = [jnp.exp2((scores[n] - peaks[n]) * (scale * LOG2E)) for n in several]
        shares = [1.0 / jnp.sum(weights[n], axis=1, keepdims=True) for n in several]
        probs = [weights[n] * shares[n] for n in several]
        probs_low = [probs[n].astype(BF16) for n in several]
        inner = [jnp.sum(probs[n] * grad_probs[n], axis=1, keepdims=True) for n in several]
        out = [dot(probs_low[n], values[n], 1, 0) for n in several]
        grad_values = [dot(probs_low[n], gs[n], 0, 0) for n in several]
        grad_scores = [
            (probs[n] * ((grad_probs[n] - inner[n]) * scale)).astype(BF16) for n in several
        ]
        grad_q = [dot(grad_scores[n], keys[n], 1, 0) for n in several]
        grad_keys = [dot(grad_scores[n], qs[n], 0, 0) for n in several]
        for n, (a, b) in enumerate(slots):
            sums[a, 0] += grad_keys[n][:NBLEN]
            sums[b, 0] += grad_keys[n][NBLEN:]
            sums[a, 1] += grad_values[n][:NBLEN]
            sums[b, 1] += grad_values[n][NBLEN:]
        return out, grad_q

    def one_part(part, carry):
        inputs = []
        for n in range(2):
            later = jnp.where(first_row, rows[part, n, :BLOCK], rows[part + 1, n, :BLOCK])
            inputs.append([rows[part, n, BLOCK:].astype(BF16), later.astype(BF16)])
        for n, (even, odd) in enumerate(blocks_of(2 * part, *inputs)):
            made[part, n, BLOCK:] = even
            made[part + 1, n, :BLOCK] = odd
            made[part, n, :1] = odd[:1]
        return carry

    if parts <= 4:
        for part in range(parts):
            one_part(part, 0)
    else:
        lax.fori_loop(0, parts, one_part, 0)

    for step in range(parts):
        for n in range(2):
            piece = made[partner(mine, step, parts), n]
            rows_out[step][n] = pltpu.roll(piece, 2 * BLOCK - 1, 0).astype(BF16)
    for slot, piece in kv_views(kv_out, seqs, forms[1]):
        piece[...] = sums[slot].astype(BF16)


def heads_spec(shape, wide):
    return pl.BlockSpec((*shape[:-1], wide), lambda i, n=len(shape) - 1: (0,) * n + (i,))


def attend(seqs, forms, uses, rows_in, kv_in):
    parts, part_rows = len(rows_in), rows_in[0].shape[1]
    chunk = kv_in[0].shape[-1]
    heads = chunk // DH
    rows_shapes = [array.shape for array in rows_in]
    in_shapes, out_shapes = (kv_shapes(seqs, chunk, form) for form in forms)
    pairs = heads * parts * part_rows * 2 * NBLEN
    held = [pltpu.VMEM((seqs, 2, NBLEN, DH), BF16)] if forms[0] else []
    pieces = (len(in_shapes), len(out_shapes))
    outs = pl.pallas_call(
        functools.partial(attend_kernel, seqs, parts, forms, pieces),
        grid=(heads,),
        in_specs=[SCALARS] + [heads_spec(shape, DH) for shape in rows_shapes + in_shapes],
        out_specs=[heads_spec(shape, DH) for shape in rows_shapes + out_shapes],
        scratch_shapes=held
        + [
            pltpu.VMEM((parts + 1, 2, part_rows, DH), F32),
            pltpu.VMEM((parts + 1, 2, part_rows, DH), F32),
            pltpu.VMEM((seqs, 2, NBLEN, DH), F32),
        ],
        out_shape=[in_hbm(shape) for shape in rows_shapes + out_shapes],
        compiler_params=PARAMS,
        cost_estimate=cost(
            8 * (seqs + parts) * NBLEN * chunk, ATTEND_WEIGHT * 12 * DH * pairs, pairs
        ),
        name="attend_blocks",
    )(uses, *rows_in, *kv_in)
    return outs[:parts], outs[parts:]


def owner_kernel(seqs, form, pieces, lists, *rest):
    out_ref, acc = rest[-2], rest[-1]
    acc[...] = jnp.zeros_like(acc)
    for seq, piece in kv_views(rest[:pieces], seqs, form):
        acc[lists[0, seq]] += piece[...].astype(F32)
    out_ref[...] = acc[...].astype(BF16)


def owner_sum(first, form, send_lists, back, shape, so_far):
    seqs = send_lists.shape[1]
    chunk = back[0].shape[-1]
    wide = math.gcd(math.gcd(first, chunk), 256)
    skip, steps = first // wide, chunk // wide
    extra = [] if so_far is None else [so_far]
    specs = [heads_spec(array.shape, wide) for array in back]
    return pl.pallas_call(
        functools.partial(owner_kernel, seqs, form, len(back)),
        grid=(steps,),
        in_specs=[SCALARS] + specs + [ANYWHERE] * len(extra),
        out_specs=pl.BlockSpec(
            (shape[0], 2, NBLEN, wide), lambda i: (0, 0, 0, skip + i)
        ),
        scratch_shapes=[pltpu.VMEM((shape[0], 2, NBLEN, wide), F32)],
        out_shape=in_hbm(shape),
        input_output_aliases={len(back) + 1: 0} if extra else {},
        compiler_params=PARAMS,
        cost_estimate=cost(4 * (seqs + shape[0]) * NBLEN * chunk, 2 * seqs * NBLEN * chunk),
        name="owner_sum",
    )(send_lists, *back, *extra)


def swap_far(pieces, depth):
    half = len(pieces)
    got = []
    for step, piece in enumerate(pieces):
        there = [half + (i + step) % half for i in range(half)]
        pairs = list(enumerate(there)) + [(peer, i) for i, peer in enumerate(there)]
        if step >= depth:
            piece = after(piece, got[step - depth])
        got.append(lax.ppermute(piece, "enc", pairs))
    return got


def local(seqs, parts, queries, kv_pool, send_lists, block_slots, grad_context):
    width = kv_pool.shape[-1]
    send_lists = send_lists[:, :, 0]
    cut = (SHARE * width // DH // 16) * DH
    bounds = [(0, cut), (cut, width - cut)]
    firsts = [first for first, _ in bounds]

    picked = pick(*bounds[0], 0, send_lists, kv_pool)
    send_lists, queries = after((send_lists, queries), picked[0])
    early = swap_pool(picked[0])
    near, *far = pick(*bounds[1], 1, send_lists, kv_pool)
    queries = after(queries, near)
    rows = [
        swap_rows(pack(first, chunk, queries, grad_context, width, parts))
        for first, chunk in bounds
    ]
    far = after(far, rows)
    far = swap_far(far[:2] + after(far[2:], early), seqs)
    near = swap_near(near, seqs)

    early = after(early, far[0])
    rows_out, (near_back, *far_back) = attend(seqs, (0, 1), block_slots, rows[0], [early])
    far_back = swap_far([after(*pair) for pair in zip(far_back, far)], seqs)
    early_rows = after(rows_out, far_back)
    rows_out, back = attend(seqs, (1, 2), block_slots, rows[1], [near, *far])
    near, far = back[: seqs // 2], list(back[seqs // 2 :])
    far[:2] = [after(*pair) for pair in zip(far[:2], far_back)]
    far = swap_far(far, 2)
    token_parts = [swap_rows(after(rows_out, far_back))]
    near_back = swap_near(after(near_back, token_parts[0]), seqs)
    near = swap_half(after(near, token_parts[0]), seqs)
    token_parts.insert(0, swap_rows(after(early_rows, near)))
    returns = [[near_back, *far_back], [*near, *far]]

    context, grad_queries = unpack(token_parts, firsts, width, queries.shape)
    pool_grads = None
    for first, form, back in zip(firsts, (1, 2), returns):
        pool_grads = owner_sum(first, form, send_lists, back, kv_pool.shape, pool_grads)
    return (context, grad_queries, pool_grads)


def solution(mesh):
    in_specs = (
        P("enc", "seq", None),
        P("enc", None, None, "seq"),
        P("enc", None, None),
        P("enc", None, None),
        P("enc", "seq", None),
    )
    out_specs = (P("enc", "seq", None), P("enc", "seq", None), P("enc", None, None, "seq"))
    body = functools.partial(local, mesh.shape["enc"], mesh.shape["seq"])
    return jax.shard_map(body, mesh=mesh, in_specs=in_specs, out_specs=out_specs, check_vma=False)
```

```python
import functools
import math

import jax
import jax.numpy as jnp
from jax import lax
from jax.experimental import pallas as pl
from jax.experimental.pallas import tpu as pltpu
from jax.sharding import PartitionSpec as P

DH = 128
BLOCK = 64
NBLEN = 128
ATTEND_WEIGHT = 24
SHARE = 10
F32 = jnp.float32
BF16 = jnp.bfloat16
LOG2E = 1.4426950408889634
VMEM_BYTES = 40 * 1024 * 1024


def partner(index, step, count):
    if count & (count - 1) == 0:
        return index ^ step
    return (step - index) % count


def exchange(array, axis, step, count):
    pairs = [(i, partner(i, step, count)) for i in range(count)]
    return lax.ppermute(array, axis, pairs)


def across(index, step, count):
    half = count // 2
    there = half + (index + step) % half
    return jnp.where(index < half, there, (index - step) % half)


def swap_near(array, count):
    half = count // 2
    groups = [list(range(half)), list(range(half, count))]
    return lax.all_to_all(
        array, "enc", split_axis=0, concat_axis=0, axis_index_groups=groups, tiled=True
    )


def swap_half(pieces, count):
    half = count // 2
    got = [pieces[0]]
    for step in range(1, half):
        pairs = [(i, i - i % half + partner(i % half, step, half)) for i in range(count)]
        got.append(lax.ppermute(pieces[step], "enc", pairs))
    return got


def swap_rows(pieces):
    count = len(pieces)
    return [pieces[0]] + [exchange(pieces[step], "seq", step, count) for step in range(1, count)]


def swap_pool(array):
    return lax.all_to_all(array, "enc", split_axis=0, concat_axis=0, tiled=True)


def after(array, earlier):
    return lax.optimization_barrier((array, earlier))[0]


def in_hbm(shape):
    return pltpu.HBM(shape, BF16)


def cost(moved, flops=0, exps=0):
    return pl.CostEstimate(flops=flops, bytes_accessed=moved, transcendentals=exps)


PARAMS = pltpu.CompilerParams(vmem_limit_bytes=VMEM_BYTES)
SCALARS = pl.BlockSpec(memory_space=pltpu.SMEM)
ANYWHERE = pl.BlockSpec(memory_space=pl.ANY)
IN_HBM = pl.BlockSpec(memory_space=pltpu.HBM)


def pack_kernel(first, width, q_ref, g_ref, *rest):
    outs, sems = rest[:-1], rest[-1]
    parts, chunk = len(outs), outs[0].shape[-1]
    me = lax.axis_index("seq")
    copies = []
    for step, out in enumerate(outs):
        start = pl.multiple_of(partner(me, step, parts) * width + first, DH)
        for n, ref in enumerate((q_ref, g_ref)):
            source = ref.at[0, :, pl.ds(start, chunk)]
            copies.append(pltpu.make_async_copy(source, out.at[n], sems.at[2 * step + n]))
            copies[-1].start()
    for copy in copies:
        copy.wait()


def pack(first, chunk, queries, grads, width, parts):
    shape = (2, queries.shape[1], chunk)
    return pl.pallas_call(
        functools.partial(pack_kernel, first, width),
        grid=(1,),
        in_specs=[IN_HBM, IN_HBM],
        out_specs=[pl.BlockSpec(shape, lambda i: (0, 0, 0))] * parts,
        out_shape=[in_hbm(shape)] * parts,
        scratch_shapes=[pltpu.SemaphoreType.DMA((2 * parts,))],
        compiler_params=PARAMS,
        cost_estimate=cost(8 * parts * queries.shape[1] * chunk),
        name="pack_rows",
    )(queries, grads)


def unpack_kernel(firsts, width, *refs):
    ins, (ctx_ref, gq_ref, sems) = refs[:-3], refs[-3:]
    parts = len(ins) // len(firsts)
    me = lax.axis_index("seq")
    copies = []
    for n, src in enumerate(ins):
        first, step = firsts[n // parts], n % parts
        start = pl.multiple_of(partner(me, step, parts) * width + first, DH)
        for k, ref in enumerate((ctx_ref, gq_ref)):
            target = ref.at[0, :, pl.ds(start, src.shape[-1])]
            copies.append(pltpu.make_async_copy(src.at[k], target, sems.at[2 * n + k]))
            copies[-1].start()
    for copy in copies:
        copy.wait()


def unpack(pieces, firsts, width, shape):
    flat = [array for piece in pieces for array in piece]
    return pl.pallas_call(
        functools.partial(unpack_kernel, firsts, width),
        grid=(1,),
        in_specs=[pl.BlockSpec(array.shape, lambda i: (0, 0, 0)) for array in flat],
        out_specs=[IN_HBM, IN_HBM],
        out_shape=[in_hbm(shape)] * 2,
        scratch_shapes=[pltpu.SemaphoreType.DMA((2 * len(flat),))],
        compiler_params=PARAMS,
        cost_estimate=cost(8 * shape[1] * shape[2]),
        name="unpack_rows",
    )(*flat)


def kv_shapes(seqs, chunk, form):
    half = seqs // 2
    one = (2, NBLEN, chunk)
    return [[(seqs, *one)], [(half, *one)] + [one] * half, [one] * seqs][form]


def kv_views(refs, seqs, form):
    if form == 0:
        return [(seq, refs[0].at[seq]) for seq in range(seqs)]
    half = seqs // 2
    me = lax.axis_index("enc")
    base = me - me % half
    if form == 1:
        near = [(base + step, refs[0].at[step]) for step in range(half)]
    else:
        near = [(base + partner(me % half, step, half), refs[step]) for step in range(half)]
    return near + [(across(me, step, seqs), refs[step - half]) for step in range(half)]


def pick_kernel(first, form, seqs, lists, pool_ref, *rest):
    outs, held, sems = rest[:-2], rest[-2], rest[-1]
    chunk = held.shape[-1]
    arriving, leaving = [], []
    for n, (seq, out) in enumerate(kv_views(outs, seqs, form)):
        source = pool_ref.at[lists[0, seq], :, :, first : first + chunk]
        arriving.append(pltpu.make_async_copy(source, held.at[n], sems.at[0, n]))
        leaving.append(pltpu.make_async_copy(held.at[n], out, sems.at[1, n]))
        arriving[n].start()
    for n in range(seqs):
        arriving[n].wait()
        leaving[n].start()
    for n in range(seqs):
        leaving[n].wait()


def pick(first, chunk, form, send_lists, kv_pool):
    seqs = send_lists.shape[1]
    shapes = kv_shapes(seqs, chunk, form)
    return pl.pallas_call(
        functools.partial(pick_kernel, first, form, seqs),
        grid=(1,),
        in_specs=[SCALARS, IN_HBM],
        out_specs=[IN_HBM] * len(shapes),
        out_shape=[in_hbm(shape) for shape in shapes],
        scratch_shapes=[
            pltpu.VMEM((seqs, 2, NBLEN, chunk), BF16),
            pltpu.SemaphoreType.DMA((2, seqs)),
        ],
        compiler_params=PARAMS,
        cost_estimate=cost(8 * seqs * NBLEN * chunk),
        name="pick_entries",
    )(send_lists, pltpu.with_memory_space_constraint(kv_pool, pltpu.HBM))


def dot(left, right, left_dim, right_dim):
    return lax.dot_general(
        left, right, (((left_dim,), (right_dim,)), ((), ())), preferred_element_type=F32
    )


def attend_kernel(seqs, parts, forms, pieces, uses, *rest):
    rows_in, rest = rest[:parts], rest[parts:]
    kv_in, rest = rest[: pieces[0]], rest[pieces[0] :]
    rows_out, rest = rest[:parts], rest[parts:]
    kv_out, rest = rest[: pieces[1]], rest[pieces[1] :]
    held, rows, made, sums = rest if forms[0] else (kv_in[0], *rest)
    scale = DH ** (-0.5)
    mine = lax.axis_index("seq")

    if forms[0]:
        for slot, piece in kv_views(kv_in, seqs, forms[0]):
            held[slot] = piece[...]
    for step in range(parts):
        for n in range(2):
            piece = rows_in[step][n].astype(F32)
            rows[partner(mine, step, parts), n] = pltpu.roll(piece, 1, 0)
    rows[parts] = jnp.zeros(rows.shape[1:], F32)
    made[0, :, :BLOCK] = jnp.zeros((2, BLOCK, DH), F32)
    sums[...] = jnp.zeros_like(sums)
    first_row = lax.broadcasted_iota(jnp.int32, (BLOCK, DH), 0) == 0

    def blocks_of(first, qs, gs):
        several = range(len(qs))
        slots = [(uses[0, first + n, 0], uses[0, first + n, 1]) for n in several]
        keys = [jnp.concatenate([held[a, 0], held[b, 0]], axis=0) for a, b in slots]
        values = [jnp.concatenate([held[a, 1], held[b, 1]], axis=0) for a, b in slots]
        scores = [dot(qs[n], keys[n], 1, 1) for n in several]
        grad_probs = [dot(gs[n], values[n], 1, 1) for n in several]
        peaks = [jnp.max(scores[n], axis=1, keepdims=True) for n in several]
        weights = [jnp.exp2((scores[n] - peaks[n]) * (scale * LOG2E)) for n in several]
        shares = [1.0 / jnp.sum(weights[n], axis=1, keepdims=True) for n in several]
        probs = [weights[n] * shares[n] for n in several]
        probs_low = [probs[n].astype(BF16) for n in several]
        inner = [jnp.sum(probs[n] * grad_probs[n], axis=1, keepdims=True) for n in several]
        out = [dot(probs_low[n], values[n], 1, 0) for n in several]
        grad_values = [dot(probs_low[n], gs[n], 0, 0) for n in several]
        grad_scores = [
            (probs[n] * ((grad_probs[n] - inner[n]) * scale)).astype(BF16) for n in several
        ]
        grad_q = [dot(grad_scores[n], keys[n], 1, 0) for n in several]
        grad_keys = [dot(grad_scores[n], qs[n], 0, 0) for n in several]
        for n, (a, b) in enumerate(slots):
            sums[a, 0] += grad_keys[n][:NBLEN]
            sums[b, 0] += grad_keys[n][NBLEN:]
            sums[a, 1] += grad_values[n][:NBLEN]
            sums[b, 1] += grad_values[n][NBLEN:]
        return out, grad_q

    def one_part(part, carry):
        inputs = []
        for n in range(2):
            later = jnp.where(first_row, rows[part, n, :BLOCK], rows[part + 1, n, :BLOCK])
            inputs.append([rows[part, n, BLOCK:].astype(BF16), later.astype(BF16)])
        for n, (even, odd) in enumerate(blocks_of(2 * part, *inputs)):
            made[part, n, BLOCK:] = even
            made[part + 1, n, :BLOCK] = odd
            made[part, n, :1] = odd[:1]
        return carry

    if parts <= 4:
        for part in range(parts):
            one_part(part, 0)
    else:
        lax.fori_loop(0, parts, one_part, 0)

    for step in range(parts):
        for n in range(2):
            piece = made[partner(mine, step, parts), n]
            rows_out[step][n] = pltpu.roll(piece, 2 * BLOCK - 1, 0).astype(BF16)
    for slot, piece in kv_views(kv_out, seqs, forms[1]):
        piece[...] = sums[slot].astype(BF16)


def heads_spec(shape, wide):
    return pl.BlockSpec((*shape[:-1], wide), lambda i, n=len(shape) - 1: (0,) * n + (i,))


def attend(seqs, forms, uses, rows_in, kv_in):
    parts, part_rows = len(rows_in), rows_in[0].shape[1]
    chunk = kv_in[0].shape[-1]
    heads = chunk // DH
    rows_shapes = [array.shape for array in rows_in]
    in_shapes, out_shapes = (kv_shapes(seqs, chunk, form) for form in forms)
    pairs = heads * parts * part_rows * 2 * NBLEN
    held = [pltpu.VMEM((seqs, 2, NBLEN, DH), BF16)] if forms[0] else []
    pieces = (len(in_shapes), len(out_shapes))
    outs = pl.pallas_call(
        functools.partial(attend_kernel, seqs, parts, forms, pieces),
        grid=(heads,),
        in_specs=[SCALARS] + [heads_spec(shape, DH) for shape in rows_shapes + in_shapes],
        out_specs=[heads_spec(shape, DH) for shape in rows_shapes + out_shapes],
        scratch_shapes=held
        + [
            pltpu.VMEM((parts + 1, 2, part_rows, DH), F32),
            pltpu.VMEM((parts + 1, 2, part_rows, DH), F32),
            pltpu.VMEM((seqs, 2, NBLEN, DH), F32),
        ],
        out_shape=[in_hbm(shape) for shape in rows_shapes + out_shapes],
        compiler_params=PARAMS,
        cost_estimate=cost(
            8 * (seqs + parts) * NBLEN * chunk, ATTEND_WEIGHT * 12 * DH * pairs, pairs
        ),
        name="attend_blocks",
    )(uses, *rows_in, *kv_in)
    return outs[:parts], outs[parts:]


def owner_kernel(seqs, form, pieces, lists, *rest):
    out_ref, acc = rest[-2], rest[-1]
    acc[...] = jnp.zeros_like(acc)
    for seq, piece in kv_views(rest[:pieces], seqs, form):
        acc[lists[0, seq]] += piece[...].astype(F32)
    out_ref[...] = acc[...].astype(BF16)


def owner_sum(first, form, send_lists, back, shape, so_far):
    seqs = send_lists.shape[1]
    chunk = back[0].shape[-1]
    wide = math.gcd(math.gcd(first, chunk), 256)
    skip, steps = first // wide, chunk // wide
    extra = [] if so_far is None else [so_far]
    specs = [heads_spec(array.shape, wide) for array in back]
    return pl.pallas_call(
        functools.partial(owner_kernel, seqs, form, len(back)),
        grid=(steps,),
        in_specs=[SCALARS] + specs + [ANYWHERE] * len(extra),
        out_specs=pl.BlockSpec(
            (shape[0], 2, NBLEN, wide), lambda i: (0, 0, 0, skip + i)
        ),
        scratch_shapes=[pltpu.VMEM((shape[0], 2, NBLEN, wide), F32)],
        out_shape=in_hbm(shape),
        input_output_aliases={len(back) + 1: 0} if extra else {},
        compiler_params=PARAMS,
        cost_estimate=cost(4 * (seqs + shape[0]) * NBLEN * chunk, 2 * seqs * NBLEN * chunk),
        name="owner_sum",
    )(send_lists, *back, *extra)


def swap_far(pieces, depth):
    half = len(pieces)
    got = []
    for step, piece in enumerate(pieces):
        there = [half + (i + step) % half for i in range(half)]
        pairs = list(enumerate(there)) + [(peer, i) for i, peer in enumerate(there)]
        if step >= depth:
            piece = after(piece, got[step - depth])
        got.append(lax.ppermute(piece, "enc", pairs))
    return got


def local(seqs, parts, queries, kv_pool, send_lists, block_slots, grad_context):
    width = kv_pool.shape[-1]
    send_lists = send_lists[:, :, 0]
    cut = (SHARE * width // DH // 16) * DH
    bounds = [(0, cut), (cut, width - cut)]
    firsts = [first for first, _ in bounds]

    picked = pick(*bounds[0], 0, send_lists, kv_pool)
    send_lists, queries = after((send_lists, queries), picked[0])
    early = swap_pool(picked[0])
    near, *far = pick(*bounds[1], 1, send_lists, kv_pool)
    queries = after(queries, near)
    rows = [
        swap_rows(pack(first, chunk, queries, grad_context, width, parts))
        for first, chunk in bounds
    ]
    far = after(far, rows)
    far = swap_far(far[:2] + after(far[2:], early), seqs)
    near = swap_near(near, seqs)

    early = after(early, far[0])
    rows_out, whole = attend(seqs, (0, 0), block_slots, rows[0], [early])
    token_parts = [swap_rows(rows_out)]
    returns = [[swap_pool(after(whole[0], far))]]
    block_slots = after(block_slots, token_parts[0])
    rows_out, back = attend(seqs, (1, 2), block_slots, rows[1], [near, *far])
    near, far = back[: seqs // 2], back[seqs // 2 :]
    far = swap_far(far, 2)
    token_parts.append(swap_rows(rows_out))
    near = swap_half(after(near, token_parts[1]), seqs)
    returns.append([*near, *far])

    context, grad_queries = unpack(token_parts, firsts, width, queries.shape)
    pool_grads = None
    for first, form, back in zip(firsts, (0, 2), returns):
        pool_grads = owner_sum(first, form, send_lists, back, kv_pool.shape, pool_grads)
    return (context, grad_queries, pool_grads)


def solution(mesh):
    in_specs = (
        P("enc", "seq", None),
        P("enc", None, None, "seq"),
        P("enc", None, None),
        P("enc", None, None),
        P("enc", "seq", None),
    )
    out_specs = (P("enc", "seq", None), P("enc", "seq", None), P("enc", None, None, "seq"))
    body = functools.partial(local, mesh.shape["enc"], mesh.shape["seq"])
    return jax.shard_map(body, mesh=mesh, in_specs=in_specs, out_specs=out_specs, check_vma=False)
```
